32 devices in a mesh: dp: 16 (over z, y, core), mp: 2 (over x).
Axes of the slice: x: 2, y: 2, z: 4, core: 2. Of those that a mesh axis runs over, the one named last changes fastest.
Arguments:
- stream: bfloat16 [768, 32768], P('mp', 'dp'), may hold values from -6 to 6
- lengths: int32 [16], P('dp'), may hold values from 64 to 2048, as said below
- w_qkv: bfloat16 [3, 768, 767], P(None, 'mp'), may hold values from -0.21875 to 0.21875
- b_qkv: bfloat16 [3, 768], P(None, 'mp'), may hold values from -3 to 3
- w_out: bfloat16 [768, 767], P('mp'), may hold values from -3.5 to 3.5
- b_out: bfloat16 [767], replicated, may hold values from -2 to 2
- w_up: bfloat16 [767, 3072], P(None, 'mp'), may hold values from -0.21875 to 0.21875
- b_up: bfloat16 [3072], P('mp'), may hold values from -3 to 3
- w_down: bfloat16 [3072, 767], P('mp'), may hold values from -0.21875 to 0.21875
- b_down: bfloat16 [767], replicated, may hold values from -2 to 2
- cotangent: bfloat16 [768, 32768], P('mp', 'dp'), may hold values from -6 to 6
Outputs:
- output: bfloat16 [768, 32768], P('mp', 'dp')
- grad_stream: float32 [768, 32768], P('mp', 'dp')
- grad_w_qkv: float32 [3, 768, 767], P(None, 'mp')
- grad_b_qkv: float32 [3, 768], P(None, 'mp')
- grad_w_out: float32 [768, 767], P('mp')
- grad_b_out: float32 [767], replicated
- grad_w_up: float32 [767, 3072], P(None, 'mp')
- grad_b_up: float32 [3072], P('mp')
- grad_w_down: float32 [3072, 767], P('mp')
- grad_b_down: float32 [767], replicated
The draws below stay inside these ranges and needn't reach their ends.
Inputs may be any that keep to these rules, and one draw needn't show every extreme that they name: `lengths`: valid rows of each padded sequence of 2048 rows; in every draw some sequence has exactly 2048.
All inputs are finite; a program needn't handle non-finite values.
Results may differ from the reference program's by a relative error of at most 0.0095.
Values may be sent and summed in bfloat16 or wider, within the bound.
No kernel may reach another device: no remote copies, remote signals or barrier semaphores. Data moves between devices by JAX's collectives and lax.ppermute only.
A program may use at most 256 MiB of HBM per device.

```python
import jax
import jax.numpy as jnp
from jax import lax

H = 12
HS = 64
FF = 3072
SEQ_DEV = 1
SLOT = 2048
MINLEN = 64
QBLK = 512
HW = 768
DS = 767
NSEQ = 16
TOKENS = 32768


def draw_lengths(key, part):
    key = jax.random.fold_in(key, 11)
    key_power, key_extra, key_long = jax.random.split(key, 3)
    levels = (SLOT // MINLEN).bit_length() - 1
    power = jax.random.randint(key_power, (NSEQ,), 0, levels + 1)
    base = MINLEN * 2 ** power
    extra = jax.random.randint(key_extra, (NSEQ,), 0, 1 << 30) % base
    length = jnp.minimum(base + extra, SLOT)
    longest = jax.random.randint(key_long, (), 0, NSEQ)
    length = jnp.where(jnp.arange(NSEQ) == longest, SLOT, length)
    return length.astype(jnp.int32)


def shard_levels(key, extent, cuts, least, high):
    def one(dim, blocks):
        draws = jax.random.uniform(jax.random.fold_in(jax.random.fold_in(key, 6), dim), (blocks,), jnp.float32, least / len(cuts), high / len(cuts))
        return jnp.repeat(jnp.exp(draws), extent[dim] // blocks).reshape((-1,) + (1,) * (len(extent) - dim - 1))

    factor_of = one(*cuts[0])
    for cut in cuts[1:]:
        factor_of = factor_of * one(*cut)
    return factor_of


def centred(key, dims, scale, bound, shards=(), kind=jnp.bfloat16):
    factor_of = shard_levels(key, dims, shards, -0.22, 0.18) if shards else 1.0
    entries = jax.random.normal(key, dims, jnp.float32) * scale * factor_of
    return jnp.minimum(jnp.maximum(entries, -bound), bound).astype(kind)


def setup_inputs(seed: int = 0) -> dict:
    streams_of = jax.random.split(jax.random.key(seed), 12)
    stream = centred(streams_of[0], (HW, TOKENS), 1.0, 6.0, ((0, 2), (1, 16)))
    lengths = draw_lengths(jax.random.fold_in(streams_of[11], 71), 0)
    w_qkv = centred(streams_of[2], (3, HW, DS), DS ** -0.5, 0.21875, ((1, 2),))
    b_qkv = centred(streams_of[3], (3, HW), 0.5, 3.0, ((1, 2),))
    w_out = centred(streams_of[4], (HW, DS), (max(1, HW // 256)) ** -0.5, 3.5, ((0, 2),))
    b_out = centred(streams_of[5], (DS,), 0.3, 2.0)
    w_up = centred(streams_of[6], (DS, FF), DS ** -0.5, 0.21875, ((1, 2),))
    b_up = centred(streams_of[7], (FF,), 0.5, 3.0, ((0, 2),))
    w_down = centred(streams_of[8], (FF, DS), (FF // 4) ** -0.5, 0.21875, ((0, 2),))
    b_down = centred(streams_of[9], (DS,), 0.3, 2.0)
    cotangent = centred(streams_of[10], (HW, TOKENS), 1.0, 6.0, ((0, 2), (1, 16)))
    return {"stream": stream, "lengths": lengths, "w_qkv": w_qkv, "b_qkv": b_qkv, "w_out": w_out, "b_out": b_out, "w_up": w_up, "b_up": b_up, "w_down": w_down, "b_down": b_down, "cotangent": cotangent}


EPSILON = 1e-05
NEGATIVE = -1e+30
HIGH = lax.Precision.HIGHEST

@jax.custom_vjp
def low(v):
    return lax.optimization_barrier(v.astype(jnp.bfloat16)).astype(jnp.float32)

@jax.custom_vjp
def low_back(v):
    return v

def low_keep(v):
    return (low(v), None)

def low_pass(kept, grad):
    return (grad,)

def back_keep(v):
    return (v, None)

def back_low(kept, grad):
    return (low(grad),)
low.defvjp(low_keep, low_pass)
low_back.defvjp(back_keep, back_low)

def crms(stream_cols):
    column_sum = lax.optimization_barrier(jnp.sum(stream_cols, axis=-1, keepdims=True))
    square_sum = lax.optimization_barrier(jnp.sum(stream_cols * stream_cols, axis=-1, keepdims=True))
    return stream_cols * lax.rsqrt((square_sum + column_sum * column_sum) / (DS + 1) + EPSILON)

def attention(queries, key_rows, value_rows, lengths):
    per_seq = SLOT // QBLK
    block_count = queries.shape[0] // QBLK

    def one_block(block_id):
        seq_id = block_id // per_seq
        query_blk = lax.dynamic_slice_in_dim(queries, block_id * QBLK, QBLK, 0)
        key_seq = lax.dynamic_slice_in_dim(key_rows, seq_id * SLOT, SLOT, 0)
        value_seq = lax.dynamic_slice_in_dim(value_rows, seq_id * SLOT, SLOT, 0)
        scores = low_back(jnp.einsum('qhe,khe->hqk', query_blk, key_seq, precision=HIGH) * 0.125)
        query_pos = block_id % per_seq * QBLK + jnp.arange(QBLK, dtype=jnp.int32)
        key_pos = jnp.arange(SLOT, dtype=jnp.int32)
        allowed = (key_pos[None, :] <= query_pos[:, None]) & (key_pos[None, :] < lengths[seq_id])
        probs = jax.nn.softmax(jnp.where(allowed[None], scores, NEGATIVE), axis=-1)
        return jnp.einsum('hqk,khe->qhe', low(probs), value_seq, precision=HIGH)
    blocks = lax.map(jax.checkpoint(one_block), jnp.arange(block_count, dtype=jnp.int32))
    return blocks.reshape(queries.shape[0], H * HS)

def forward(stream_all, lengths, params):
    w_qkv, b_qkv, w_out, b_out, w_up, b_up, w_down, b_down = params
    row_count = stream_all.shape[0]
    stream_cols = stream_all[:, :DS]
    row_pos = jnp.arange(row_count, dtype=jnp.int32)
    valid = (row_pos % SLOT < lengths[row_pos // SLOT]).astype(jnp.float32)[:, None]
    normed = low(crms(stream_cols))
    projected = low(low_back(jnp.einsum('td,chd->tch', normed, w_qkv, precision=HIGH) + b_qkv))
    heads_shape = (row_count, H, HS)
    mixed = low(low_back(attention(projected[:, 0].reshape(heads_shape), projected[:, 1].reshape(heads_shape), projected[:, 2].reshape(heads_shape), lengths)))
    branch = low_back(jnp.dot(mixed, w_out, precision=HIGH) + b_out)
    hidden_stream = stream_cols + valid * branch
    normed_two = low(crms(hidden_stream))
    pre_act = low_back(jnp.dot(normed_two, w_up, precision=HIGH) + b_up)
    activated = low(jax.nn.gelu(pre_act, approximate=True))
    branch_two = low_back(jnp.dot(activated, w_down, precision=HIGH) + b_down)
    result = hidden_stream + valid * branch_two
    return jnp.concatenate([result, stream_all[:, DS:]], axis=1)

def reference(stream, lengths, w_qkv, b_qkv, w_out, b_out, w_up, b_up, w_down, b_down, cotangent):
    params = tuple((p.astype(jnp.float32) for p in (w_qkv, b_qkv, w_out, b_out, w_up, b_up, w_down, b_down)))
    group_rows = SEQ_DEV * SLOT
    width = stream.shape[0]
    row_total = stream.shape[1]
    group_count = row_total // group_rows
    stream_groups = stream.astype(jnp.float32).T.reshape(group_count, group_rows, width)
    cot_groups = cotangent.astype(jnp.float32).T.reshape(group_count, group_rows, width)
    length_groups = lengths.reshape(group_count, SEQ_DEV)

    def step(totals, item):
        stream_g, cot_g, length_g = item
        result, pull = jax.vjp(lambda inputs, weights: forward(inputs, length_g, weights), stream_g, params)
        grad_in, grad_params = pull(cot_g)
        totals = tuple((a + b for a, b in zip(totals, grad_params)))
        return (totals, (result.astype(jnp.bfloat16), grad_in))
    zeros = tuple((jnp.zeros_like(p) for p in params))
    grads, (results, grad_rows) = lax.scan(step, zeros, (stream_groups, cot_groups, length_groups))
    return (results.reshape(row_total, width).T, grad_rows.reshape(row_total, width).T, grads[0], grads[1], grads[2], grads[3], grads[4], grads[5], grads[6], grads[7])
```

```python
import functools

import jax
import jax.numpy as jnp
from jax import lax
from jax.experimental import pallas as pl
from jax.experimental.pallas import tpu as pltpu
from jax.sharding import Mesh
from jax.sharding import PartitionSpec as P

HS = 64
DS = 767
DP = 768
BLK = 256
EPSILON = 1e-05
NEGATIVE = -1e30
F32 = jnp.float32
BF = jnp.bfloat16
VMEM_BYTES = 56 * 1024 * 1024
ROWS_BLK = 512
UNIT_BLK = 256


def dot(left, right, left_dim, right_dim):
    return lax.dot_general(
        left, right, (((left_dim,), (right_dim,)), ((), ())), preferred_element_type=F32
    )


def call(body, name, grid, in_specs, out_specs, out_shape, scratch, prefetch=0):
    return pl.pallas_call(
        body,
        grid_spec=pltpu.PrefetchScalarGridSpec(
            num_scalar_prefetch=prefetch,
            grid=grid,
            in_specs=in_specs,
            out_specs=out_specs,
            scratch_shapes=scratch,
        ),
        out_shape=out_shape,
        compiler_params=pltpu.CompilerParams(vmem_limit_bytes=VMEM_BYTES),
        name=name,
    )


def rows_spec(height, block):
    return pl.BlockSpec((height, block), lambda i, *_: (0, i))


def whole_spec(shape):
    return pl.BlockSpec(shape, lambda i, *_: (0,) * len(shape), pipeline_mode=pl.Buffered(1))


def shape_of(shape, dtype):
    return jax.ShapeDtypeStruct(shape, dtype)


def join_halves(scratch, mine_ref, other_ref, core):
    half = mine_ref.shape[0]
    scratch[pl.ds(pl.multiple_of(core * half, half), half), :] = mine_ref[...]
    scratch[pl.ds(pl.multiple_of((1 - core) * half, half), half), :] = other_ref[...]
    return scratch[...]


def crms_stats(values):
    kept = jnp.where(lax.broadcasted_iota(jnp.int32, values.shape, 0) < DS, values, 0.0)
    total = jnp.sum(kept, 0, keepdims=True)
    squares = jnp.sum(kept * kept, 0, keepdims=True)
    scale = lax.rsqrt((squares + total * total) / DP + EPSILON)
    return kept, scale, total


def project_body(where_ref, mine_ref, other_ref, w_ref, b_ref, normed_ref, qkv_ref, stats_ref, x_scr):
    stream = join_halves(x_scr, mine_ref, other_ref, where_ref[0]).astype(F32)
    kept, scale, total = crms_stats(stream)
    normed = (kept * scale).astype(BF)
    normed_ref[...] = normed
    qkv_ref[...] = (dot(w_ref[...], normed, 1, 0) + b_ref[...]).astype(BF)
    stats_ref[0:1, :] = scale
    stats_ref[1:2, :] = total


def project_own(where, mine, other, weights, bias):
    half, rows = mine.shape
    outs = weights.shape[0]
    block = ROWS_BLK
    return call(
        project_body,
        "norm_project",
        (rows // block,),
        [rows_spec(half, block), rows_spec(half, block), whole_spec((outs, DP)), whole_spec((outs, 1))],
        [rows_spec(DP, block), rows_spec(outs, block), rows_spec(8, block)],
        [shape_of((DP, rows), BF), shape_of((outs, rows), BF), shape_of((8, rows), F32)],
        [pltpu.VMEM((DP, block), BF)],
        1,
    )(where, mine, other, weights, bias)


def project_more_body(normed_ref, w_ref, b_ref, qkv_ref):
    qkv_ref[...] = (dot(w_ref[...], normed_ref[...], 1, 0) + b_ref[...]).astype(BF)


def project_more(normed, weights, bias):
    rows = normed.shape[1]
    outs = weights.shape[0]
    block = ROWS_BLK
    return call(
        project_more_body,
        "project",
        (rows // block,),
        [rows_spec(DP, block), whole_spec((outs, DP)), whole_spec((outs, 1))],
        [rows_spec(outs, block)],
        [shape_of((outs, rows), BF)],
        [],
    )(normed, weights, bias)[0]


def causal_tile():
    key_pos = lax.broadcasted_iota(jnp.int32, (BLK, BLK), 0)
    query_pos = lax.broadcasted_iota(jnp.int32, (BLK, BLK), 1)
    return key_pos <= query_pos


def attend_body(q_ref, k_ref, v_ref, a_ref, log_ref, s_scr, p_scr):
    rows = q_ref.shape[1]
    key_rows = k_ref[...].T
    queries = q_ref[...] * jnp.asarray(0.125, BF)
    allowed = causal_tile()
    for query_blk in range(rows // BLK):
        at = slice(query_blk * BLK, (query_blk + 1) * BLK)
        slot = query_blk % 2
        top = None
        for key_blk in range(query_blk + 1):
            keys = slice(key_blk * BLK, (key_blk + 1) * BLK)
            scores = dot(key_rows[keys], queries[:, at], 1, 0)
            if key_blk == query_blk:
                scores = jnp.where(allowed, scores, NEGATIVE)
            s_scr[slot, keys] = scores
            most = jnp.max(scores, axis=0, keepdims=True)
            top = most if top is None else jnp.maximum(top, most)
        total = None
        for key_blk in range(query_blk + 1):
            keys = slice(key_blk * BLK, (key_blk + 1) * BLK)
            expo = jnp.exp(s_scr[slot, keys] - top)
            part = jnp.sum(expo, axis=0, keepdims=True)
            total = part if total is None else total + part
            p_scr[slot, keys] = expo.astype(BF)
        count = (query_blk + 1) * BLK
        mixed = dot(v_ref[:, :count], p_scr[slot, :count], 1, 0)
        a_ref[:, at] = (mixed * (1.0 / total)).astype(BF)
        log_ref[0, :, at] = top + jnp.log(total)


def head_specs(heads, rows):
    return [
        pl.BlockSpec((HS, rows), lambda h, part=part: (part * heads + h, 0)) for part in range(3)
    ]


def attend(qkv):
    outs, rows = qkv.shape
    heads = outs // (3 * HS)
    return call(
        attend_body,
        "attend",
        (heads,),
        head_specs(heads, rows),
        [
            pl.BlockSpec((HS, rows), lambda h: (h, 0)),
            pl.BlockSpec((1, 1, rows), lambda h: (h, 0, 0)),
        ],
        [shape_of((heads * HS, rows), BF), shape_of((heads, 1, rows), F32)],
        [pltpu.VMEM((2, rows, BLK), F32), pltpu.VMEM((2, rows, BLK), BF)],
    )(qkv, qkv, qkv)


def attend_back_body(
    q_ref, k_ref, v_ref, da_ref, a_ref, log_ref, dq_ref, dk_ref, dv_ref, p_scr, ds_scr, dq_scr
):
    rows = q_ref.shape[1]
    blocks = rows // BLK
    queries = q_ref[...] * jnp.asarray(0.125, BF)
    query_rows = queries.T
    key_rows = k_ref[...].T
    value_rows = v_ref[...].T
    grad = da_ref[...]
    grad_rows = grad.T
    row_dot = jnp.sum(grad.astype(F32) * a_ref[...].astype(F32), axis=0, keepdims=True)
    logs = log_ref[0]
    allowed = causal_tile()
    for key_blk in range(blocks):
        keys = slice(key_blk * BLK, (key_blk + 1) * BLK)
        slot = key_blk % 2
        for query_blk in range(key_blk, blocks):
            at = slice(query_blk * BLK, (query_blk + 1) * BLK)
            scores = dot(key_rows[keys], queries[:, at], 1, 0)
            probs = jnp.exp(scores - logs[:, at])
            if key_blk == query_blk:
                probs = jnp.where(allowed, probs, 0.0)
            grad_probs = dot(value_rows[keys], grad[:, at], 1, 0)
            grad_scores = (probs * (grad_probs - row_dot[:, at])).astype(BF)
            p_scr[slot, :, at] = probs.astype(BF)
            ds_scr[slot, :, at] = grad_scores
            part = dot(k_ref[:, keys], grad_scores, 1, 0)
            if key_blk == 0:
                dq_scr[:, at] = part
            else:
                dq_scr[:, at] += part
        start = key_blk * BLK
        grad_keys = dot(ds_scr[slot, :, start:], query_rows[start:], 1, 0)
        grad_values = dot(p_scr[slot, :, start:], grad_rows[start:], 1, 0)
        dk_ref[:, keys] = grad_keys.T.astype(BF)
        dv_ref[:, keys] = grad_values.T.astype(BF)
    dq_ref[...] = (dq_scr[...] * 0.125).astype(BF)


def attend_back(qkv, grad, mixed, logs, part):
    outs, rows = qkv.shape
    heads = outs // (3 * HS)
    one = pl.BlockSpec((HS, rows), lambda h: (h, 0))
    return call(
        attend_back_body,
        "attend_back",
        (heads,),
        head_specs(heads, rows)
        + [
            pl.BlockSpec((HS, rows), lambda h: (part * heads + h, 0)),
            one,
            pl.BlockSpec((1, 1, rows), lambda h: (h, 0, 0)),
        ],
        [one, one, one],
        [shape_of((heads * HS, rows), BF)] * 3,
        [pltpu.VMEM((2, BLK, rows), BF), pltpu.VMEM((2, BLK, rows), BF), pltpu.VMEM((HS, rows), F32)],
    )(qkv, qkv, qkv, grad, mixed, logs)


GELU_A = 0.7978845608028654
GELU_B = 0.044715


def gelu_pair(pre):
    square = pre * pre
    bent = jnp.tanh(GELU_A * pre * (1.0 + GELU_B * square))
    half_up = 0.5 * (1.0 + bent)
    slope = half_up + 0.5 * pre * (1.0 - bent * bent) * (GELU_A * (1.0 + 3.0 * GELU_B * square))
    return pre * half_up, slope


def mlp_body(
    where_ref, a0, a1, a2, a3, wout_t, b_out, x_mine, x_other, c_mine, c_other,
    up_t0, up_t1, up0, up1, down_t0, down_t1, down0, down1, b_up0, b_up1,
    h_ref, stats_ref, m_own_ref, m_other_ref, dn_ref, pack0, pack1,
    a_scr, x_scr, c_scr, g_scr, du_scr, m_scr, gd0, gd1, gu0, gu1, gb_scr,
):
    step = pl.program_id(0)
    core = where_ref[0]
    block = x_mine.shape[1]
    for i, a_ref in enumerate((a0, a1, a2, a3)):
        part = a_ref.shape[0]
        a_scr[i * part : (i + 1) * part, :] = a_ref[...]
    position = step * block + lax.broadcasted_iota(jnp.int32, (1, block), 1)
    valid = (position < where_ref[1]).astype(F32)
    stream = join_halves(x_scr, x_mine, x_other, core).astype(F32)
    branch = dot(wout_t[...], a_scr[...], 1, 0) + b_out[...]
    hidden = stream + valid * branch
    h_ref[...] = hidden
    kept, scale, total = crms_stats(hidden)
    stats_ref[0:1, :] = scale
    stats_ref[1:2, :] = total
    normed = (kept * scale).astype(BF)
    grad_out = join_halves(c_scr, c_mine, c_other, core)
    keep_row = lax.broadcasted_iota(jnp.int32, (DP, 1), 0) < DS
    dm_f = jnp.where(keep_row, grad_out.astype(F32) * valid, 0.0)
    dm = dm_f.astype(BF)

    @pl.when(step == 0)
    def _():
        for ref in (gd0, gd1, gu0, gu1, gb_scr):
            ref[...] = jnp.zeros_like(ref)

    units = up_t0.shape[0]
    gb_scr[2] += jnp.sum(dm_f, 1, keepdims=True)
    for which, (up_t, down, b_up, gd, gu) in enumerate(
        ((up_t0, down0, b_up0, gd0, gu0), (up_t1, down1, b_up1, gd1, gu1))
    ):
        for start in range(0, units, UNIT_BLK):
            at = slice(start, start + UNIT_BLK)
            to = slice(which * units + start, which * units + start + UNIT_BLK)
            pre = dot(up_t[at], normed, 1, 0) + b_up[at]
            grad_act = dot(down[at], dm, 1, 0)
            act, slope = gelu_pair(pre)
            act = act.astype(BF)
            grad_pre = (grad_act * slope).astype(BF)
            g_scr[to, :] = act
            du_scr[to, :] = grad_pre
            gd[at, :] += dot(act, dm, 1, 1)
            gu[:, at] += dot(normed, grad_pre, 1, 1)
            gb_scr[which, at] += jnp.sum(grad_pre.astype(F32), 1, keepdims=True)
    m_scr[...] = dot(down_t0[...], g_scr[:units], 1, 0) + dot(down_t1[...], g_scr[units:], 1, 0)
    half = DP // 2
    m_own_ref[...] = m_scr[pl.ds(pl.multiple_of(core * half, half), half), :]
    m_other_ref[...] = m_scr[pl.ds(pl.multiple_of((1 - core) * half, half), half), :].astype(BF)
    dn_ref[...] = (
        dot(up0[...], du_scr[:units], 1, 0) + dot(up1[...], du_scr[units:], 1, 0)
    ).astype(BF)

    @pl.when(step == pl.num_programs(0) - 1)
    def _():
        for which, (pack, gd, gu) in enumerate(((pack0, gd0, gu0), (pack1, gd1, gu1))):
            pack[0:units, :] = gd[...].astype(BF)
            pack[units : units + DP, :] = gu[...].astype(BF)
            pack[units + DP : units + DP + 16, :] = jnp.zeros((16, units), BF)
            pack[units + DP : units + DP + 1, :] = gb_scr[which].T.astype(BF)
            pack[units + DP + 1 : units + DP + 2, :] = gb_scr[2].T.astype(BF)


def mlp(where, mixed, wout_t, b_out, stream, cot, up_t, up, down_t, down, b_up):
    half, rows = stream[0].shape
    part = mixed[0].shape[0]
    units = up_t[0].shape[0]
    block = ROWS_BLK
    square = whole_spec((DP, units))
    return call(
        mlp_body,
        "out_project_mlp",
        (rows // block,),
        [rows_spec(part, block)] * 4
        + [whole_spec((DP, DP)), whole_spec((DP, 1))]
        + [rows_spec(half, block)] * 4
        + [square] * 8
        + [whole_spec((units, 1))] * 2,
        [
            rows_spec(DP, block),
            rows_spec(8, block),
            rows_spec(half, block),
            rows_spec(half, block),
            rows_spec(DP, block),
            whole_spec((units + DP + 16, DP)),
            whole_spec((units + DP + 16, DP)),
        ],
        [
            shape_of((DP, rows), F32),
            shape_of((8, rows), F32),
            shape_of((half, rows), F32),
            shape_of((half, rows), BF),
            shape_of((DP, rows), BF),
            shape_of((units + DP + 16, DP), BF),
            shape_of((units + DP + 16, DP), BF),
        ],
        [
            pltpu.VMEM((DP, block), BF),
            pltpu.VMEM((DP, block), BF),
            pltpu.VMEM((DP, block), BF),
            pltpu.VMEM((2 * units, block), BF),
            pltpu.VMEM((2 * units, block), BF),
            pltpu.VMEM((DP, block), F32),
            pltpu.VMEM((units, DP), F32),
            pltpu.VMEM((units, DP), F32),
            pltpu.VMEM((DP, units), F32),
            pltpu.VMEM((DP, units), F32),
            pltpu.VMEM((3, DP, 1), F32),
        ],
        1,
    )(where, *mixed, wout_t, b_out, *stream, *cot, *up_t, *up, *down_t, *down, *b_up)


def crms_pull(grad_norm, values, scale, total, inner, row_mask):
    pulled = scale * grad_norm - scale * scale * scale * (values + total) * inner / DP
    return jnp.where(row_mask, pulled, 0.0)


def out_back_body(
    where_ref, dn_mine, dn_other, h_ref, stats_ref, c_mine, c_other, w_ref, a0, a1,
    dh_ref, da_ref, gw_ref, gb_ref, c_scr, dh_scr,
):
    step = pl.program_id(0)
    core = where_ref[0]
    block = h_ref.shape[1]
    position = step * block + lax.broadcasted_iota(jnp.int32, (1, block), 1)
    valid = (position < where_ref[1]).astype(F32)
    row_mask = lax.broadcasted_iota(jnp.int32, (DP, 1), 0) < DS
    grad_norm = dn_mine[...].astype(F32) + dn_other[...].astype(F32)
    hidden = h_ref[...]
    inner = jnp.sum(jnp.where(row_mask, grad_norm * hidden, 0.0), 0, keepdims=True)
    grad_out = join_halves(c_scr, c_mine, c_other, core).astype(F32)
    grad_hidden = grad_out + crms_pull(
        grad_norm, hidden, stats_ref[0:1, :], stats_ref[1:2, :], inner, row_mask
    )
    dh_scr[...] = grad_hidden
    half = DP // 2
    dh_ref[...] = dh_scr[pl.ds(pl.multiple_of(core * half, half), half), :]
    branch_f = jnp.where(row_mask, grad_hidden * valid, 0.0)
    branch = branch_f.astype(BF)
    da_ref[...] = dot(w_ref[...], branch, 1, 0).astype(BF)

    @pl.when(step == 0)
    def _():
        gw_ref[...] = jnp.zeros_like(gw_ref)
        gb_ref[...] = jnp.zeros_like(gb_ref)

    part = a0.shape[0]
    gw_ref[:part] += dot(a0[...], branch, 1, 1)
    gw_ref[part:] += dot(a1[...], branch, 1, 1)
    gb_ref[...] += jnp.sum(branch_f, 1, keepdims=True)


def out_back(where, dn, hidden, stats, cot, weights, mixed):
    rows = hidden.shape[1]
    half = cot[0].shape[0]
    part = mixed[0].shape[0]
    block = ROWS_BLK
    return call(
        out_back_body,
        "out_project_back",
        (rows // block,),
        [rows_spec(DP, block)] * 3
        + [rows_spec(8, block)]
        + [rows_spec(half, block)] * 2
        + [whole_spec((2 * part, DP))]
        + [rows_spec(part, block)] * 2,
        [
            rows_spec(half, block),
            rows_spec(2 * part, block),
            whole_spec((2 * part, DP)),
            whole_spec((DP, 1)),
        ],
        [
            shape_of((half, rows), F32),
            shape_of((2 * part, rows), BF),
            shape_of((2 * part, DP), F32),
            shape_of((DP, 1), F32),
        ],
        [pltpu.VMEM((DP, block), BF), pltpu.VMEM((DP, block), F32)],
        1,
    )(where, *dn, hidden, stats, *cot, weights, *mixed)


def project_back_body(
    where_ref, q0, k0, v0, q1, k1, v1, normed_ref, w_t0, w_t1,
    dn_own_ref, dn_other_ref, inner_ref, gw0, gw1, gb_ref, p_scr, dn_scr,
):
    step = pl.program_id(0)
    core = where_ref[0]
    part = q0.shape[0]
    for i, ref in enumerate((q0, k0, v0, q1, k1, v1)):
        p_scr[i * part : (i + 1) * part, :] = ref[...]
    outs = 3 * part

    @pl.when(step == 0)
    def _():
        gw0[...] = jnp.zeros_like(gw0)
        gw1[...] = jnp.zeros_like(gw1)
        gb_ref[...] = jnp.zeros_like(gb_ref)

    normed = normed_ref[...]
    gw0[...] += dot(p_scr[:outs], normed, 1, 1)
    gw1[...] += dot(p_scr[outs:], normed, 1, 1)
    gb_ref[...] += jnp.sum(p_scr[...].astype(F32), 1, keepdims=True)
    grad_norm = dot(w_t0[...], p_scr[:outs], 1, 0) + dot(w_t1[...], p_scr[outs:], 1, 0)
    dn_scr[...] = grad_norm
    half = DP // 2
    dn_own_ref[...] = dn_scr[pl.ds(pl.multiple_of(core * half, half), half), :]
    dn_other_ref[...] = dn_scr[pl.ds(pl.multiple_of((1 - core) * half, half), half), :].astype(BF)
    inner = jnp.sum(grad_norm * normed.astype(F32), 0, keepdims=True)
    inner_ref[...] = jnp.broadcast_to(inner, inner_ref.shape)


def project_back(where, own, other, normed, w_t):
    part, rows = own[0].shape
    half = DP // 2
    block = ROWS_BLK
    return call(
        project_back_body,
        "project_back",
        (rows // block,),
        [rows_spec(part, block)] * 6 + [rows_spec(DP, block)] + [whole_spec((DP, 3 * part))] * 2,
        [
            rows_spec(half, block),
            rows_spec(half, block),
            rows_spec(8, block),
            whole_spec((3 * part, DP)),
            whole_spec((3 * part, DP)),
            whole_spec((6 * part, 1)),
        ],
        [
            shape_of((half, rows), F32),
            shape_of((half, rows), BF),
            shape_of((8, rows), F32),
            shape_of((3 * part, DP), F32),
            shape_of((3 * part, DP), F32),
            shape_of((6 * part, 1), F32),
        ],
        [pltpu.VMEM((6 * part, block), BF), pltpu.VMEM((DP, block), F32)],
        1,
    )(where, *own, *other, normed, *w_t)


def swap(value, axis):
    return lax.ppermute(value, axis, [(0, 1), (1, 0)])


def cross(value):
    return lax.ppermute(value, ("core", "x"), [(1, 2), (2, 1)])


def quarter(value, core, axis):
    size = value.shape[axis] // 2
    return lax.dynamic_slice_in_dim(value, core * size, size, axis)


def both(mine, other, core, axis):
    first = jnp.where(core == 0, mine, other)
    second = jnp.where(core == 0, other, mine)
    return jnp.concatenate([first, second], axis)


def pad_last(value):
    return jnp.pad(value, [(0, 0)] * (value.ndim - 1) + [(0, DP - value.shape[-1])])


def on_device(stream, lengths, w_qkv, b_qkv, w_out, b_out, w_up, b_up, w_down, b_down, cotangent):
    core = lax.axis_index("core")
    chip = lax.axis_index("x")
    stays = core == chip
    half, rows = stream.shape

    def home(value):
        return jnp.where(stays, value, cross(value))

    x_mine = home(stream)
    x_other = swap(x_mine, "core")
    length = jnp.where(stays, lengths, swap(lengths.astype(F32), "core").astype(jnp.int32))
    where = jnp.concatenate([core[None].astype(jnp.int32), length])

    own_qkv = pad_last(quarter(w_qkv, core, 1)).reshape(-1, DP)
    own_bq = quarter(b_qkv, core, 1).reshape(1, -1)
    heads_rows = own_qkv.shape[0]
    pack_qkv = jnp.concatenate([own_qkv, jnp.pad(pad_last(own_bq), ((0, 15), (0, 0)))])
    got_qkv = swap(pack_qkv, "x")
    other_qkv = got_qkv[:heads_rows]
    other_bq = got_qkv[heads_rows, :heads_rows]

    c_mine = home(cotangent)
    c_other = swap(c_mine, "core")

    own_up = jnp.pad(quarter(w_up, core, 1), ((0, DP - DS), (0, 0)))
    own_down = pad_last(quarter(w_down, core, 0))
    own_out = pad_last(quarter(w_out, core, 0))
    own_bu = quarter(b_up, core, 0)
    units = own_up.shape[1]
    part = own_out.shape[0]
    pack_rest = jnp.concatenate([own_out, own_up, own_down, jnp.pad(own_bu[None], ((0, 15), (0, 0)))])
    got_rest = swap(pack_rest, "x")
    other_out = got_rest[:part]
    other_up = got_rest[part : part + DP]
    other_down = got_rest[part + DP : part + DP + units]
    other_bu = got_rest[part + DP + units]

    normed_one, qkv_own, stats_one = project_own(
        where, x_mine, x_other, own_qkv, own_bq.astype(F32).reshape(-1, 1)
    )
    mixed_own, logs_own = attend(qkv_own)
    mixed_own_far = swap(mixed_own, "core")
    qkv_other = project_more(normed_one, other_qkv, other_bq.astype(F32).reshape(-1, 1))
    mixed_other, logs_other = attend(qkv_other)
    mixed_other_far = swap(mixed_other, "core")

    far_out = swap(jnp.concatenate([own_out, other_out]), "core")
    wout_all = jnp.concatenate([own_out, other_out, far_out])
    hidden, stats_two, m_own, m_other, dn_two, pack_own, pack_other = mlp(
        where,
        (mixed_own, mixed_other, mixed_own_far, mixed_other_far),
        wout_all.T,
        jnp.pad(b_out, (0, 1)).astype(F32)[:, None],
        (x_mine, x_other),
        (c_mine, c_other),
        (own_up.T, other_up.T),
        (own_up, other_up),
        (own_down.T, other_down.T),
        (own_down, other_down),
        (own_bu.astype(F32)[:, None], other_bu.astype(F32)[:, None]),
    )
    dn_two_far = swap(dn_two, "core")
    m_far = swap(m_other, "core")
    got_mlp = swap(pack_other, "x")
    sum_mlp = lax.psum(pack_own + got_mlp, "zy")
    far_mlp = swap(sum_mlp, "core")

    position = lax.iota(jnp.int32, rows)
    valid = (position < length[0]).astype(F32)[None, :]
    hidden_own = lax.dynamic_slice_in_dim(hidden, core * half, half, 0)
    b_down_own = lax.dynamic_slice_in_dim(jnp.pad(b_down, (0, 1)), core * half, half, 0)
    result = hidden_own + valid * (m_own + m_far.astype(F32) + b_down_own.astype(F32)[:, None])
    output = home(result.astype(BF))

    dh_own, grad_mixed, gw_out, gb_out = out_back(
        where,
        (dn_two, dn_two_far),
        hidden,
        stats_two,
        (c_mine, c_other),
        wout_all[: 2 * part],
        (mixed_own, mixed_other),
    )
    dp_other = attend_back(qkv_other, grad_mixed, mixed_other, logs_other, 1)
    dp_own = attend_back(qkv_own, grad_mixed, mixed_own, logs_own, 0)
    dn_own, dn_other, inner, gw_own, gw_other, gb_qkv = project_back(
        where, dp_own, dp_other, normed_one, (own_qkv.T, other_qkv.T)
    )
    dn_far = swap(dn_other, "core")
    inner = inner[0:1] + swap(inner, "core")[0:1]
    row_mask = core * half + lax.broadcasted_iota(jnp.int32, (half, 1), 0) < DS
    scale_one, total_one = stats_one[0:1], stats_one[1:2]
    grad_in = dh_own + jnp.where(
        row_mask,
        scale_one * (dn_own + dn_far.astype(F32))
        - scale_one * scale_one * (x_mine.astype(F32) + total_one) * inner / DP,
        0.0,
    )
    grad_stream = jnp.where(stays, grad_in, cross(grad_in.astype(BF)).astype(F32))

    def attn_pack(gw, gwo, gb):
        tail = jnp.concatenate([jnp.pad(gb.reshape(1, -1), ((0, 0), (0, DP - heads_rows))), gb_out.T])
        return jnp.concatenate([gw, gwo, jnp.pad(tail, ((0, 14), (0, 0)))]).astype(BF)

    attn_own = attn_pack(gw_own, gw_out[:part], gb_qkv[:heads_rows])
    attn_other = attn_pack(gw_other, gw_out[part:], gb_qkv[heads_rows:])
    sum_attn = lax.psum(attn_own + swap(attn_other, "x"), "zy")
    far_attn = swap(sum_attn, "core")

    def gather(pick, axis):
        return both(pick(sum_mlp), pick(far_mlp), core, axis).astype(F32)

    def gather_attn(pick, axis):
        return both(pick(sum_attn), pick(far_attn), core, axis).astype(F32)

    edge = units + DP
    attn_edge = heads_rows + part
    return (
        output,
        grad_stream,
        gather_attn(lambda v: v[:heads_rows, :DS].reshape(3, -1, DS), 1),
        gather_attn(lambda v: v[attn_edge, :heads_rows].reshape(3, -1), 1),
        gather_attn(lambda v: v[heads_rows:attn_edge, :DS], 0),
        sum_attn[attn_edge + 1, :DS].astype(F32),
        gather(lambda v: v[units : units + DS], 1),
        gather(lambda v: v[edge], 0),
        gather(lambda v: v[:units, :DS], 0),
        sum_mlp[edge + 1, :DS].astype(F32),
    )


def solution(mesh):
    dp, mp = mesh.shape["dp"], mesh.shape["mp"]
    fine = Mesh(mesh.devices.reshape(dp // 2, 2, mp), ("zy", "core", "x"))
    seqs = ("zy", "core")
    placed = (
        P("x", seqs),
        P(seqs),
        P(None, "x", None),
        P(None, "x"),
        P("x", None),
        P(),
        P(None, "x"),
        P("x"),
        P("x", None),
        P(),
        P("x", seqs),
    )
    return jax.shard_map(
        on_device,
        mesh=fine,
        in_specs=placed,
        out_specs=(
            P("x", seqs),
            P("x", seqs),
            P(None, "x", None),
            P(None, "x"),
            P("x", None),
            P(),
            P(None, "x"),
            P("x"),
            P("x", None),
            P(),
        ),
        check_vma=False,
    )
```

```python
import functools

import jax
import jax.numpy as jnp
from jax import lax
from jax.experimental import pallas as pl
from jax.experimental.pallas import tpu as pltpu
from jax.sharding import Mesh
from jax.sharding import PartitionSpec as P

HS = 64
DS = 767
DP = 768
BLK = 256
EPSILON = 1e-05
NEGATIVE = -1e30
F32 = jnp.float32
BF = jnp.bfloat16
VMEM_BYTES = 56 * 1024 * 1024
ROWS_BLK = 512
UNIT_BLK = 256
PAD = 16
BACK_MICROS = (20, 20, 20, 4, 4, 4)


def dot(left, right, left_dim, right_dim):
    return lax.dot_general(
        left, right, (((left_dim,), (right_dim,)), ((), ())), preferred_element_type=F32
    )


def call(body, name, micros, grid, in_specs, out_specs, out_shape, scratch, prefetch=0):
    return pl.pallas_call(
        body,
        grid_spec=pltpu.PrefetchScalarGridSpec(
            num_scalar_prefetch=prefetch,
            grid=grid,
            in_specs=in_specs,
            out_specs=out_specs,
            scratch_shapes=scratch,
        ),
        out_shape=out_shape,
        compiler_params=pltpu.CompilerParams(vmem_limit_bytes=VMEM_BYTES),
        cost_estimate=pl.CostEstimate(flops=int(micros * 1e9), bytes_accessed=0, transcendentals=0),
        name=name,
    )


def rows_spec(height, block):
    return pl.BlockSpec((height, block), lambda i, *_: (0, i))


def whole_spec(shape):
    return pl.BlockSpec(shape, lambda i, *_: (0,) * len(shape), pipeline_mode=pl.Buffered(1))


def shape_of(shape, dtype):
    return jax.ShapeDtypeStruct(shape, dtype)


def join_halves(scratch, mine_ref, other_ref, core):
    half = mine_ref.shape[0]
    scratch[pl.ds(pl.multiple_of(core * half, half), half), :] = mine_ref[...]
    scratch[pl.ds(pl.multiple_of((1 - core) * half, half), half), :] = other_ref[...]
    return scratch[...]


def crms_stats(values):
    kept = jnp.where(lax.broadcasted_iota(jnp.int32, values.shape, 0) < DS, values, 0.0)
    total = jnp.sum(kept, 0, keepdims=True)
    squares = jnp.sum(kept * kept, 0, keepdims=True)
    scale = lax.rsqrt((squares + total * total) / DP + EPSILON)
    return kept, scale, total


def causal_tile():
    key_pos = lax.broadcasted_iota(jnp.int32, (BLK, BLK), 0)
    query_pos = lax.broadcasted_iota(jnp.int32, (BLK, BLK), 1)
    return key_pos <= query_pos


def attend_head(w_ref, normed_ref, qkv_ref, a_ref, log_ref, s_scr, p_scr):
    rows = normed_ref.shape[1]
    blocks = rows // BLK
    outs = 3 * HS
    bias = w_ref[outs : outs + 1, :outs].astype(F32).T
    qkv_ref[...] = (dot(w_ref[:outs, :], normed_ref[...], 1, 0) + bias).astype(BF)
    key_rows = qkv_ref[HS : 2 * HS, :].T
    queries = qkv_ref[:HS, :] * jnp.asarray(0.125, BF)
    allowed = causal_tile()

    def score(blk):
        at = slice(blk * BLK, (blk + 1) * BLK)
        count = (blk + 1) * BLK
        scores = dot(key_rows[:count], queries[:, at], 1, 0)
        if blk:
            s_scr[blk % 2, : count - BLK] = scores[: count - BLK]
        s_scr[blk % 2, count - BLK : count] = jnp.where(allowed, scores[count - BLK :], NEGATIVE)

    def soften(blk):
        count = (blk + 1) * BLK
        top = jnp.max(s_scr[blk % 2, :count], axis=0, keepdims=True)
        expo = jnp.exp(s_scr[blk % 2, :count] - top)
        total = jnp.sum(expo, axis=0, keepdims=True)
        p_scr[blk % 2, :count] = expo.astype(BF)
        log_ref[0, :, blk * BLK : count] = top + jnp.log(total)
        return total

    def mix(blk, total):
        count = (blk + 1) * BLK
        mixed = dot(qkv_ref[2 * HS :, :count], p_scr[blk % 2, :count], 1, 0)
        a_ref[:, blk * BLK : count] = (mixed * (1.0 / total)).astype(BF)

    score(0)
    totals = {}
    for blk in range(blocks):
        if blk + 1 < blocks:
            score(blk + 1)
        if blk:
            mix(blk - 1, totals[blk - 1])
        totals[blk] = soften(blk)
    mix(blocks - 1, totals[blocks - 1])


def norm_attend_body(
    where_ref, mine_ref, other_ref, w_ref, normed_ref, stats_ref, qkv_ref, a_ref, log_ref, s_scr, p_scr
):
    @pl.when(pl.program_id(0) == 0)
    def _():
        half = mine_ref.shape[0]
        core = where_ref[0]
        first = pl.ds(pl.multiple_of(core * half, half), half)
        second = pl.ds(pl.multiple_of((1 - core) * half, half), half)
        normed_ref[first, :] = mine_ref[...]
        normed_ref[second, :] = other_ref[...]
        for start in range(0, normed_ref.shape[1], BLK):
            at = slice(start, start + BLK)
            kept, scale, total = crms_stats(normed_ref[:, at].astype(F32))
            normed_ref[:, at] = (kept * scale).astype(BF)
            stats_ref[0:1, at] = scale
            stats_ref[1:2, at] = total

    attend_head(w_ref, normed_ref, qkv_ref, a_ref, log_ref, s_scr, p_scr)


def attend_specs(heads, rows):
    outs = 3 * HS
    ins = [pl.BlockSpec((outs + PAD, DP), lambda h, *_: (h, 0))]
    results = [
        pl.BlockSpec((outs, rows), lambda h, *_: (h, 0)),
        pl.BlockSpec((HS, rows), lambda h, *_: (h, 0)),
        pl.BlockSpec((1, 1, rows), lambda h, *_: (h, 0, 0)),
    ]
    shapes = [
        shape_of((heads * outs, rows), BF),
        shape_of((heads * HS, rows), BF),
        shape_of((heads, 1, rows), F32),
    ]
    scratch = [pltpu.VMEM((2, rows, BLK), F32), pltpu.VMEM((2, rows, BLK), BF)]
    return ins, results, shapes, scratch


def norm_attend(where, mine, other, weights):
    half, rows = mine.shape
    heads = weights.shape[0] // (3 * HS + PAD)
    ins, results, shapes, scratch = attend_specs(heads, rows)
    return call(
        norm_attend_body,
        "norm_attend",
        22,
        (heads,),
        [whole_spec((half, rows)), whole_spec((half, rows))] + ins,
        [whole_spec((DP, rows)), whole_spec((8, rows))] + results,
        [shape_of((DP, rows), BF), shape_of((8, rows), F32)] + shapes,
        scratch,
        1,
    )(where, mine, other, weights)


def more_attend_body(normed_ref, w_ref, qkv_ref, a_ref, log_ref, s_scr, p_scr):
    attend_head(w_ref, normed_ref, qkv_ref, a_ref, log_ref, s_scr, p_scr)


def more_attend(normed, weights):
    rows = normed.shape[1]
    heads = weights.shape[0] // (3 * HS + PAD)
    ins, results, shapes, scratch = attend_specs(heads, rows)
    return call(
        more_attend_body,
        "attend",
        20,
        (heads,),
        [whole_spec((DP, rows))] + ins,
        results,
        shapes,
        scratch,
    )(normed, weights)


def attend_back_body(
    qkv_ref, da_ref, a_ref, log_ref, normed_hbm, grad_ref, gw_ref,
    p_scr, ds_scr, dq_scr, normed_scr, sem,
):
    fetch = pltpu.make_async_copy(normed_hbm, normed_scr, sem)
    fetch.start()
    rows = qkv_ref.shape[1]
    blocks = rows // BLK
    queries = qkv_ref[:HS, :] * jnp.asarray(0.125, BF)
    query_rows = queries.T
    key_rows = qkv_ref[HS : 2 * HS, :].T
    value_rows = qkv_ref[2 * HS :, :].T
    grad = da_ref[...]
    grad_rows = grad.T
    row_dot = jnp.sum(grad.astype(F32) * a_ref[...].astype(F32), axis=0, keepdims=True)
    logs = log_ref[0]
    allowed = causal_tile()
    for key_blk in range(blocks):
        keys = slice(key_blk * BLK, (key_blk + 1) * BLK)
        slot = key_blk % 2
        for query_blk in range(key_blk, blocks):
            at = slice(query_blk * BLK, (query_blk + 1) * BLK)
            scores = dot(key_rows[keys], queries[:, at], 1, 0)
            probs = jnp.exp(scores - logs[:, at])
            if key_blk == query_blk:
                probs = jnp.where(allowed, probs, 0.0)
            grad_probs = dot(value_rows[keys], grad[:, at], 1, 0)
            grad_scores = (probs * (grad_probs - row_dot[:, at])).astype(BF)
            p_scr[slot, :, at] = probs.astype(BF)
            ds_scr[slot, :, at] = grad_scores
            part = dot(qkv_ref[HS : 2 * HS, keys], grad_scores, 1, 0)
            if key_blk == 0:
                dq_scr[:, at] = part
            else:
                dq_scr[:, at] += part
        start = key_blk * BLK
        grad_keys = dot(ds_scr[slot, :, start:], query_rows[start:], 1, 0)
        grad_values = dot(p_scr[slot, :, start:], grad_rows[start:], 1, 0)
        grad_ref[HS : 2 * HS, keys] = grad_keys.T.astype(BF)
        grad_ref[2 * HS :, keys] = grad_values.T.astype(BF)
    grad_ref[:HS, :] = (dq_scr[...] * 0.125).astype(BF)
    fetch.wait()
    outs = 3 * HS
    gw_ref[:outs, :] = dot(grad_ref[...], normed_scr[...], 1, 1).astype(BF)
    gw_ref[outs:, :] = jnp.zeros((PAD, DP), BF)
    gw_ref[outs : outs + 1, :outs] = jnp.sum(grad_ref[...].astype(F32), 1, keepdims=True).T.astype(BF)


def attend_back(qkv, grad, mixed, logs, normed, head, grad_head):
    rows = qkv.shape[1]
    outs = 3 * HS
    return call(
        attend_back_body,
        "attend_back",
        BACK_MICROS[grad_head],
        (1,),
        [
            pl.BlockSpec((outs, rows), lambda i: (head, 0)),
            pl.BlockSpec((HS, rows), lambda i: (grad_head, 0)),
            pl.BlockSpec((HS, rows), lambda i: (head, 0)),
            pl.BlockSpec((1, 1, rows), lambda i: (head, 0, 0)),
            pl.BlockSpec(memory_space=pl.ANY),
        ],
        [
            pl.BlockSpec((outs, rows), lambda i: (0, 0)),
            pl.BlockSpec((outs + PAD, DP), lambda i: (0, 0)),
        ],
        [shape_of((outs, rows), BF), shape_of((outs + PAD, DP), BF)],
        [
            pltpu.VMEM((2, BLK, rows), BF),
            pltpu.VMEM((2, BLK, rows), BF),
            pltpu.VMEM((HS, rows), F32),
            pltpu.VMEM((DP, rows), BF),
            pltpu.SemaphoreType.DMA(()),
        ],
    )(qkv, grad, mixed, logs, normed)


GELU_A = 0.7978845608028654
GELU_B = 0.044715


def gelu_pair(pre):
    square = pre * pre
    bent = jnp.tanh(GELU_A * pre * (1.0 + GELU_B * square))
    half_up = 0.5 * (1.0 + bent)
    slope = half_up + 0.5 * pre * (1.0 - bent * bent) * (GELU_A * (1.0 + 3.0 * GELU_B * square))
    return pre * half_up, slope


def mlp_body(
    where_ref, a0, a1, a2, a3, wout0, wout1, wout2, b_out, b_down, x_mine, x_other, c_mine, c_other, w_own, w_other,
    y_ref, stats_ref, normed_ref, m_other_ref, dn_ref, pack_own, pack_other,
    wout, a_scr, x_scr, c_scr, h_scr, up_scr, down_scr, bias_scr, g_scr, du_scr, gd, gu, gb, pack_scr, w_sem, pack_sem,
):
    step = pl.program_id(0)
    last = pl.num_programs(0) - 1
    core = where_ref[0]
    half, block = x_mine.shape
    units = DP
    fetch = []
    for i, ref in enumerate((w_own, w_other)):
        at = pl.ds(i * units, units)
        for j, (source, target) in enumerate(
            (
                (ref.at[pl.ds(0, DP), :], up_scr.at[:, at]),
                (ref.at[pl.ds(DP, units), :], down_scr.at[at, :]),
                (ref.at[pl.ds(DP + units, PAD), :], bias_scr.at[:, at]),
            )
        ):
            fetch.append(pltpu.make_async_copy(source, target, w_sem.at[i, j]))
    store = [
        pltpu.make_async_copy(pack_scr.at[i], ref, pack_sem.at[i]) for i, ref in enumerate((pack_own, pack_other))
    ]

    @pl.when(step == 0)
    def _():
        for copy in fetch:
            copy.start()
        start = 0
        for ref in (wout0, wout1, wout2):
            wout[start : start + ref.shape[0], :] = ref[...]
            start += ref.shape[0]
        for ref in (gd, gu, gb):
            ref[...] = jnp.zeros_like(ref)

    for i, a_ref in enumerate((a0, a1, a2, a3)):
        part = a_ref.shape[0]
        a_scr[i * part : (i + 1) * part, :] = a_ref[...]
    position = step * block + lax.broadcasted_iota(jnp.int32, (1, block), 1)
    valid = (position < where_ref[1]).astype(F32)
    stream = join_halves(x_scr, x_mine, x_other, core).astype(F32)
    branch = dot(wout[...], a_scr[...], 0, 0) + b_out[...].astype(F32).T
    hidden = stream + valid * branch
    h_scr[...] = hidden
    kept, scale, total = crms_stats(hidden)
    stats_ref[0:1, :] = scale
    stats_ref[1:2, :] = total
    normed = (kept * scale).astype(BF)
    normed_ref[...] = normed
    grad_out = join_halves(c_scr, c_mine, c_other, core)
    keep_row = lax.broadcasted_iota(jnp.int32, (DP, block), 0) < DS
    dm = jnp.where(keep_row, grad_out.astype(F32) * valid, 0.0).astype(BF)

    @pl.when(step == 0)
    def _():
        for copy in fetch:
            copy.wait()

    ones = jnp.ones((block, 128), BF)
    gb[2 * units :] += dot(dm, ones, 1, 0)
    for which in (1, 0):
        mine = slice(which * units, (which + 1) * units)

        for start in range(which * units, (which + 1) * units, UNIT_BLK):
            at = slice(start, start + UNIT_BLK)
            pre = dot(up_scr[:, at], normed, 0, 0) + bias_scr[0:1, at].astype(F32).T
            grad_act = dot(down_scr[at, :], dm, 1, 0)
            act, slope = gelu_pair(pre)
            act = act.astype(BF)
            grad_pre = (grad_act * slope).astype(BF)
            g_scr[at, :] = act
            du_scr[at, :] = grad_pre
            gd[at, :] += dot(act, dm, 1, 1)
            gu[:, at] += dot(normed, grad_pre, 1, 1)
            gb[at] += dot(grad_pre, ones, 1, 0)

        @pl.when(step == last)
        def _():
            pack_scr[which, 0:units, :] = gd[mine, :].astype(BF)
            pack_scr[which, units : units + DP, :] = gu[:, mine].astype(BF)
            pack_scr[which, units + DP :, :] = jnp.zeros((PAD, DP), BF)
            pack_scr[which, units + DP : units + DP + 1, :] = gb[mine].T[:1].astype(BF)
            pack_scr[which, units + DP + 1 : units + DP + 2, :] = gb[2 * units :].T[:1].astype(BF)
            store[which].start()

    own = pl.ds(pl.multiple_of(core * half, half), half)
    far = pl.ds(pl.multiple_of((1 - core) * half, half), half)
    m_part = h_scr
    column = b_down[...].astype(F32).T
    bias = jnp.where(core == 0, column[:half], column[half:])
    y_ref[...] = h_scr[own, :] + valid * bias
    m_part[...] = dot(down_scr[...], g_scr[...], 0, 0)
    y_ref[...] += valid * m_part[own, :]
    m_other_ref[...] = (valid * m_part[far, :]).astype(BF)
    dn_ref[...] = dot(up_scr[...], du_scr[...], 1, 0).astype(BF)

    @pl.when(step == last)
    def _():
        for copy in store:
            copy.wait()


def mlp(where, mixed, wout, b_out, b_down, stream, cot, weights):
    half, rows = stream[0].shape
    part = mixed[0].shape[0]
    units = DP
    block = ROWS_BLK
    pack = (units + DP + PAD, DP)
    anywhere = pl.BlockSpec(memory_space=pl.ANY)
    return call(
        mlp_body,
        "out_project_mlp",
        40,
        (rows // block,),
        [rows_spec(part, block)] * 4
        + [whole_spec(w.shape) for w in wout]
        + [whole_spec((1, DP))] * 2
        + [rows_spec(half, block)] * 4
        + [anywhere] * 2,
        [
            rows_spec(half, block),
            rows_spec(8, block),
            rows_spec(DP, block),
            rows_spec(half, block),
            rows_spec(DP, block),
        ]
        + [anywhere] * 2,
        [
            shape_of((half, rows), F32),
            shape_of((8, rows), F32),
            shape_of((DP, rows), BF),
            shape_of((half, rows), BF),
            shape_of((DP, rows), BF),
        ]
        + [shape_of(pack, BF)] * 2,
        [pltpu.VMEM((DP, DP), BF)]
        + [pltpu.VMEM((DP, block), BF)] * 3
        + [
            pltpu.VMEM((DP, block), F32),
            pltpu.VMEM((DP, 2 * units), BF),
            pltpu.VMEM((2 * units, DP), BF),
            pltpu.VMEM((PAD, 2 * units), BF),
            pltpu.VMEM((2 * units, block), BF),
            pltpu.VMEM((2 * units, block), BF),
            pltpu.VMEM((2 * units, DP), F32),
            pltpu.VMEM((DP, 2 * units), F32),
            pltpu.VMEM((2 * units + DP, 128), F32),
            pltpu.VMEM((2, *pack), BF),
            pltpu.SemaphoreType.DMA((2, 3)),
            pltpu.SemaphoreType.DMA((2,)),
        ],
        1,
    )(where, *mixed, *wout, b_out, b_down, *stream, *cot, *weights)


def out_back_body(
    where_ref, dn_mine, dn_other, normed_ref, stats_ref, c_mine, c_other, w0, w1, a0, a1,
    dh_ref, da_ref, pack_own, pack_other, c_scr, dh_scr, gw_scr, gb_scr,
):
    step = pl.program_id(0)
    core = where_ref[0]
    half, block = c_mine.shape
    position = step * block + lax.broadcasted_iota(jnp.int32, (1, block), 1)
    valid = (position < where_ref[1]).astype(F32)
    row_mask = lax.broadcasted_iota(jnp.int32, (DP, 1), 0) < DS
    grad_norm = dn_mine[...].astype(F32) + dn_other[...].astype(F32)
    normed = normed_ref[...].astype(F32)
    scale, total = stats_ref[0:1, :], stats_ref[1:2, :]
    inner = jnp.sum(grad_norm * normed, 0, keepdims=True) * (1.0 / DP)
    grad_out = join_halves(c_scr, c_mine, c_other, core).astype(F32)
    pulled = scale * (grad_norm - (normed + scale * total) * inner)
    grad_hidden = grad_out + jnp.where(row_mask, pulled, 0.0)
    dh_scr[...] = grad_hidden
    dh_ref[...] = dh_scr[pl.ds(pl.multiple_of(core * half, half), half), :]
    branch_f = jnp.where(row_mask, grad_hidden * valid, 0.0)
    branch = branch_f.astype(BF)
    part = a0.shape[0]
    da_ref[:part, :] = dot(w0[...], branch, 1, 0).astype(BF)
    da_ref[part:, :] = dot(w1[...], branch, 1, 0).astype(BF)

    @pl.when(step == 0)
    def _():
        gw_scr[...] = jnp.zeros_like(gw_scr)
        gb_scr[...] = jnp.zeros_like(gb_scr)

    gw_scr[:part] += dot(a0[...], branch, 1, 1)
    gw_scr[part:] += dot(a1[...], branch, 1, 1)
    gb_scr[...] += jnp.sum(branch_f, 1, keepdims=True)

    @pl.when(step == pl.num_programs(0) - 1)
    def _():
        for i, pack in enumerate((pack_own, pack_other)):
            pack[:part, :] = gw_scr[i * part : (i + 1) * part, :].astype(BF)
            pack[part:, :] = jnp.zeros((PAD, DP), BF)
            pack[part : part + 1, :] = gb_scr[...].T.astype(BF)


def out_back(where, dn, normed, stats, cot, weights, mixed):
    rows = normed.shape[1]
    half = cot[0].shape[0]
    part = mixed[0].shape[0]
    block = ROWS_BLK
    return call(
        out_back_body,
        "out_project_back",
        12,
        (rows // block,),
        [rows_spec(DP, block)] * 3
        + [rows_spec(8, block)]
        + [rows_spec(half, block)] * 2
        + [whole_spec((part, DP))] * 2
        + [rows_spec(part, block)] * 2,
        [
            rows_spec(half, block),
            rows_spec(2 * part, block),
            whole_spec((part + PAD, DP)),
            whole_spec((part + PAD, DP)),
        ],
        [
            shape_of((half, rows), F32),
            shape_of((2 * part, rows), BF),
            shape_of((part + PAD, DP), BF),
            shape_of((part + PAD, DP), BF),
        ],
        [
            pltpu.VMEM((DP, block), BF),
            pltpu.VMEM((DP, block), F32),
            pltpu.VMEM((2 * part, DP), F32),
            pltpu.VMEM((DP, 1), F32),
        ],
        1,
    )(where, *dn, normed, stats, *cot, *weights, *mixed)


def project_back_body(
    where_ref, g0, g1, g2, g3, g4, g5, normed_ref, w0, w1, dn_own_ref, dn_other_ref, inner_ref, p_scr, dn_scr, w_scr
):
    core = where_ref[0]
    outs = 3 * HS

    @pl.when(pl.program_id(0) == 0)
    def _():
        at = 0
        for ref in (w0, w1):
            for start in range(0, ref.shape[0], outs + PAD):
                w_scr[at : at + outs, :] = ref[start : start + outs, :]
                at += outs

    part = g0.shape[0]
    for i, ref in enumerate((g0, g1, g2, g3, g4, g5)):
        p_scr[i * part : (i + 1) * part, :] = ref[...]
    grad_norm = dot(w_scr[...], p_scr[...], 0, 0)
    dn_scr[...] = grad_norm
    half = DP // 2
    dn_own_ref[...] = dn_scr[pl.ds(pl.multiple_of(core * half, half), half), :]
    dn_other_ref[...] = dn_scr[pl.ds(pl.multiple_of((1 - core) * half, half), half), :].astype(BF)
    inner = jnp.sum(grad_norm * normed_ref[...].astype(F32), 0, keepdims=True)
    inner_ref[...] = jnp.broadcast_to(inner, inner_ref.shape)


def project_back(where, grads, normed, weights):
    part, rows = grads[0].shape
    half = DP // 2
    block = ROWS_BLK
    return call(
        project_back_body,
        "project_back",
        8,
        (rows // block,),
        [rows_spec(part, block)] * 6 + [rows_spec(DP, block)] + [whole_spec(w.shape) for w in weights],
        [rows_spec(half, block), rows_spec(half, block), rows_spec(8, block)],
        [shape_of((half, rows), F32), shape_of((half, rows), BF), shape_of((8, rows), F32)],
        [pltpu.VMEM((6 * part, block), BF), pltpu.VMEM((DP, block), F32), pltpu.VMEM((6 * part, DP), BF)],
        1,
    )(where, *grads, normed, *weights)


def swap(value, axis):
    return lax.ppermute(value, axis, [(0, 1), (1, 0)])


def cross(value):
    return lax.ppermute(value, ("core", "x"), [(1, 2), (2, 1)])


def after(value, *others):
    return lax.optimization_barrier((value, *others))[0]


def quarter(value, core, axis):
    size = value.shape[axis] // 2
    return lax.dynamic_slice_in_dim(value, core * size, size, axis)


def both(mine, other, core, axis):
    first = jnp.where(core == 0, mine, other)
    second = jnp.where(core == 0, other, mine)
    return jnp.concatenate([first, second], axis)


def pad_last(value):
    return jnp.pad(value, [(0, 0)] * (value.ndim - 1) + [(0, DP - value.shape[-1])])


def pad_rows(value, count):
    return jnp.pad(value, ((0, count - value.shape[0]), (0, 0)))


def sum_steps(value, index, count):
    levels = count.bit_length() - 1
    for level in range(levels):
        halves = value.reshape(2, -1, value.shape[-1])
        low = (index >> level) & 1 == 0
        keep = jnp.where(low, halves[0], halves[1])
        value = keep + (yield level, jnp.where(low, halves[1], halves[0]))
    for level in reversed(range(levels)):
        low = (index >> level) & 1 == 0
        got = yield level, value
        value = jnp.concatenate([jnp.where(low, value, got), jnp.where(low, got, value)])
    yield None, value


class ChipSum:
    def __init__(self, value, index, count):
        self.count = count
        self.steps = sum_steps(value, index, count)
        self.level, self.value = next(self.steps)
        self.got = None

    def send(self):
        if self.level is not None:
            pairs = [(i, i ^ (1 << self.level)) for i in range(self.count)]
            self.got = lax.ppermute(self.value, "zy", pairs)

    def take(self, *others):
        if self.level is not None:
            got = after(self.got, *others) if others else self.got
            self.level, self.value = self.steps.send(got)
            self.got = None
        return self.value

    def finish(self, *others):
        while self.level is not None:
            if self.got is None:
                self.send()
            self.take(*others)
        return self.value


def on_device(chips, stream, lengths, w_qkv, b_qkv, w_out, b_out, w_up, b_up, w_down, b_down, cotangent):
    core = lax.axis_index("core")
    chip = lax.axis_index("x")
    place = lax.axis_index("zy")
    stays = core == chip
    half, rows = stream.shape

    def home(value):
        return jnp.where(stays, value, cross(value))

    x_mine = home(stream)
    side = core[None].astype(jnp.int32)

    own_mlp = jnp.concatenate(
        [
            jnp.pad(quarter(w_up, core, 1), ((0, DP - DS), (0, 0))),
            pad_last(quarter(w_down, core, 0)),
            pad_rows(quarter(b_up, core, 0)[None], 256),
        ]
    )
    units = DP
    share = own_mlp.shape[0] // chips
    piece = swap(lax.dynamic_slice_in_dim(own_mlp, place * share, share, 0), "x")
    other_mlp = lax.all_gather(piece, "zy", axis=0, tiled=True)

    outs = 3 * HS
    heads = b_qkv.shape[1] // (2 * HS)
    head_w = pad_last(quarter(w_qkv, core, 1)).reshape(3, heads, HS, DP).swapaxes(0, 1).reshape(heads, outs, DP)
    head_b = quarter(b_qkv, core, 1).reshape(3, heads, HS).swapaxes(0, 1).reshape(heads, 1, outs)
    head_b = jnp.pad(head_b, ((0, 0), (0, PAD - 1), (0, DP - outs)))
    own_qkv = jnp.concatenate([head_w, head_b], 1).reshape(-1, DP)
    own_out = pad_last(quarter(w_out, core, 0))
    x_mine, own_qkv = lax.optimization_barrier((x_mine, own_qkv, piece, own_out))[:2]
    x_other = swap(x_mine, "core")
    other_qkv = swap(own_qkv, "x")
    part = own_out.shape[0]

    normed_one, stats_one, qkv_own, mixed_own, logs_own = norm_attend(side, x_mine, x_other, own_qkv)
    mixed_own_far = swap(mixed_own, "core")
    length = after(lengths, mixed_own)
    length = jnp.where(stays, length, swap(length.astype(F32), "core").astype(jnp.int32))
    where = jnp.concatenate([side, length])
    c_mine = home(after(cotangent, mixed_own))
    other_out = swap(after(own_out, mixed_own), "x")
    qkv_other, mixed_other, logs_other = more_attend(normed_one, other_qkv)
    mixed_other_far = swap(mixed_other, "core")
    c_mine = after(c_mine, mixed_other)
    c_other = swap(c_mine, "core")
    far_out = swap(after(jnp.concatenate([own_out, other_out]), mixed_other), "core")

    y_own, stats_two, normed_two, m_other, dn_two, pack_own, pack_other = mlp(
        where,
        (mixed_own, mixed_other, mixed_own_far, mixed_other_far),
        (own_out, other_out, far_out),
        jnp.pad(b_out, (0, 1))[None],
        jnp.pad(b_down, (0, 1))[None],
        (x_mine, x_other),
        (c_mine, c_other),
        (own_mlp, other_mlp),
    )
    dn_two_far = swap(dn_two, "core")
    got_mlp = swap(pack_other, "x")
    m_far = swap(m_other, "core")
    dh_own, grad_mixed, out_own, out_other = out_back(
        where,
        (dn_two, dn_two_far),
        normed_two,
        stats_two,
        (c_mine, c_other),
        (own_out, other_out),
        (mixed_own, mixed_other),
    )

    got_out = swap(out_other, "x")
    back = {}
    sets = {0: (qkv_own, mixed_own, logs_own), 1: (qkv_other, mixed_other, logs_other)}

    def run_head(which, head, *first):
        qkv, mixed, logs = sets[which]
        done = attend_back(after(qkv, *first), grad_mixed, mixed, logs, normed_one, head, which * heads + head)
        back[which, head] = done
        return done[0]

    last = run_head(1, 0, grad_mixed)
    last = run_head(1, 1, last)
    got_mlp = after(got_mlp, last)
    total_down = pack_own[:units] + got_mlp[:units]
    result = (y_own + after(m_far, last).astype(F32)).astype(BF)
    last = run_head(1, 2, last, result, total_down)
    sum_down = lax.psum(total_down, "zy")
    output = home(result)
    total_rest = jnp.concatenate([pack_own[units:] + got_mlp[units:], out_own + after(got_out, last)])
    rest = ChipSum(pad_rows(total_rest, 1024), place, chips)

    def qkv_pack(which):
        return pad_rows(jnp.concatenate([back[which, head][1] for head in range(heads)]), 640)

    got_qkv = swap(qkv_pack(1), "x")
    for head in range(heads):
        rest.send()
        last = run_head(0, head, last, rest.value, *([output] if head == heads - 1 else []))
        rest.take(last)
    rest.send()
    qkv = ChipSum(qkv_pack(0) + after(got_qkv, last), place, chips)
    qkv.send()
    normed_late = after(normed_one, qkv.value, rest.value, sum_down, last)
    dn_own, dn_other, inner = project_back(
        where,
        [back[which, head][0] for which in (0, 1) for head in range(heads)],
        normed_late,
        (own_qkv, other_qkv),
    )
    dn_far = swap(dn_other, "core")
    inner = inner[0:1] + swap(inner, "core")[0:1]
    row_mask = core * half + lax.broadcasted_iota(jnp.int32, (half, 1), 0) < DS
    scale_one, total_one = stats_one[0:1], stats_one[1:2]
    grad_in = dh_own + jnp.where(
        row_mask,
        scale_one * (dn_own + dn_far.astype(F32))
        - scale_one * scale_one * (x_mine.astype(F32) + total_one) * inner / DP,
        0.0,
    )
    grad_sent = grad_in.astype(BF)
    grad_got = cross(grad_sent)
    grad_stream = jnp.where(stays, grad_in, grad_got.astype(F32))
    def gather(mine, far, pick, axis):
        return both(pick(mine), pick(far), core, axis).astype(F32)

    def by_head(value):
        return value[: heads * (outs + PAD)].reshape(heads, outs + PAD, DP)

    def pick_w(value):
        return by_head(value)[:, :outs, :DS].reshape(heads, 3, HS, DS).swapaxes(0, 1).reshape(3, -1, DS)

    def pick_b(value):
        return by_head(value)[:, outs, :outs].reshape(heads, 3, HS).swapaxes(0, 1).reshape(3, -1)

    qkv.take(dn_own)
    qkv.send()
    rest.take(qkv.value)
    rest.send()
    qkv.take(grad_sent)
    qkv.send()
    far_down = swap(after(sum_down, qkv.value), "core")
    rest.take(qkv.value)
    rest.send()
    qkv.take()
    qkv.send()
    grad_w_down = gather(sum_down, far_down, lambda v: v[:, :DS], 0)
    qkv.take(grad_w_down)
    qkv.send()
    sum_rest = rest.finish(qkv.value)
    far_rest = swap(sum_rest, "core")
    qkv.take(grad_got)
    qkv.send()
    grad_w_up = gather(sum_rest, far_rest, lambda v: v[:DS], 1)
    sum_qkv = qkv.finish(grad_w_up)
    far_qkv = swap(sum_qkv, "core")

    edge = DP + PAD
    return (
        output,
        grad_stream,
        gather(sum_qkv, far_qkv, pick_w, 1),
        gather(sum_qkv, far_qkv, pick_b, 1),
        gather(sum_rest, far_rest, lambda v: v[edge : edge + part, :DS], 0),
        sum_rest[edge + part, :DS].astype(F32),
        grad_w_up,
        gather(sum_rest, far_rest, lambda v: v[DP], 0),
        grad_w_down,
        sum_rest[DP + 1, :DS].astype(F32),
    )


def solution(mesh):
    dp, mp = mesh.shape["dp"], mesh.shape["mp"]
    fine = Mesh(mesh.devices.reshape(dp // 2, 2, mp), ("zy", "core", "x"))
    seqs = ("zy", "core")
    placed = (
        P("x", seqs),
        P(seqs),
        P(None, "x", None),
        P(None, "x"),
        P("x", None),
        P(),
        P(None, "x"),
        P("x"),
        P("x", None),
        P(),
        P("x", seqs),
    )
    return jax.shard_map(
        functools.partial(on_device, dp // 2),
        mesh=fine,
        in_specs=placed,
        out_specs=(
            P("x", seqs),
            P("x", seqs),
            P(None, "x", None),
            P(None, "x"),
            P("x", None),
            P(),
            P(None, "x"),
            P("x"),
            P("x", None),
            P(),
        ),
        check_vma=False,
    )
```

```python
import functools

import jax
import jax.numpy as jnp
from jax import lax
from jax.experimental import pallas as pl
from jax.experimental.pallas import tpu as pltpu
from jax.sharding import Mesh
from jax.sharding import PartitionSpec as P

HS = 64
DS = 767
DP = 768
BLK = 256
EPSILON = 1e-05
NEGATIVE = -1e30
F32 = jnp.float32
BF = jnp.bfloat16
VMEM_BYTES = 56 * 1024 * 1024
ROWS_BLK = 512
UNIT_BLK = 256
PAD = 16
BACK_MICROS = (8, 3, 3, 4, 4, 4)


def dot(left, right, left_dim, right_dim):
    return lax.dot_general(
        left, right, (((left_dim,), (right_dim,)), ((), ())), preferred_element_type=F32
    )


def call(body, name, micros, grid, in_specs, out_specs, out_shape, scratch, prefetch=0):
    return pl.pallas_call(
        body,
        grid_spec=pltpu.PrefetchScalarGridSpec(
            num_scalar_prefetch=prefetch,
            grid=grid,
            in_specs=in_specs,
            out_specs=out_specs,
            scratch_shapes=scratch,
        ),
        out_shape=out_shape,
        compiler_params=pltpu.CompilerParams(vmem_limit_bytes=VMEM_BYTES),
        cost_estimate=pl.CostEstimate(flops=int(micros * 1e9), bytes_accessed=0, transcendentals=0),
        name=name,
    )


def rows_spec(height, block):
    return pl.BlockSpec((height, block), lambda i, *_: (0, i))


def whole_spec(shape):
    return pl.BlockSpec(shape, lambda i, *_: (0,) * len(shape), pipeline_mode=pl.Buffered(1))


def shape_of(shape, dtype):
    return jax.ShapeDtypeStruct(shape, dtype)


def join_halves(scratch, mine_ref, other_ref, core):
    half = mine_ref.shape[0]
    scratch[pl.ds(pl.multiple_of(core * half, half), half), :] = mine_ref[...]
    scratch[pl.ds(pl.multiple_of((1 - core) * half, half), half), :] = other_ref[...]
    return scratch[...]


def crms_stats(values):
    kept = jnp.where(lax.broadcasted_iota(jnp.int32, values.shape, 0) < DS, values, 0.0)
    total = jnp.sum(kept, 0, keepdims=True)
    squares = jnp.sum(kept * kept, 0, keepdims=True)
    scale = lax.rsqrt((squares + total * total) / DP + EPSILON)
    return kept, scale, total


def causal_tile():
    key_pos = lax.broadcasted_iota(jnp.int32, (BLK, BLK), 0)
    query_pos = lax.broadcasted_iota(jnp.int32, (BLK, BLK), 1)
    return key_pos <= query_pos


def attend_head(w_ref, normed_ref, qkv_ref, a_ref, log_ref, s_scr, p_scr):
    rows = normed_ref.shape[1]
    blocks = rows // BLK
    outs = 3 * HS
    bias = w_ref[outs : outs + 1, :outs].astype(F32).T
    qkv_ref[...] = (dot(w_ref[:outs, :], normed_ref[...], 1, 0) + bias).astype(BF)
    key_rows = qkv_ref[HS : 2 * HS, :].T
    queries = qkv_ref[:HS, :] * jnp.asarray(0.125, BF)
    allowed = causal_tile()

    def score(blk):
        at = slice(blk * BLK, (blk + 1) * BLK)
        count = (blk + 1) * BLK
        scores = dot(key_rows[:count], queries[:, at], 1, 0)
        if blk:
            s_scr[blk % 2, : count - BLK] = scores[: count - BLK]
        s_scr[blk % 2, count - BLK : count] = jnp.where(allowed, scores[count - BLK :], NEGATIVE)

    def soften(blk):
        count = (blk + 1) * BLK
        top = jnp.max(s_scr[blk % 2, :count], axis=0, keepdims=True)
        expo = jnp.exp(s_scr[blk % 2, :count] - top)
        total = jnp.sum(expo, axis=0, keepdims=True)
        p_scr[blk % 2, :count] = expo.astype(BF)
        log_ref[0, :, blk * BLK : count] = top + jnp.log(total)
        return total

    def mix(blk, total):
        count = (blk + 1) * BLK
        mixed = dot(qkv_ref[2 * HS :, :count], p_scr[blk % 2, :count], 1, 0)
        a_ref[:, blk * BLK : count] = (mixed * (1.0 / total)).astype(BF)

    score(0)
    totals = {}
    for blk in range(blocks):
        if blk + 1 < blocks:
            score(blk + 1)
        if blk:
            mix(blk - 1, totals[blk - 1])
        totals[blk] = soften(blk)
    mix(blocks - 1, totals[blocks - 1])


def norm_attend_body(
    where_ref, mine_ref, other_ref, w_ref, normed_ref, stats_ref, qkv_ref, a_ref, log_ref, s_scr, p_scr
):
    @pl.when(pl.program_id(0) == 0)
    def _():
        half = mine_ref.shape[0]
        core = where_ref[0]
        first = pl.ds(pl.multiple_of(core * half, half), half)
        second = pl.ds(pl.multiple_of((1 - core) * half, half), half)
        normed_ref[first, :] = mine_ref[...]
        normed_ref[second, :] = other_ref[...]
        for start in range(0, normed_ref.shape[1], BLK):
            at = slice(start, start + BLK)
            kept, scale, total = crms_stats(normed_ref[:, at].astype(F32))
            normed_ref[:, at] = (kept * scale).astype(BF)
            stats_ref[0:1, at] = scale
            stats_ref[1:2, at] = total

    attend_head(w_ref, normed_ref, qkv_ref, a_ref, log_ref, s_scr, p_scr)


def attend_specs(heads, rows):
    outs = 3 * HS
    ins = [pl.BlockSpec((outs + PAD, DP), lambda h, *_: (h, 0))]
    results = [
        pl.BlockSpec((outs, rows), lambda h, *_: (h, 0)),
        pl.BlockSpec((HS, rows), lambda h, *_: (h, 0)),
        pl.BlockSpec((1, 1, rows), lambda h, *_: (h, 0, 0)),
    ]
    shapes = [
        shape_of((heads * outs, rows), BF),
        shape_of((heads * HS, rows), BF),
        shape_of((heads, 1, rows), F32),
    ]
    scratch = [pltpu.VMEM((2, rows, BLK), F32), pltpu.VMEM((2, rows, BLK), BF)]
    return ins, results, shapes, scratch


def norm_attend(where, mine, other, weights):
    half, rows = mine.shape
    heads = weights.shape[0] // (3 * HS + PAD)
    ins, results, shapes, scratch = attend_specs(heads, rows)
    return call(
        norm_attend_body,
        "norm_attend",
        22,
        (heads,),
        [whole_spec((half, rows)), whole_spec((half, rows))] + ins,
        [whole_spec((DP, rows)), whole_spec((8, rows))] + results,
        [shape_of((DP, rows), BF), shape_of((8, rows), F32)] + shapes,
        scratch,
        1,
    )(where, mine, other, weights)


def more_attend_body(normed_ref, w_ref, qkv_ref, a_ref, log_ref, s_scr, p_scr):
    attend_head(w_ref, normed_ref, qkv_ref, a_ref, log_ref, s_scr, p_scr)


def more_attend(normed, weights):
    rows = normed.shape[1]
    heads = weights.shape[0] // (3 * HS + PAD)
    ins, results, shapes, scratch = attend_specs(heads, rows)
    return call(
        more_attend_body,
        "attend",
        20,
        (heads,),
        [whole_spec((DP, rows))] + ins,
        results,
        shapes,
        scratch,
    )(normed, weights)


def attend_back_body(
    qkv_ref, da_ref, a_ref, log_ref, normed_hbm, grad_ref, gw_ref,
    p_scr, ds_scr, s_scr, dp_scr, dq_scr, normed_scr, sem,
):
    fetch = pltpu.make_async_copy(normed_hbm, normed_scr, sem)
    fetch.start()
    rows = qkv_ref.shape[1]
    blocks = rows // BLK
    queries = qkv_ref[:HS, :] * jnp.asarray(0.125, BF)
    query_rows = queries.T
    key_rows = qkv_ref[HS : 2 * HS, :].T
    value_rows = qkv_ref[2 * HS :, :].T
    grad = da_ref[...]
    grad_rows = grad.T
    row_dot = jnp.sum(grad.astype(F32) * a_ref[...].astype(F32), axis=0, keepdims=True)
    logs = log_ref[0]
    allowed = causal_tile()

    def span(blk):
        return slice(blk * BLK, (blk + 1) * BLK)

    def score(blk):
        start = blk * BLK
        s_scr[blk % 2, :, start:] = dot(key_rows[span(blk)], queries[:, start:], 1, 0)
        dp_scr[blk % 2, :, start:] = dot(value_rows[span(blk)], grad[:, start:], 1, 0)

    def soften(blk):
        slot = blk % 2
        for query_blk in range(blk, blocks):
            at = span(query_blk)
            probs = jnp.exp(s_scr[slot, :, at] - logs[:, at])
            if query_blk == blk:
                probs = jnp.where(allowed, probs, 0.0)
            p_scr[slot, :, at] = probs.astype(BF)
            ds_scr[slot, :, at] = (probs * (dp_scr[slot, :, at] - row_dot[:, at])).astype(BF)

    def mix(blk):
        slot, start = blk % 2, blk * BLK
        grad_keys = dot(ds_scr[slot, :, start:], query_rows[start:], 1, 0)
        grad_values = dot(p_scr[slot, :, start:], grad_rows[start:], 1, 0)
        grad_queries = dot(qkv_ref[HS : 2 * HS, span(blk)], ds_scr[slot, :, start:], 1, 0)
        if blk:
            dq_scr[:, start:] += grad_queries
        else:
            dq_scr[...] = grad_queries
        grad_ref[HS : 2 * HS, span(blk)] = grad_keys.T.astype(BF)
        grad_ref[2 * HS :, span(blk)] = grad_values.T.astype(BF)

    score(0)
    for blk in range(blocks):
        if blk + 1 < blocks:
            score(blk + 1)
        if blk:
            mix(blk - 1)
        soften(blk)
    mix(blocks - 1)
    grad_ref[:HS, :] = (dq_scr[...] * 0.125).astype(BF)
    fetch.wait()
    outs = 3 * HS
    gw_ref[:outs, :] = dot(grad_ref[...], normed_scr[...], 1, 1).astype(BF)
    gw_ref[outs:, :] = jnp.zeros((PAD, DP), BF)
    gw_ref[outs : outs + 1, :outs] = jnp.sum(grad_ref[...].astype(F32), 1, keepdims=True).T.astype(BF)


def attend_back(qkv, grad, mixed, logs, normed, head, grad_head):
    rows = qkv.shape[1]
    outs = 3 * HS
    return call(
        attend_back_body,
        "attend_back",
        BACK_MICROS[grad_head],
        (1,),
        [
            pl.BlockSpec((outs, rows), lambda i: (head, 0)),
            pl.BlockSpec((HS, rows), lambda i: (grad_head, 0)),
            pl.BlockSpec((HS, rows), lambda i: (head, 0)),
            pl.BlockSpec((1, 1, rows), lambda i: (head, 0, 0)),
            pl.BlockSpec(memory_space=pl.ANY),
        ],
        [
            pl.BlockSpec((outs, rows), lambda i: (0, 0)),
            pl.BlockSpec((outs + PAD, DP), lambda i: (0, 0)),
        ],
        [shape_of((outs, rows), BF), shape_of((outs + PAD, DP), BF)],
        [
            pltpu.VMEM((2, BLK, rows), BF),
            pltpu.VMEM((2, BLK, rows), BF),
            pltpu.VMEM((2, BLK, rows), F32),
            pltpu.VMEM((2, BLK, rows), F32),
            pltpu.VMEM((HS, rows), F32),
            pltpu.VMEM((DP, rows), BF),
            pltpu.SemaphoreType.DMA(()),
        ],
    )(qkv, grad, mixed, logs, normed)


GELU_A = 0.7978845608028654
GELU_B = 0.044715


def gelu_pair(pre):
    square = pre * pre
    bent = jnp.tanh(GELU_A * pre * (1.0 + GELU_B * square))
    half_up = 0.5 * (1.0 + bent)
    slope = half_up + 0.5 * pre * (1.0 - bent * bent) * (GELU_A * (1.0 + 3.0 * GELU_B * square))
    return pre * half_up, slope


def mlp_body(
    where_ref, a0, a1, a2, a3, wout0, wout1, wout2, b_out, b_down, x_mine, x_other, c_mine, c_other, w_own, w_other,
    y_ref, stats_ref, normed_ref, m_other_ref, dn_ref, gd_own, gu_own, gd_other, gu_other,
    wout, a_scr, x_scr, c_scr, h_scr, up_scr, down_scr, bias_scr, pre_scr, back_scr, g_scr, du_scr, gd, gu, gb, pack_scr, w_sem, pack_sem,
):
    step = pl.program_id(0)
    last = pl.num_programs(0) - 1
    core = where_ref[0]
    half, block = x_mine.shape
    units = DP
    fetch = []
    for i, ref in enumerate((w_own, w_other)):
        at = pl.ds(i * units, units)
        for j, (source, target) in enumerate(
            (
                (ref.at[pl.ds(0, DP), :], up_scr.at[:, at]),
                (ref.at[pl.ds(DP, units), :], down_scr.at[at, :]),
                (ref.at[pl.ds(DP + units, PAD), :], bias_scr.at[:, at]),
            )
        ):
            fetch.append(pltpu.make_async_copy(source, target, w_sem.at[i, j]))
    split = ((gd_own, pl.ds(0, units)), (gu_own, pl.ds(units, DP + PAD)))
    split += ((gd_other, pl.ds(0, units)), (gu_other, pl.ds(units, DP + PAD)))
    store = [
        pltpu.make_async_copy(pack_scr.at[i // 2, at, :], ref, pack_sem.at[i]) for i, (ref, at) in enumerate(split)
    ]

    @pl.when(step == 0)
    def _():
        for copy in fetch:
            copy.start()
        start = 0
        for ref in (wout0, wout1, wout2):
            wout[start : start + ref.shape[0], :] = ref[...]
            start += ref.shape[0]
        for ref in (gd, gu, gb):
            ref[...] = jnp.zeros_like(ref)

    for i, a_ref in enumerate((a0, a1, a2, a3)):
        part = a_ref.shape[0]
        a_scr[i * part : (i + 1) * part, :] = a_ref[...]
    position = step * block + lax.broadcasted_iota(jnp.int32, (1, block), 1)
    valid = (position < where_ref[1]).astype(F32)
    stream = join_halves(x_scr, x_mine, x_other, core).astype(F32)
    branch = dot(wout[...], a_scr[...], 0, 0) + b_out[...].astype(F32).T
    hidden = stream + valid * branch
    h_scr[...] = hidden
    kept, scale, total = crms_stats(hidden)
    stats_ref[0:1, :] = scale
    stats_ref[1:2, :] = total
    normed = (kept * scale).astype(BF)
    normed_ref[...] = normed
    grad_out = join_halves(c_scr, c_mine, c_other, core)
    keep_row = lax.broadcasted_iota(jnp.int32, (DP, block), 0) < DS
    dm = jnp.where(keep_row, grad_out.astype(F32) * valid, 0.0).astype(BF)

    @pl.when(step == 0)
    def _():
        for copy in fetch:
            copy.wait()

    ones = jnp.ones((block, 128), BF)
    gb[2 * units :] += dot(dm, ones, 1, 0)
    starts = [which * units + start for which in (1, 0) for start in range(0, units, UNIT_BLK)]

    def expand(i):
        at = slice(starts[i], starts[i] + UNIT_BLK)
        pre_scr[i % 2] = dot(up_scr[:, at], normed, 0, 0)
        back_scr[i % 2] = dot(down_scr[at, :], dm, 1, 0)

    def bend(i):
        at = slice(starts[i], starts[i] + UNIT_BLK)
        act, slope = gelu_pair(pre_scr[i % 2] + bias_scr[0:1, at].astype(F32).T)
        g_scr[at, :] = act.astype(BF)
        du_scr[at, :] = (back_scr[i % 2] * slope).astype(BF)

    def collect(i):
        at = slice(starts[i], starts[i] + UNIT_BLK)
        gd[at, :] += dot(g_scr[at, :], dm, 1, 1)
        gu[:, at] += dot(normed, du_scr[at, :], 1, 1)
        gb[at] += dot(du_scr[at, :], ones, 1, 0)

    expand(0)
    for i in range(len(starts)):
        if i + 1 < len(starts):
            expand(i + 1)
        if i:
            collect(i - 1)
        bend(i)
    collect(len(starts) - 1)

    @pl.when(step == last)
    def _():
        for which in (1, 0):
            mine = slice(which * units, (which + 1) * units)
            pack_scr[which, 0:units, :] = gd[mine, :].astype(BF)
            pack_scr[which, units : units + DP, :] = gu[:, mine].astype(BF)
            pack_scr[which, units + DP :, :] = jnp.zeros((PAD, DP), BF)
            pack_scr[which, units + DP : units + DP + 1, :] = gb[mine].T[:1].astype(BF)
            pack_scr[which, units + DP + 1 : units + DP + 2, :] = gb[2 * units :].T[:1].astype(BF)
            store[2 * which].start()
            store[2 * which + 1].start()

    own = pl.ds(pl.multiple_of(core * half, half), half)
    far = pl.ds(pl.multiple_of((1 - core) * half, half), half)
    m_part = h_scr
    column = b_down[...].astype(F32).T
    bias = jnp.where(core == 0, column[:half], column[half:])
    y_ref[...] = h_scr[own, :] + valid * bias
    m_part[...] = dot(down_scr[...], g_scr[...], 0, 0)
    y_ref[...] += valid * m_part[own, :]
    m_other_ref[...] = (valid * m_part[far, :]).astype(BF)
    dn_ref[...] = dot(up_scr[...], du_scr[...], 1, 0).astype(BF)

    @pl.when(step == last)
    def _():
        for copy in store:
            copy.wait()


def mlp(where, mixed, wout, b_out, b_down, stream, cot, weights):
    half, rows = stream[0].shape
    part = mixed[0].shape[0]
    units = DP
    block = ROWS_BLK
    pack = (units + DP + PAD, DP)
    anywhere = pl.BlockSpec(memory_space=pl.ANY)
    return call(
        mlp_body,
        "out_project_mlp",
        40,
        (rows // block,),
        [rows_spec(part, block)] * 4
        + [whole_spec(w.shape) for w in wout]
        + [whole_spec((1, DP))] * 2
        + [rows_spec(half, block)] * 4
        + [anywhere] * 2,
        [
            rows_spec(half, block),
            rows_spec(8, block),
            rows_spec(DP, block),
            rows_spec(half, block),
            rows_spec(DP, block),
        ]
        + [anywhere] * 4,
        [
            shape_of((half, rows), F32),
            shape_of((8, rows), F32),
            shape_of((DP, rows), BF),
            shape_of((half, rows), BF),
            shape_of((DP, rows), BF),
        ]
        + [shape_of((units, DP), BF), shape_of((DP + PAD, DP), BF)] * 2,
        [pltpu.VMEM((DP, DP), BF)]
        + [pltpu.VMEM((DP, block), BF)] * 3
        + [
            pltpu.VMEM((DP, block), F32),
            pltpu.VMEM((DP, 2 * units), BF),
            pltpu.VMEM((2 * units, DP), BF),
            pltpu.VMEM((PAD, 2 * units), BF),
            pltpu.VMEM((2, UNIT_BLK, block), F32),
            pltpu.VMEM((2, UNIT_BLK, block), F32),
            pltpu.VMEM((2 * units, block), BF),
            pltpu.VMEM((2 * units, block), BF),
            pltpu.VMEM((2 * units, DP), F32),
            pltpu.VMEM((DP, 2 * units), F32),
            pltpu.VMEM((2 * units + DP, 128), F32),
            pltpu.VMEM((2, *pack), BF),
            pltpu.SemaphoreType.DMA((2, 3)),
            pltpu.SemaphoreType.DMA((4,)),
        ],
        1,
    )(where, *mixed, *wout, b_out, b_down, *stream, *cot, *weights)


def out_back_body(
    where_ref, dn_mine, dn_other, normed_ref, stats_ref, c_mine, c_other, w0, w1, a0, a1,
    dh_ref, da_ref, pack_own, pack_other, c_scr, dh_scr, gw_scr, gb_scr,
):
    step = pl.program_id(0)
    core = where_ref[0]
    half, block = c_mine.shape
    position = step * block + lax.broadcasted_iota(jnp.int32, (1, block), 1)
    valid = (position < where_ref[1]).astype(F32)
    row_mask = lax.broadcasted_iota(jnp.int32, (DP, 1), 0) < DS
    grad_norm = dn_mine[...].astype(F32) + dn_other[...].astype(F32)
    normed = normed_ref[...].astype(F32)
    scale, total = stats_ref[0:1, :], stats_ref[1:2, :]
    inner = jnp.sum(grad_norm * normed, 0, keepdims=True) * (1.0 / DP)
    grad_out = join_halves(c_scr, c_mine, c_other, core).astype(F32)
    pulled = scale * (grad_norm - (normed + scale * total) * inner)
    grad_hidden = grad_out + jnp.where(row_mask, pulled, 0.0)
    dh_scr[...] = grad_hidden
    dh_ref[...] = dh_scr[pl.ds(pl.multiple_of(core * half, half), half), :]
    branch_f = jnp.where(row_mask, grad_hidden * valid, 0.0)
    branch = branch_f.astype(BF)
    part = a0.shape[0]
    da_ref[:part, :] = dot(w0[...], branch, 1, 0).astype(BF)
    da_ref[part:, :] = dot(w1[...], branch, 1, 0).astype(BF)

    @pl.when(step == 0)
    def _():
        gw_scr[...] = jnp.zeros_like(gw_scr)
        gb_scr[...] = jnp.zeros_like(gb_scr)

    gw_scr[:part] += dot(a0[...], branch, 1, 1)
    gw_scr[part:] += dot(a1[...], branch, 1, 1)
    gb_scr[...] += jnp.sum(branch_f, 1, keepdims=True)

    @pl.when(step == pl.num_programs(0) - 1)
    def _():
        for i, pack in enumerate((pack_own, pack_other)):
            pack[:part, :] = gw_scr[i * part : (i + 1) * part, :].astype(BF)
            pack[part:, :] = jnp.zeros((PAD, DP), BF)
            pack[part : part + 1, :] = gb_scr[...].T.astype(BF)


def out_back(where, dn, normed, stats, cot, weights, mixed):
    rows = normed.shape[1]
    half = cot[0].shape[0]
    part = mixed[0].shape[0]
    block = ROWS_BLK
    return call(
        out_back_body,
        "out_project_back",
        12,
        (rows // block,),
        [rows_spec(DP, block)] * 3
        + [rows_spec(8, block)]
        + [rows_spec(half, block)] * 2
        + [whole_spec((part, DP))] * 2
        + [rows_spec(part, block)] * 2,
        [
            rows_spec(half, block),
            rows_spec(2 * part, block),
            whole_spec((part + PAD, DP)),
            whole_spec((part + PAD, DP)),
        ],
        [
            shape_of((half, rows), F32),
            shape_of((2 * part, rows), BF),
            shape_of((part + PAD, DP), BF),
            shape_of((part + PAD, DP), BF),
        ],
        [
            pltpu.VMEM((DP, block), BF),
            pltpu.VMEM((DP, block), F32),
            pltpu.VMEM((2 * part, DP), F32),
            pltpu.VMEM((DP, 1), F32),
        ],
        1,
    )(where, *dn, normed, stats, *cot, *weights, *mixed)


def project_back_body(
    where_ref, g0, g1, g2, g3, g4, g5, normed_ref, w0, w1, dn_own_ref, dn_other_ref, inner_ref, p_scr, dn_scr, w_scr
):
    core = where_ref[0]
    outs = 3 * HS

    @pl.when(pl.program_id(0) == 0)
    def _():
        at = 0
        for ref in (w0, w1):
            for start in range(0, ref.shape[0], outs + PAD):
                w_scr[at : at + outs, :] = ref[start : start + outs, :]
                at += outs

    part = g0.shape[0]
    for i, ref in enumerate((g0, g1, g2, g3, g4, g5)):
        p_scr[i * part : (i + 1) * part, :] = ref[...]
    grad_norm = dot(w_scr[...], p_scr[...], 0, 0)
    dn_scr[...] = grad_norm
    half = DP // 2
    dn_own_ref[...] = dn_scr[pl.ds(pl.multiple_of(core * half, half), half), :].astype(BF)
    dn_other_ref[...] = dn_scr[pl.ds(pl.multiple_of((1 - core) * half, half), half), :].astype(BF)
    inner = jnp.sum(grad_norm * normed_ref[...].astype(F32), 0, keepdims=True)
    inner_ref[...] = jnp.broadcast_to(inner, inner_ref.shape)


def project_back(where, grads, normed, weights):
    part, rows = grads[0].shape
    half = DP // 2
    block = ROWS_BLK
    return call(
        project_back_body,
        "project_back",
        8,
        (rows // block,),
        [rows_spec(part, block)] * 6 + [rows_spec(DP, block)] + [whole_spec(w.shape) for w in weights],
        [rows_spec(half, block), rows_spec(half, block), rows_spec(8, block)],
        [shape_of((half, rows), BF), shape_of((half, rows), BF), shape_of((8, rows), F32)],
        [pltpu.VMEM((6 * part, block), BF), pltpu.VMEM((DP, block), F32), pltpu.VMEM((6 * part, DP), BF)],
        1,
    )(where, *grads, normed, *weights)


def swap(value, axis):
    return lax.ppermute(value, axis, [(0, 1), (1, 0)])


def cross(value):
    return lax.ppermute(value, ("core", "x"), [(1, 2), (2, 1)])


def after(value, *others):
    return lax.optimization_barrier((value, *others))[0]


def quarter(value, core, axis):
    size = value.shape[axis] // 2
    return lax.dynamic_slice_in_dim(value, core * size, size, axis)


def both(mine, other, core, axis):
    first = jnp.where(core == 0, mine, other)
    second = jnp.where(core == 0, other, mine)
    return jnp.concatenate([first, second], axis)


def pad_last(value):
    return jnp.pad(value, [(0, 0)] * (value.ndim - 1) + [(0, DP - value.shape[-1])])


def pad_rows(value, count):
    return jnp.pad(value, ((0, count - value.shape[0]), (0, 0)))


def sum_steps(value, index, count):
    levels = count.bit_length() - 1
    for level in range(levels):
        halves = value.reshape(2, -1, value.shape[-1])
        low = (index >> level) & 1 == 0
        keep = jnp.where(low, halves[0], halves[1])
        value = keep + (yield level, jnp.where(low, halves[1], halves[0]))
    for level in reversed(range(levels)):
        low = (index >> level) & 1 == 0
        got = yield level, value
        value = jnp.concatenate([jnp.where(low, value, got), jnp.where(low, got, value)])
    yield None, value


class ChipSum:
    def __init__(self, value, index, count):
        self.count = count
        self.steps = sum_steps(value, index, count)
        self.level, self.value = next(self.steps)
        self.got = None

    def send(self):
        if self.level is not None:
            pairs = [(i, i ^ (1 << self.level)) for i in range(self.count)]
            self.got = lax.ppermute(self.value, "zy", pairs)

    def take(self, *others):
        if self.level is not None:
            got = after(self.got, *others) if others else self.got
            self.level, self.value = self.steps.send(got)
            self.got = None
        return self.value

    def finish(self, *others):
        while self.level is not None:
            if self.got is None:
                self.send()
            self.take(*others)
        return self.value


def on_device(chips, stream, lengths, w_qkv, b_qkv, w_out, b_out, w_up, b_up, w_down, b_down, cotangent):
    core = lax.axis_index("core")
    chip = lax.axis_index("x")
    place = lax.axis_index("zy")
    stays = core == chip
    half, rows = stream.shape

    def home(value):
        return jnp.where(stays, value, cross(value))

    side = core[None].astype(jnp.int32)

    own_out = pad_last(quarter(w_out, core, 0))
    part = own_out.shape[0]
    units = DP
    low = units + DP + PAD
    own_mlp = jnp.concatenate(
        [
            jnp.pad(quarter(w_up, core, 1), ((0, DP - DS), (0, 0))),
            pad_last(quarter(w_down, core, 0)),
            pad_rows(quarter(b_up, core, 0)[None], PAD),
            pad_rows(own_out, 256 - PAD),
        ]
    )
    share = own_mlp.shape[0] // chips
    piece = lax.dynamic_slice_in_dim(own_mlp, place * share, share, 0)
    got_piece = swap(piece, "x")
    x_mine = home(stream)
    other_mlp = lax.all_gather(got_piece, "zy", axis=0, tiled=True)

    outs = 3 * HS
    heads = b_qkv.shape[1] // (2 * HS)
    head_w = pad_last(quarter(w_qkv, core, 1)).reshape(3, heads, HS, DP).swapaxes(0, 1).reshape(heads, outs, DP)
    head_b = quarter(b_qkv, core, 1).reshape(3, heads, HS).swapaxes(0, 1).reshape(heads, 1, outs)
    head_b = jnp.pad(head_b, ((0, 0), (0, PAD - 1), (0, DP - outs)))
    own_qkv = jnp.concatenate([head_w, head_b], 1).reshape(-1, DP)
    x_mine, own_qkv = lax.optimization_barrier((x_mine, own_qkv, got_piece))[:2]
    x_other = swap(x_mine, "core")
    other_qkv = swap(own_qkv, "x")

    normed_one, stats_one, qkv_own, mixed_own, logs_own = norm_attend(side, x_mine, x_other, own_qkv)
    mixed_own_far = swap(mixed_own, "core")
    length = after(lengths, mixed_own)
    length = jnp.where(stays, length, swap(length.astype(F32), "core").astype(jnp.int32))
    where = jnp.concatenate([side, length])
    c_mine = home(after(cotangent, mixed_own))
    qkv_other, mixed_other, logs_other = more_attend(normed_one, other_qkv)
    mixed_other_far = swap(mixed_other, "core")
    c_mine = after(c_mine, mixed_other)
    c_other = swap(c_mine, "core")
    other_out = other_mlp[low : low + part]
    far_out = swap(after(jnp.concatenate([own_out, other_out]), mixed_other), "core")

    y_own, stats_two, normed_two, m_other, dn_two, gd_own, gu_own, gd_other, gu_other = mlp(
        where,
        (mixed_own, mixed_other, mixed_own_far, mixed_other_far),
        (own_out, other_out, far_out),
        jnp.pad(b_out, (0, 1))[None],
        jnp.pad(b_down, (0, 1))[None],
        (x_mine, x_other),
        (c_mine, c_other),
        (own_mlp, other_mlp),
    )
    dn_two_far = swap(dn_two, "core")
    got_down = swap(gd_other, "x")
    got_up = swap(gu_other, "x")
    m_far = swap(m_other, "core")
    dh_own, grad_mixed, out_own, out_other = out_back(
        where,
        (dn_two, dn_two_far),
        normed_two,
        stats_two,
        (c_mine, c_other),
        (own_out, other_out),
        (mixed_own, mixed_other),
    )

    got_out = swap(out_other, "x")
    back = {}
    sets = {0: (qkv_own, mixed_own, logs_own), 1: (qkv_other, mixed_other, logs_other)}

    def run_head(which, head, *first):
        qkv, mixed, logs = sets[which]
        done = attend_back(after(qkv, *first), grad_mixed, mixed, logs, normed_one, head, which * heads + head)
        back[which, head] = done
        return done[0]

    total_down = gd_own + after(got_down, grad_mixed)
    last = run_head(1, 0, grad_mixed, total_down)
    sum_down = lax.psum(total_down, "zy")
    last = run_head(1, 1, last)
    result = (y_own + after(m_far, last).astype(F32)).astype(BF)
    last = run_head(1, 2, last, result)
    total_rest = jnp.concatenate([gu_own + after(got_up, last), out_own + after(got_out, last)])
    rest = ChipSum(pad_rows(total_rest, 1024), place, chips)
    output = home(after(result, total_rest))

    def qkv_pack(which):
        return pad_rows(jnp.concatenate([back[which, head][1] for head in range(heads)]), 640)

    got_qkv = swap(qkv_pack(1), "x")
    rest.send()
    for head in range(heads):
        last = run_head(0, head, last, rest.value)
        if head:
            rest.take(last)
            rest.send()
    qkv = ChipSum(qkv_pack(0) + after(got_qkv, last), place, chips)
    qkv.send()
    normed_late = after(normed_one, qkv.value, rest.value, output, last)
    dn_own, dn_other, inner = project_back(
        where,
        [back[which, head][0] for which in (0, 1) for head in range(heads)],
        normed_late,
        (own_qkv, other_qkv),
    )
    rest.take(dn_own)
    rest.send()
    qkv.take(dn_own)
    qkv.send()
    dn_far = swap(after(dn_other, rest.value, qkv.value, sum_down), "core")
    inner = inner[0:1] + swap(inner, "core")[0:1]
    qkv.take(dn_far)
    qkv.send()
    dn_far = after(dn_far, qkv.value)
    row_mask = core * half + lax.broadcasted_iota(jnp.int32, (half, 1), 0) < DS
    scale_one, total_one = stats_one[0:1], stats_one[1:2]
    grad_in = dh_own + jnp.where(
        row_mask,
        scale_one * (dn_own.astype(F32) + dn_far.astype(F32))
        - scale_one * scale_one * (x_mine.astype(F32) + total_one) * inner / DP,
        0.0,
    )
    grad_sent = grad_in.astype(BF)
    grad_got = cross(grad_sent)
    grad_stream = jnp.where(stays, grad_in, grad_got.astype(F32))
    def gather(mine, far, pick, axis):
        return both(pick(mine), pick(far), core, axis).astype(F32)

    def by_head(value):
        return value[: heads * (outs + PAD)].reshape(heads, outs + PAD, DP)

    def pick_w(value):
        return by_head(value)[:, :outs, :DS].reshape(heads, 3, HS, DS).swapaxes(0, 1).reshape(3, -1, DS)

    def pick_b(value):
        return by_head(value)[:, outs, :outs].reshape(heads, 3, HS).swapaxes(0, 1).reshape(3, -1)

    rest.take(grad_sent)
    rest.send()
    far_down = swap(after(sum_down, grad_sent), "core")
    qkv.take(grad_sent)
    qkv.send()
    rest.take(qkv.value)
    rest.send()
    grad_w_down = gather(sum_down, far_down, lambda v: v[:, :DS], 0)
    qkv.take(grad_w_down)
    qkv.send()
    qkv.take()
    qkv.send()
    sum_rest = rest.finish(qkv.value)
    far_rest = swap(sum_rest, "core")
    edge = DP + PAD
    grad_w_up = gather(sum_rest, far_rest, lambda v: v[:DS], 1)
    grad_w_out = gather(sum_rest, far_rest, lambda v: v[edge : edge + part, :DS], 0)
    sum_qkv = qkv.finish(grad_w_up, grad_w_out, grad_stream)
    far_qkv = swap(sum_qkv, "core")

    return (
        output,
        grad_stream,
        gather(sum_qkv, far_qkv, pick_w, 1),
        gather(sum_qkv, far_qkv, pick_b, 1),
        grad_w_out,
        sum_rest[edge + part, :DS].astype(F32),
        grad_w_up,
        gather(sum_rest, far_rest, lambda v: v[DP], 0),
        grad_w_down,
        sum_rest[DP + 1, :DS].astype(F32),
    )


def solution(mesh):
    dp, mp = mesh.shape["dp"], mesh.shape["mp"]
    fine = Mesh(mesh.devices.reshape(dp // 2, 2, mp), ("zy", "core", "x"))
    seqs = ("zy", "core")
    placed = (
        P("x", seqs),
        P(seqs),
        P(None, "x", None),
        P(None, "x"),
        P("x", None),
        P(),
        P(None, "x"),
        P("x"),
        P("x", None),
        P(),
        P("x", seqs),
    )
    return jax.shard_map(
        functools.partial(on_device, dp // 2),
        mesh=fine,
        in_specs=placed,
        out_specs=(
            P("x", seqs),
            P("x", seqs),
            P(None, "x", None),
            P(None, "x"),
            P("x", None),
            P(),
            P(None, "x"),
            P("x"),
            P("x", None),
            P(),
        ),
        check_vma=False,
    )
```

```python
import functools

import jax
import jax.numpy as jnp
from jax import lax
from jax.experimental import pallas as pl
from jax.experimental.pallas import tpu as pltpu
from jax.sharding import Mesh
from jax.sharding import PartitionSpec as P

HS = 64
DS = 767
DP = 768
BLK = 256
EPSILON = 1e-05
NEGATIVE = -1e30
F32 = jnp.float32
BF = jnp.bfloat16
VMEM_BYTES = 56 * 1024 * 1024
ROWS_BLK = 512
UNIT_BLK = 256
PAD = 16
BACK_MICROS = (8, 3, 3, 4, 4, 4)


def dot(left, right, left_dim, right_dim):
    return lax.dot_general(
        left, right, (((left_dim,), (right_dim,)), ((), ())), preferred_element_type=F32
    )


def call(body, name, micros, grid, in_specs, out_specs, out_shape, scratch, prefetch=0):
    return pl.pallas_call(
        body,
        grid_spec=pltpu.PrefetchScalarGridSpec(
            num_scalar_prefetch=prefetch,
            grid=grid,
            in_specs=in_specs,
            out_specs=out_specs,
            scratch_shapes=scratch,
        ),
        out_shape=out_shape,
        compiler_params=pltpu.CompilerParams(vmem_limit_bytes=VMEM_BYTES),
        cost_estimate=pl.CostEstimate(flops=int(micros * 1e9), bytes_accessed=0, transcendentals=0),
        name=name,
    )


def rows_spec(height, block):
    return pl.BlockSpec((height, block), lambda i, *_: (0, i))


def whole_spec(shape):
    return pl.BlockSpec(shape, lambda i, *_: (0,) * len(shape), pipeline_mode=pl.Buffered(1))


def shape_of(shape, dtype):
    return jax.ShapeDtypeStruct(shape, dtype)


def join_halves(scratch, mine_ref, other_ref, core):
    half = mine_ref.shape[0]
    scratch[pl.ds(pl.multiple_of(core * half, half), half), :] = mine_ref[...]
    scratch[pl.ds(pl.multiple_of((1 - core) * half, half), half), :] = other_ref[...]
    return scratch[...]


def crms_stats(values):
    kept = jnp.where(lax.broadcasted_iota(jnp.int32, values.shape, 0) < DS, values, 0.0)
    total = jnp.sum(kept, 0, keepdims=True)
    squares = jnp.sum(kept * kept, 0, keepdims=True)
    scale = lax.rsqrt((squares + total * total) / DP + EPSILON)
    return kept, scale, total


def causal_tile():
    key_pos = lax.broadcasted_iota(jnp.int32, (BLK, BLK), 0)
    query_pos = lax.broadcasted_iota(jnp.int32, (BLK, BLK), 1)
    return key_pos <= query_pos


def attend_head(w_ref, normed_ref, qkv_ref, a_ref, log_ref, s_scr, p_scr):
    rows = normed_ref.shape[1]
    blocks = rows // BLK
    outs = 3 * HS
    bias = w_ref[outs : outs + 1, :outs].astype(F32).T
    qkv_ref[...] = (dot(w_ref[:outs, :], normed_ref[...], 1, 0) + bias).astype(BF)
    key_rows = qkv_ref[HS : 2 * HS, :].T
    queries = qkv_ref[:HS, :] * jnp.asarray(0.125, BF)
    allowed = causal_tile()

    def score(blk):
        at = slice(blk * BLK, (blk + 1) * BLK)
        count = (blk + 1) * BLK
        scores = dot(key_rows[:count], queries[:, at], 1, 0)
        if blk:
            s_scr[blk % 2, : count - BLK] = scores[: count - BLK]
        s_scr[blk % 2, count - BLK : count] = jnp.where(allowed, scores[count - BLK :], NEGATIVE)

    def soften(blk):
        count = (blk + 1) * BLK
        top = jnp.max(s_scr[blk % 2, :count], axis=0, keepdims=True)
        expo = jnp.exp(s_scr[blk % 2, :count] - top)
        total = jnp.sum(expo, axis=0, keepdims=True)
        p_scr[blk % 2, :count] = expo.astype(BF)
        log_ref[0, :, blk * BLK : count] = top + jnp.log(total)
        return total

    def mix(blk, total):
        count = (blk + 1) * BLK
        mixed = dot(qkv_ref[2 * HS :, :count], p_scr[blk % 2, :count], 1, 0)
        a_ref[:, blk * BLK : count] = (mixed * (1.0 / total)).astype(BF)

    score(0)
    totals = {}
    for blk in range(blocks):
        if blk + 1 < blocks:
            score(blk + 1)
        if blk:
            mix(blk - 1, totals[blk - 1])
        totals[blk] = soften(blk)
    mix(blocks - 1, totals[blocks - 1])


def norm_attend_body(
    where_ref, mine_ref, other_ref, w_ref, normed_ref, stats_ref, qkv_ref, a_ref, log_ref, s_scr, p_scr
):
    @pl.when(pl.program_id(0) == 0)
    def _():
        half = mine_ref.shape[0]
        core = where_ref[0]
        first = pl.ds(pl.multiple_of(core * half, half), half)
        second = pl.ds(pl.multiple_of((1 - core) * half, half), half)
        normed_ref[first, :] = mine_ref[...]
        normed_ref[second, :] = other_ref[...]
        for start in range(0, normed_ref.shape[1], BLK):
            at = slice(start, start + BLK)
            kept, scale, total = crms_stats(normed_ref[:, at].astype(F32))
            normed_ref[:, at] = (kept * scale).astype(BF)
            stats_ref[0:1, at] = scale
            stats_ref[1:2, at] = total

    attend_head(w_ref, normed_ref, qkv_ref, a_ref, log_ref, s_scr, p_scr)


def attend_specs(heads, rows):
    outs = 3 * HS
    ins = [pl.BlockSpec((outs + PAD, DP), lambda h, *_: (h, 0))]
    results = [
        pl.BlockSpec((outs, rows), lambda h, *_: (h, 0)),
        pl.BlockSpec((HS, rows), lambda h, *_: (h, 0)),
        pl.BlockSpec((1, 1, rows), lambda h, *_: (h, 0, 0)),
    ]
    shapes = [
        shape_of((heads * outs, rows), BF),
        shape_of((heads * HS, rows), BF),
        shape_of((heads, 1, rows), F32),
    ]
    scratch = [pltpu.VMEM((2, rows, BLK), F32), pltpu.VMEM((2, rows, BLK), BF)]
    return ins, results, shapes, scratch


def norm_attend(where, mine, other, weights):
    half, rows = mine.shape
    heads = weights.shape[0] // (3 * HS + PAD)
    ins, results, shapes, scratch = attend_specs(heads, rows)
    return call(
        norm_attend_body,
        "norm_attend",
        22,
        (heads,),
        [whole_spec((half, rows)), whole_spec((half, rows))] + ins,
        [whole_spec((DP, rows)), whole_spec((8, rows))] + results,
        [shape_of((DP, rows), BF), shape_of((8, rows), F32)] + shapes,
        scratch,
        1,
    )(where, mine, other, weights)


def more_attend_body(normed_ref, w_ref, qkv_ref, a_ref, log_ref, s_scr, p_scr):
    attend_head(w_ref, normed_ref, qkv_ref, a_ref, log_ref, s_scr, p_scr)


def more_attend(normed, weights):
    rows = normed.shape[1]
    heads = weights.shape[0] // (3 * HS + PAD)
    ins, results, shapes, scratch = attend_specs(heads, rows)
    return call(
        more_attend_body,
        "attend",
        20,
        (heads,),
        [whole_spec((DP, rows))] + ins,
        results,
        shapes,
        scratch,
    )(normed, weights)


def attend_back_body(
    qkv_ref, da_ref, a_ref, log_ref, normed_hbm, grad_ref, gw_ref,
    p_scr, ds_scr, s_scr, dp_scr, dq_scr, normed_scr, sem,
):
    fetch = pltpu.make_async_copy(normed_hbm, normed_scr, sem)
    fetch.start()
    rows = qkv_ref.shape[1]
    blocks = rows // BLK
    queries = qkv_ref[:HS, :] * jnp.asarray(0.125, BF)
    query_rows = queries.T
    key_rows = qkv_ref[HS : 2 * HS, :].T
    value_rows = qkv_ref[2 * HS :, :].T
    grad = da_ref[...]
    grad_rows = grad.T
    row_dot = jnp.sum(grad.astype(F32) * a_ref[...].astype(F32), axis=0, keepdims=True)
    logs = log_ref[0]
    allowed = causal_tile()

    def span(blk):
        return slice(blk * BLK, (blk + 1) * BLK)

    def score(blk):
        start = blk * BLK
        s_scr[blk % 2, :, start:] = dot(key_rows[span(blk)], queries[:, start:], 1, 0)
        dp_scr[blk % 2, :, start:] = dot(value_rows[span(blk)], grad[:, start:], 1, 0)

    def soften(blk):
        slot = blk % 2
        for query_blk in range(blk, blocks):
            at = span(query_blk)
            probs = jnp.exp(s_scr[slot, :, at] - logs[:, at])
            if query_blk == blk:
                probs = jnp.where(allowed, probs, 0.0)
            p_scr[slot, :, at] = probs.astype(BF)
            ds_scr[slot, :, at] = (probs * (dp_scr[slot, :, at] - row_dot[:, at])).astype(BF)

    def mix(blk):
        slot, start = blk % 2, blk * BLK
        grad_keys = dot(ds_scr[slot, :, start:], query_rows[start:], 1, 0)
        grad_values = dot(p_scr[slot, :, start:], grad_rows[start:], 1, 0)
        grad_queries = dot(qkv_ref[HS : 2 * HS, span(blk)], ds_scr[slot, :, start:], 1, 0)
        if blk:
            dq_scr[:, start:] += grad_queries
        else:
            dq_scr[...] = grad_queries
        grad_ref[HS : 2 * HS, span(blk)] = grad_keys.T.astype(BF)
        grad_ref[2 * HS :, span(blk)] = grad_values.T.astype(BF)

    score(0)
    for blk in range(blocks):
        if blk + 1 < blocks:
            score(blk + 1)
        if blk:
            mix(blk - 1)
        soften(blk)
    mix(blocks - 1)
    grad_ref[:HS, :] = (dq_scr[...] * 0.125).astype(BF)
    fetch.wait()
    outs = 3 * HS
    gw_ref[:outs, :] = dot(grad_ref[...], normed_scr[...], 1, 1).astype(BF)
    gw_ref[outs:, :] = jnp.zeros((PAD, DP), BF)
    gw_ref[outs : outs + 1, :outs] = jnp.sum(grad_ref[...].astype(F32), 1, keepdims=True).T.astype(BF)


def attend_back(qkv, grad, mixed, logs, normed, head, grad_head):
    rows = qkv.shape[1]
    outs = 3 * HS
    return call(
        attend_back_body,
        "attend_back",
        BACK_MICROS[grad_head],
        (1,),
        [
            pl.BlockSpec((outs, rows), lambda i: (head, 0)),
            pl.BlockSpec((HS, rows), lambda i: (grad_head, 0)),
            pl.BlockSpec((HS, rows), lambda i: (head, 0)),
            pl.BlockSpec((1, 1, rows), lambda i: (head, 0, 0)),
            pl.BlockSpec(memory_space=pl.ANY),
        ],
        [
            pl.BlockSpec((outs, rows), lambda i: (0, 0)),
            pl.BlockSpec((outs + PAD, DP), lambda i: (0, 0)),
        ],
        [shape_of((outs, rows), BF), shape_of((outs + PAD, DP), BF)],
        [
            pltpu.VMEM((2, BLK, rows), BF),
            pltpu.VMEM((2, BLK, rows), BF),
            pltpu.VMEM((2, BLK, rows), F32),
            pltpu.VMEM((2, BLK, rows), F32),
            pltpu.VMEM((HS, rows), F32),
            pltpu.VMEM((DP, rows), BF),
            pltpu.SemaphoreType.DMA(()),
        ],
    )(qkv, grad, mixed, logs, normed)


GELU_A = 0.7978845608028654
GELU_B = 0.044715


def gelu_pair(pre):
    square = pre * pre
    bent = jnp.tanh(GELU_A * pre * (1.0 + GELU_B * square))
    half_up = 0.5 * (1.0 + bent)
    slope = half_up + 0.5 * pre * (1.0 - bent * bent) * (GELU_A * (1.0 + 3.0 * GELU_B * square))
    return pre * half_up, slope


def mlp_body(
    where_ref, a0, a1, a2, a3, wout0, wout1, wout2, wout3, b_out, b_down, x_mine, x_other, c_mine, c_other, w_own, w_other,
    y_ref, stats_ref, normed_ref, m_other_ref, dn_ref, gd_own, gu_own, gd_other, gu_other,
    wout, a_scr, x_scr, c_scr, h_scr, up_scr, down_scr, bias_scr, pre_scr, back_scr, g_scr, du_scr, gd, gu, gb, pack_scr, w_sem, pack_sem,
):
    step = pl.program_id(0)
    last = pl.num_programs(0) - 1
    core = where_ref[0]
    half, block = x_mine.shape
    units = DP
    fetch = []
    for i, ref in enumerate((w_own, w_other)):
        at = pl.ds(i * units, units)
        for j, (source, target) in enumerate(
            (
                (ref.at[pl.ds(0, DP), :], up_scr.at[:, at]),
                (ref.at[pl.ds(DP, units), :], down_scr.at[at, :]),
                (ref.at[pl.ds(DP + units + 2 * a0.shape[0], PAD), :], bias_scr.at[:, at]),
            )
        ):
            fetch.append(pltpu.make_async_copy(source, target, w_sem.at[i, j]))
    split = ((gd_own, pl.ds(0, units)), (gu_own, pl.ds(units, DP + PAD)))
    split += ((gd_other, pl.ds(0, units)), (gu_other, pl.ds(units, DP + PAD)))
    store = [
        pltpu.make_async_copy(pack_scr.at[i // 2, at, :], ref, pack_sem.at[i]) for i, (ref, at) in enumerate(split)
    ]

    @pl.when(step == 0)
    def _():
        for copy in fetch:
            copy.start()
        start = 0
        for ref in (wout0, wout1, wout2, wout3):
            wout[start : start + ref.shape[0], :] = ref[...]
            start += ref.shape[0]
        for ref in (gd, gu, gb):
            ref[...] = jnp.zeros_like(ref)

    for i, a_ref in enumerate((a0, a1, a2, a3)):
        part = a_ref.shape[0]
        a_scr[i * part : (i + 1) * part, :] = a_ref[...]
    position = step * block + lax.broadcasted_iota(jnp.int32, (1, block), 1)
    valid = (position < where_ref[1]).astype(F32)
    stream = join_halves(x_scr, x_mine, x_other, core).astype(F32)
    branch = dot(wout[...], a_scr[...], 0, 0) + b_out[...].astype(F32).T
    hidden = stream + valid * branch
    h_scr[...] = hidden
    kept, scale, total = crms_stats(hidden)
    stats_ref[0:1, :] = scale
    stats_ref[1:2, :] = total
    normed = (kept * scale).astype(BF)
    normed_ref[...] = normed
    grad_out = join_halves(c_scr, c_mine, c_other, core)
    keep_row = lax.broadcasted_iota(jnp.int32, (DP, block), 0) < DS
    dm = jnp.where(keep_row, grad_out.astype(F32) * valid, 0.0).astype(BF)

    @pl.when(step == 0)
    def _():
        for copy in fetch:
            copy.wait()

    ones = jnp.ones((block, 128), BF)
    gb[2 * units :] += dot(dm, ones, 1, 0)
    starts = [which * units + start for which in (1, 0) for start in range(0, units, UNIT_BLK)]

    def expand(i):
        at = slice(starts[i], starts[i] + UNIT_BLK)
        pre_scr[i % 2] = dot(up_scr[:, at], normed, 0, 0)
        back_scr[i % 2] = dot(down_scr[at, :], dm, 1, 0)

    def bend(i):
        at = slice(starts[i], starts[i] + UNIT_BLK)
        act, slope = gelu_pair(pre_scr[i % 2] + bias_scr[0:1, at].astype(F32).T)
        g_scr[at, :] = act.astype(BF)
        du_scr[at, :] = (back_scr[i % 2] * slope).astype(BF)

    def collect(i):
        at = slice(starts[i], starts[i] + UNIT_BLK)
        gd[at, :] += dot(g_scr[at, :], dm, 1, 1)
        gu[:, at] += dot(normed, du_scr[at, :], 1, 1)
        gb[at] += dot(du_scr[at, :], ones, 1, 0)

    expand(0)
    for i in range(len(starts)):
        if i + 1 < len(starts):
            expand(i + 1)
        if i:
            collect(i - 1)
        bend(i)
    collect(len(starts) - 1)

    @pl.when(step == last)
    def _():
        for which in (1, 0):
            mine = slice(which * units, (which + 1) * units)
            pack_scr[which, 0:units, :] = gd[mine, :].astype(BF)
            pack_scr[which, units : units + DP, :] = gu[:, mine].astype(BF)
            pack_scr[which, units + DP :, :] = jnp.zeros((PAD, DP), BF)
            pack_scr[which, units + DP : units + DP + 1, :] = gb[mine].T[:1].astype(BF)
            pack_scr[which, units + DP + 1 : units + DP + 2, :] = gb[2 * units :].T[:1].astype(BF)
            store[2 * which].start()
            store[2 * which + 1].start()

    own = pl.ds(pl.multiple_of(core * half, half), half)
    far = pl.ds(pl.multiple_of((1 - core) * half, half), half)
    m_part = h_scr
    column = b_down[...].astype(F32).T
    bias = jnp.where(core == 0, column[:half], column[half:])
    y_ref[...] = h_scr[own, :] + valid * bias
    m_part[...] = dot(down_scr[...], g_scr[...], 0, 0)
    y_ref[...] += valid * m_part[own, :]
    m_other_ref[...] = (valid * m_part[far, :]).astype(BF)
    dn_ref[...] = dot(up_scr[...], du_scr[...], 1, 0).astype(BF)

    @pl.when(step == last)
    def _():
        for copy in store:
            copy.wait()


def pack_rows(part, which):
    return pl.BlockSpec((part, DP), lambda i, *_: (2 * DP // part + which, 0), pipeline_mode=pl.Buffered(1))


def mlp(where, mixed, b_out, b_down, stream, cot, weights):
    half, rows = stream[0].shape
    part = mixed[0].shape[0]
    units = DP
    block = ROWS_BLK
    pack = (units + DP + PAD, DP)
    anywhere = pl.BlockSpec(memory_space=pl.ANY)
    return call(
        mlp_body,
        "out_project_mlp",
        40,
        (rows // block,),
        [rows_spec(part, block)] * 4
        + [pack_rows(part, which) for which in (0, 0, 1, 1)]
        + [whole_spec((1, DP))] * 2
        + [rows_spec(half, block)] * 4
        + [anywhere] * 2,
        [
            rows_spec(half, block),
            rows_spec(8, block),
            rows_spec(DP, block),
            rows_spec(half, block),
            rows_spec(DP, block),
        ]
        + [anywhere] * 4,
        [
            shape_of((half, rows), F32),
            shape_of((8, rows), F32),
            shape_of((DP, rows), BF),
            shape_of((half, rows), BF),
            shape_of((DP, rows), BF),
        ]
        + [shape_of((units, DP), BF), shape_of((DP + PAD, DP), BF)] * 2,
        [pltpu.VMEM((DP, DP), BF)]
        + [pltpu.VMEM((DP, block), BF)] * 3
        + [
            pltpu.VMEM((DP, block), F32),
            pltpu.VMEM((DP, 2 * units), BF),
            pltpu.VMEM((2 * units, DP), BF),
            pltpu.VMEM((PAD, 2 * units), BF),
            pltpu.VMEM((2, UNIT_BLK, block), F32),
            pltpu.VMEM((2, UNIT_BLK, block), F32),
            pltpu.VMEM((2 * units, block), BF),
            pltpu.VMEM((2 * units, block), BF),
            pltpu.VMEM((2 * units, DP), F32),
            pltpu.VMEM((DP, 2 * units), F32),
            pltpu.VMEM((2 * units + DP, 128), F32),
            pltpu.VMEM((2, *pack), BF),
            pltpu.SemaphoreType.DMA((2, 3)),
            pltpu.SemaphoreType.DMA((4,)),
        ],
        1,
    )(where, *mixed, *weights, *weights, b_out, b_down, *stream, *cot, *weights)


def out_back_body(
    where_ref, dn_mine, dn_other, normed_ref, stats_ref, c_mine, c_other, w0, w1, a0, a1,
    dh_ref, da_ref, pack_own, pack_other, c_scr, dh_scr, gw_scr, gb_scr,
):
    step = pl.program_id(0)
    core = where_ref[0]
    half, block = c_mine.shape
    position = step * block + lax.broadcasted_iota(jnp.int32, (1, block), 1)
    valid = (position < where_ref[1]).astype(F32)
    row_mask = lax.broadcasted_iota(jnp.int32, (DP, 1), 0) < DS
    grad_norm = dn_mine[...].astype(F32) + dn_other[...].astype(F32)
    normed = normed_ref[...].astype(F32)
    scale, total = stats_ref[0:1, :], stats_ref[1:2, :]
    inner = jnp.sum(grad_norm * normed, 0, keepdims=True) * (1.0 / DP)
    grad_out = join_halves(c_scr, c_mine, c_other, core).astype(F32)
    pulled = scale * (grad_norm - (normed + scale * total) * inner)
    grad_hidden = grad_out + jnp.where(row_mask, pulled, 0.0)
    dh_scr[...] = grad_hidden
    dh_ref[...] = dh_scr[pl.ds(pl.multiple_of(core * half, half), half), :].astype(BF)
    branch_f = jnp.where(row_mask, grad_hidden * valid, 0.0)
    branch = branch_f.astype(BF)
    part = a0.shape[0]
    da_ref[:part, :] = dot(w0[...], branch, 1, 0).astype(BF)
    da_ref[part:, :] = dot(w1[...], branch, 1, 0).astype(BF)

    @pl.when(step == 0)
    def _():
        gw_scr[...] = jnp.zeros_like(gw_scr)
        gb_scr[...] = jnp.zeros_like(gb_scr)

    gw_scr[:part] += dot(a0[...], branch, 1, 1)
    gw_scr[part:] += dot(a1[...], branch, 1, 1)
    gb_scr[...] += jnp.sum(branch_f, 1, keepdims=True)

    @pl.when(step == pl.num_programs(0) - 1)
    def _():
        for i, pack in enumerate((pack_own, pack_other)):
            pack[:part, :] = gw_scr[i * part : (i + 1) * part, :].astype(BF)
            pack[part:, :] = jnp.zeros((PAD, DP), BF)
            pack[part : part + 1, :] = gb_scr[...].T.astype(BF)


def out_back(where, dn, normed, stats, cot, weights, mixed):
    rows = normed.shape[1]
    half = cot[0].shape[0]
    part = mixed[0].shape[0]
    block = ROWS_BLK
    return call(
        out_back_body,
        "out_project_back",
        12,
        (rows // block,),
        [rows_spec(DP, block)] * 3
        + [rows_spec(8, block)]
        + [rows_spec(half, block)] * 2
        + [pack_rows(part, 0)] * 2
        + [rows_spec(part, block)] * 2,
        [
            rows_spec(half, block),
            rows_spec(2 * part, block),
            whole_spec((part + PAD, DP)),
            whole_spec((part + PAD, DP)),
        ],
        [
            shape_of((half, rows), BF),
            shape_of((2 * part, rows), BF),
            shape_of((part + PAD, DP), BF),
            shape_of((part + PAD, DP), BF),
        ],
        [
            pltpu.VMEM((DP, block), BF),
            pltpu.VMEM((DP, block), F32),
            pltpu.VMEM((2 * part, DP), F32),
            pltpu.VMEM((DP, 1), F32),
        ],
        1,
    )(where, *dn, normed, stats, *cot, *weights, *mixed)


def project_back_body(
    where_ref, g0, g1, g2, g3, g4, g5, normed_ref, w0, w1, dn_own_ref, dn_other_ref, inner_ref, p_scr, dn_scr, w_scr
):
    core = where_ref[0]
    outs = 3 * HS

    @pl.when(pl.program_id(0) == 0)
    def _():
        at = 0
        for ref in (w0, w1):
            for start in range(0, ref.shape[0], outs + PAD):
                w_scr[at : at + outs, :] = ref[start : start + outs, :]
                at += outs

    part = g0.shape[0]
    for i, ref in enumerate((g0, g1, g2, g3, g4, g5)):
        p_scr[i * part : (i + 1) * part, :] = ref[...]
    grad_norm = dot(w_scr[...], p_scr[...], 0, 0)
    dn_scr[...] = grad_norm
    half = DP // 2
    dn_own_ref[...] = dn_scr[pl.ds(pl.multiple_of(core * half, half), half), :].astype(BF)
    dn_other_ref[...] = dn_scr[pl.ds(pl.multiple_of((1 - core) * half, half), half), :].astype(BF)
    inner = jnp.sum(grad_norm * normed_ref[...].astype(F32), 0, keepdims=True)
    inner_ref[...] = jnp.broadcast_to(inner, inner_ref.shape)


def project_back(where, grads, normed, weights):
    part, rows = grads[0].shape
    half = DP // 2
    block = ROWS_BLK
    return call(
        project_back_body,
        "project_back",
        8,
        (rows // block,),
        [rows_spec(part, block)] * 6 + [rows_spec(DP, block)] + [whole_spec(w.shape) for w in weights],
        [rows_spec(half, block), rows_spec(half, block), rows_spec(8, block)],
        [shape_of((half, rows), BF), shape_of((half, rows), BF), shape_of((8, rows), F32)],
        [pltpu.VMEM((6 * part, block), BF), pltpu.VMEM((DP, block), F32), pltpu.VMEM((6 * part, DP), BF)],
        1,
    )(where, *grads, normed, *weights)


def swap(value, axis):
    return lax.ppermute(value, axis, [(0, 1), (1, 0)])


def cross(value):
    return lax.ppermute(value, ("core", "x"), [(1, 2), (2, 1)])


def after(value, *others):
    return lax.optimization_barrier((value, *others))[0]


def quarter(value, core, axis):
    size = value.shape[axis] // 2
    return lax.dynamic_slice_in_dim(value, core * size, size, axis)


def both(mine, other, core, axis):
    first = jnp.where(core == 0, mine, other)
    second = jnp.where(core == 0, other, mine)
    return jnp.concatenate([first, second], axis)


def pad_last(value):
    return jnp.pad(value, [(0, 0)] * (value.ndim - 1) + [(0, DP - value.shape[-1])])


def pad_rows(value, count):
    return jnp.pad(value, ((0, count - value.shape[0]), (0, 0)))


def sum_steps(value, index, count):
    levels = count.bit_length() - 1
    for level in range(levels):
        halves = value.reshape(2, -1, value.shape[-1])
        low = (index >> level) & 1 == 0
        keep = jnp.where(low, halves[0], halves[1])
        value = keep + (yield level, jnp.where(low, halves[1], halves[0]))
    for level in reversed(range(levels)):
        low = (index >> level) & 1 == 0
        got = yield level, value
        value = jnp.concatenate([jnp.where(low, value, got), jnp.where(low, got, value)])
    yield None, value


class ChipSum:
    def __init__(self, value, index, count):
        self.count = count
        self.steps = sum_steps(value, index, count)
        self.level, self.value = next(self.steps)
        self.got = None

    def send(self):
        if self.level is not None:
            pairs = [(i, i ^ (1 << self.level)) for i in range(self.count)]
            self.got = lax.ppermute(self.value, "zy", pairs)

    def take(self, *others):
        if self.level is not None:
            got = after(self.got, *others) if others else self.got
            self.level, self.value = self.steps.send(got)
            self.got = None
        return self.value

    def finish(self, *others):
        while self.level is not None:
            if self.got is None:
                self.send()
            self.take(*others)
        return self.value


def on_device(chips, stream, lengths, w_qkv, b_qkv, w_out, b_out, w_up, b_up, w_down, b_down, cotangent):
    core = lax.axis_index("core")
    chip = lax.axis_index("x")
    place = lax.axis_index("zy")
    stays = core == chip
    half, rows = stream.shape

    def home(value):
        return jnp.where(stays, value, cross(value))

    side = core[None].astype(jnp.int32)

    part = w_out.shape[0] // 2
    units = DP
    own_mlp = jnp.concatenate(
        [
            jnp.pad(quarter(w_up, core, 1), ((0, DP - DS), (0, 0))),
            pad_last(quarter(w_down, core, 0)),
            pad_last(quarter(w_out, core, 0)),
            pad_last(quarter(w_out, 1 - core, 0)),
            pad_rows(quarter(b_up, core, 0)[None], 128),
        ]
    )
    share = own_mlp.shape[0] // chips
    piece = lax.dynamic_slice_in_dim(own_mlp, place * share, share, 0)
    got_piece = swap(piece, "x")
    x_mine = home(stream)
    other_mlp = lax.all_gather(got_piece, "zy", axis=0, tiled=True)

    outs = 3 * HS
    heads = b_qkv.shape[1] // (2 * HS)
    head_w = pad_last(quarter(w_qkv, core, 1)).reshape(3, heads, HS, DP).swapaxes(0, 1).reshape(heads, outs, DP)
    head_b = quarter(b_qkv, core, 1).reshape(3, heads, HS).swapaxes(0, 1).reshape(heads, 1, outs)
    head_b = jnp.pad(head_b, ((0, 0), (0, PAD - 1), (0, DP - outs)))
    own_qkv = jnp.concatenate([head_w, head_b], 1).reshape(-1, DP)
    x_mine, own_qkv = lax.optimization_barrier((x_mine, own_qkv, got_piece))[:2]
    x_other = swap(x_mine, "core")
    other_qkv = swap(own_qkv, "x")

    normed_one, stats_one, qkv_own, mixed_own, logs_own = norm_attend(side, x_mine, x_other, own_qkv)
    mixed_own_far = swap(mixed_own, "core")
    length = after(lengths, mixed_own)
    length = jnp.where(stays, length, swap(length.astype(F32), "core").astype(jnp.int32))
    where = jnp.concatenate([side, length])
    c_mine = home(after(cotangent, mixed_own))
    qkv_other, mixed_other, logs_other = more_attend(normed_one, other_qkv)
    mixed_other_far = swap(mixed_other, "core")
    c_mine = after(c_mine, mixed_other)
    c_other = swap(c_mine, "core")

    y_own, stats_two, normed_two, m_other, dn_two, gd_own, gu_own, gd_other, gu_other = mlp(
        where,
        (mixed_own, mixed_other, mixed_own_far, mixed_other_far),
        jnp.pad(b_out, (0, 1))[None],
        jnp.pad(b_down, (0, 1))[None],
        (x_mine, x_other),
        (c_mine, c_other),
        (own_mlp, other_mlp),
    )
    dn_two_far = swap(dn_two, "core")
    got_down = swap(gd_other, "x")
    got_up = swap(gu_other, "x")
    m_far = swap(m_other, "core")
    dh_own, grad_mixed, out_own, out_other = out_back(
        where,
        (dn_two, dn_two_far),
        normed_two,
        stats_two,
        (c_mine, c_other),
        (own_mlp, other_mlp),
        (mixed_own, mixed_other),
    )

    got_out = swap(out_other, "x")
    back = {}
    sets = {0: (qkv_own, mixed_own, logs_own), 1: (qkv_other, mixed_other, logs_other)}

    def run_head(which, head, *first):
        qkv, mixed, logs = sets[which]
        done = attend_back(after(qkv, *first), grad_mixed, mixed, logs, normed_one, head, which * heads + head)
        back[which, head] = done
        return done[0]

    total_down = gd_own + after(got_down, grad_mixed)
    last = run_head(1, 0, grad_mixed, total_down)
    sum_down = lax.psum(total_down, "zy")
    last = run_head(1, 1, last)
    result = (y_own + after(m_far, last).astype(F32)).astype(BF)
    last = run_head(1, 2, last, result)
    total_rest = jnp.concatenate([gu_own + after(got_up, last), out_own + after(got_out, last)])
    rest = ChipSum(pad_rows(total_rest, 1024), place, chips)
    output = home(after(result, total_rest))

    def qkv_pack(which):
        return pad_rows(jnp.concatenate([back[which, head][1] for head in range(heads)]), 640)

    got_qkv = swap(qkv_pack(1), "x")
    rest.send()
    for head in range(heads):
        last = run_head(0, head, last, rest.value)
        if head:
            rest.take(last)
            rest.send()
    qkv = ChipSum(qkv_pack(0) + after(got_qkv, last), place, chips)
    qkv.send()
    normed_late = after(normed_one, qkv.value, rest.value, output, last)
    dn_own, dn_other, inner = project_back(
        where,
        [back[which, head][0] for which in (0, 1) for head in range(heads)],
        normed_late,
        (own_qkv, other_qkv),
    )
    rest.take(dn_own)
    rest.send()
    qkv.take(dn_own)
    qkv.send()
    dn_far = swap(after(dn_other, rest.value, qkv.value, sum_down), "core")
    inner = inner[0:1] + swap(inner, "core")[0:1]
    row_mask = core * half + lax.broadcasted_iota(jnp.int32, (half, 1), 0) < DS
    scale_one, total_one = stats_one[0:1], stats_one[1:2]
    grad_in = dh_own.astype(F32) + jnp.where(
        row_mask,
        scale_one * (dn_own.astype(F32) + dn_far.astype(F32))
        - scale_one * scale_one * (x_mine.astype(F32) + total_one) * inner / DP,
        0.0,
    )
    grad_sent = grad_in.astype(BF)
    grad_got = cross(grad_sent)
    grad_stream = jnp.where(stays, grad_sent, grad_got).astype(F32)
    def gather(mine, far, pick, axis):
        return both(pick(mine), pick(far), core, axis).astype(F32)

    def by_head(value):
        return value[: heads * (outs + PAD)].reshape(heads, outs + PAD, DP)

    def pick_w(value):
        return by_head(value)[:, :outs, :DS].reshape(heads, 3, HS, DS).swapaxes(0, 1).reshape(3, -1, DS)

    def pick_b(value):
        return by_head(value)[:, outs, :outs].reshape(heads, 3, HS).swapaxes(0, 1).reshape(3, -1)

    qkv.take(grad_sent)
    qkv.send()
    rest.take(qkv.value)
    rest.send()
    far_down = swap(after(sum_down, qkv.value), "core")
    qkv.take()
    qkv.send()
    rest.take(qkv.value)
    rest.send()
    grad_w_down = gather(sum_down, far_down, lambda v: v[:, :DS], 0)
    qkv.take(grad_w_down)
    qkv.send()
    qkv.take()
    qkv.send()
    sum_rest = rest.finish(qkv.value)
    far_rest = swap(sum_rest, "core")
    edge = DP + PAD
    grad_w_up = gather(sum_rest, far_rest, lambda v: v[:DS], 1)
    grad_w_out = gather(sum_rest, far_rest, lambda v: v[edge : edge + part, :DS], 0)
    sum_qkv = qkv.finish(grad_w_up, grad_w_out, grad_stream)
    far_qkv = swap(sum_qkv, "core")

    return (
        output,
        grad_stream,
        gather(sum_qkv, far_qkv, pick_w, 1),
        gather(sum_qkv, far_qkv, pick_b, 1),
        grad_w_out,
        sum_rest[edge + part, :DS].astype(F32),
        grad_w_up,
        gather(sum_rest, far_rest, lambda v: v[DP], 0),
        grad_w_down,
        sum_rest[DP + 1, :DS].astype(F32),
    )


def solution(mesh):
    dp, mp = mesh.shape["dp"], mesh.shape["mp"]
    fine = Mesh(mesh.devices.reshape(dp // 2, 2, mp), ("zy", "core", "x"))
    seqs = ("zy", "core")
    placed = (
        P("x", seqs),
        P(seqs),
        P(None, "x", None),
        P(None, "x"),
        P("x", None),
        P(),
        P(None, "x"),
        P("x"),
        P("x", None),
        P(),
        P("x", seqs),
    )
    return jax.shard_map(
        functools.partial(on_device, dp // 2),
        mesh=fine,
        in_specs=placed,
        out_specs=(
            P("x", seqs),
            P("x", seqs),
            P(None, "x", None),
            P(None, "x"),
            P("x", None),
            P(),
            P(None, "x"),
            P("x"),
            P("x", None),
            P(),
        ),
        check_vma=False,
    )
```

```python
import functools

import jax
import jax.numpy as jnp
from jax import lax
from jax.experimental import pallas as pl
from jax.experimental.pallas import tpu as pltpu
from jax.sharding import Mesh
from jax.sharding import PartitionSpec as P

HS = 64
DS = 767
DP = 768
BLK = 256
EPSILON = 1e-05
NEGATIVE = -1e30
F32 = jnp.float32
BF = jnp.bfloat16
VMEM_MIB = {
    "norm_attend": 28,
    "attend": 26,
    "out_project_mlp": 54,
    "out_project_back": 56,
    "attend_back": 30,
    "project_back": 22,
}
ROWS_BLK = 512
UNIT_BLK = 256
PAD = 16
BACK_MICROS = (8, 3, 3, 4, 4, 4)


def dot(left, right, left_dim, right_dim):
    return lax.dot_general(
        left, right, (((left_dim,), (right_dim,)), ((), ())), preferred_element_type=F32
    )


def call(body, name, micros, grid, in_specs, out_specs, out_shape, scratch, prefetch=0):
    return pl.pallas_call(
        body,
        grid_spec=pltpu.PrefetchScalarGridSpec(
            num_scalar_prefetch=prefetch,
            grid=grid,
            in_specs=in_specs,
            out_specs=out_specs,
            scratch_shapes=scratch,
        ),
        out_shape=out_shape,
        compiler_params=pltpu.CompilerParams(vmem_limit_bytes=VMEM_MIB[name] * 1024 * 1024),
        cost_estimate=pl.CostEstimate(flops=int(micros * 1e9), bytes_accessed=0, transcendentals=0),
        name=name,
    )


def rows_spec(height, block):
    return pl.BlockSpec((height, block), lambda i, *_: (0, i))


def whole_spec(shape):
    return pl.BlockSpec(shape, lambda i, *_: (0,) * len(shape), pipeline_mode=pl.Buffered(1))


def shape_of(shape, dtype):
    return jax.ShapeDtypeStruct(shape, dtype)


def join_halves(scratch, mine_ref, other_ref, core):
    half = mine_ref.shape[0]
    scratch[pl.ds(pl.multiple_of(core * half, half), half), :] = mine_ref[...]
    scratch[pl.ds(pl.multiple_of((1 - core) * half, half), half), :] = other_ref[...]
    return scratch[...]


def crms_stats(values):
    kept = jnp.where(lax.broadcasted_iota(jnp.int32, values.shape, 0) < DS, values, 0.0)
    total = jnp.sum(kept, 0, keepdims=True)
    squares = jnp.sum(kept * kept, 0, keepdims=True)
    scale = lax.rsqrt((squares + total * total) / DP + EPSILON)
    return kept, scale, total


def causal_tile():
    key_pos = lax.broadcasted_iota(jnp.int32, (BLK, BLK), 0)
    query_pos = lax.broadcasted_iota(jnp.int32, (BLK, BLK), 1)
    return key_pos <= query_pos


def attend_head(w_ref, normed_ref, qkv_ref, a_ref, log_ref, s_scr, p_scr):
    rows = normed_ref.shape[1]
    blocks = rows // BLK
    outs = 3 * HS
    bias = w_ref[outs : outs + 1, :outs].astype(F32).T
    qkv_ref[...] = (dot(w_ref[:outs, :], normed_ref[...], 1, 0) + bias).astype(BF)
    key_rows = qkv_ref[HS : 2 * HS, :].T
    queries = qkv_ref[:HS, :] * jnp.asarray(0.125, BF)
    allowed = causal_tile()

    def score(blk):
        at = slice(blk * BLK, (blk + 1) * BLK)
        count = (blk + 1) * BLK
        scores = dot(key_rows[:count], queries[:, at], 1, 0)
        if blk:
            s_scr[blk % 2, : count - BLK] = scores[: count - BLK]
        s_scr[blk % 2, count - BLK : count] = jnp.where(allowed, scores[count - BLK :], NEGATIVE)

    def soften(blk):
        count = (blk + 1) * BLK
        top = jnp.max(s_scr[blk % 2, :count], axis=0, keepdims=True)
        expo = jnp.exp(s_scr[blk % 2, :count] - top)
        total = jnp.sum(expo, axis=0, keepdims=True)
        p_scr[blk % 2, :count] = expo.astype(BF)
        log_ref[0, :, blk * BLK : count] = top + jnp.log(total)
        return total

    def mix(blk, total):
        count = (blk + 1) * BLK
        mixed = dot(qkv_ref[2 * HS :, :count], p_scr[blk % 2, :count], 1, 0)
        a_ref[:, blk * BLK : count] = (mixed * (1.0 / total)).astype(BF)

    score(0)
    totals = {}
    for blk in range(blocks):
        if blk + 1 < blocks:
            score(blk + 1)
        if blk:
            mix(blk - 1, totals[blk - 1])
        totals[blk] = soften(blk)
    mix(blocks - 1, totals[blocks - 1])


def norm_attend_body(
    where_ref, mine_ref, other_ref, w_ref, normed_ref, stats_ref, qkv_ref, a_ref, log_ref, s_scr, p_scr
):
    @pl.when(pl.program_id(0) == 0)
    def _():
        half = mine_ref.shape[0]
        core = where_ref[0]
        first = pl.ds(pl.multiple_of(core * half, half), half)
        second = pl.ds(pl.multiple_of((1 - core) * half, half), half)
        normed_ref[first, :] = mine_ref[...]
        normed_ref[second, :] = other_ref[...]
        for start in range(0, normed_ref.shape[1], BLK):
            at = slice(start, start + BLK)
            kept, scale, total = crms_stats(normed_ref[:, at].astype(F32))
            normed_ref[:, at] = (kept * scale).astype(BF)
            stats_ref[0:1, at] = scale
            stats_ref[1:2, at] = total

    attend_head(w_ref, normed_ref, qkv_ref, a_ref, log_ref, s_scr, p_scr)


def attend_specs(heads, rows):
    outs = 3 * HS
    ins = [pl.BlockSpec((outs + PAD, DP), lambda h, *_: (h, 0))]
    results = [
        pl.BlockSpec((outs, rows), lambda h, *_: (h, 0)),
        pl.BlockSpec((HS, rows), lambda h, *_: (h, 0)),
        pl.BlockSpec((1, 1, rows), lambda h, *_: (h, 0, 0)),
    ]
    shapes = [
        shape_of((heads * outs, rows), BF),
        shape_of((heads * HS, rows), BF),
        shape_of((heads, 1, rows), F32),
    ]
    scratch = [pltpu.VMEM((2, rows, BLK), F32), pltpu.VMEM((2, rows, BLK), BF)]
    return ins, results, shapes, scratch


def norm_attend(where, mine, other, weights):
    half, rows = mine.shape
    heads = weights.shape[0] // (3 * HS + PAD)
    ins, results, shapes, scratch = attend_specs(heads, rows)
    return call(
        norm_attend_body,
        "norm_attend",
        22,
        (heads,),
        [whole_spec((half, rows)), whole_spec((half, rows))] + ins,
        [whole_spec((DP, rows)), whole_spec((8, rows))] + results,
        [shape_of((DP, rows), BF), shape_of((8, rows), F32)] + shapes,
        scratch,
        1,
    )(where, mine, other, weights)


def more_attend_body(normed_ref, w_ref, qkv_ref, a_ref, log_ref, s_scr, p_scr):
    attend_head(w_ref, normed_ref, qkv_ref, a_ref, log_ref, s_scr, p_scr)


def more_attend(normed, weights):
    rows = normed.shape[1]
    heads = weights.shape[0] // (3 * HS + PAD)
    ins, results, shapes, scratch = attend_specs(heads, rows)
    return call(
        more_attend_body,
        "attend",
        20,
        (heads,),
        [whole_spec((DP, rows))] + ins,
        results,
        shapes,
        scratch,
    )(normed, weights)


def attend_back_body(
    qkv_ref, da_ref, a_ref, log_ref, normed_hbm, grad_ref, gw_ref,
    p_scr, ds_scr, s_scr, dp_scr, dq_scr, normed_scr, sem,
):
    fetch = pltpu.make_async_copy(normed_hbm, normed_scr, sem)
    fetch.start()
    rows = qkv_ref.shape[1]
    blocks = rows // BLK
    queries = qkv_ref[:HS, :] * jnp.asarray(0.125, BF)
    query_rows = queries.T
    key_rows = qkv_ref[HS : 2 * HS, :].T
    value_rows = qkv_ref[2 * HS :, :].T
    grad = da_ref[...]
    grad_rows = grad.T
    row_dot = jnp.sum(grad.astype(F32) * a_ref[...].astype(F32), axis=0, keepdims=True)
    logs = log_ref[0]
    allowed = causal_tile()

    def span(blk):
        return slice(blk * BLK, (blk + 1) * BLK)

    def score(blk):
        start = blk * BLK
        s_scr[blk % 2, :, start:] = dot(key_rows[span(blk)], queries[:, start:], 1, 0)
        dp_scr[blk % 2, :, start:] = dot(value_rows[span(blk)], grad[:, start:], 1, 0)

    def soften(blk):
        slot = blk % 2
        for query_blk in range(blk, blocks):
            at = span(query_blk)
            probs = jnp.exp(s_scr[slot, :, at] - logs[:, at])
            if query_blk == blk:
                probs = jnp.where(allowed, probs, 0.0)
            p_scr[slot, :, at] = probs.astype(BF)
            ds_scr[slot, :, at] = (probs * (dp_scr[slot, :, at] - row_dot[:, at])).astype(BF)

    def mix(blk):
        slot, start = blk % 2, blk * BLK
        grad_keys = dot(ds_scr[slot, :, start:], query_rows[start:], 1, 0)
        grad_values = dot(p_scr[slot, :, start:], grad_rows[start:], 1, 0)
        grad_queries = dot(qkv_ref[HS : 2 * HS, span(blk)], ds_scr[slot, :, start:], 1, 0)
        if blk:
            dq_scr[:, start:] += grad_queries
        else:
            dq_scr[...] = grad_queries
        grad_ref[HS : 2 * HS, span(blk)] = grad_keys.T.astype(BF)
        grad_ref[2 * HS :, span(blk)] = grad_values.T.astype(BF)

    score(0)
    for blk in range(blocks):
        if blk + 1 < blocks:
            score(blk + 1)
        if blk:
            mix(blk - 1)
        soften(blk)
    mix(blocks - 1)
    grad_ref[:HS, :] = (dq_scr[...] * 0.125).astype(BF)
    fetch.wait()
    outs = 3 * HS
    gw_ref[:outs, :] = dot(grad_ref[...], normed_scr[...], 1, 1).astype(BF)
    gw_ref[outs:, :] = jnp.zeros((PAD, DP), BF)
    gw_ref[outs : outs + 1, :outs] = jnp.sum(grad_ref[...].astype(F32), 1, keepdims=True).T.astype(BF)


def attend_back(qkv, grad, mixed, logs, normed, head, grad_head):
    rows = qkv.shape[1]
    outs = 3 * HS
    return call(
        attend_back_body,
        "attend_back",
        BACK_MICROS[grad_head],
        (1,),
        [
            pl.BlockSpec((outs, rows), lambda i: (head, 0)),
            pl.BlockSpec((HS, rows), lambda i: (grad_head, 0)),
            pl.BlockSpec((HS, rows), lambda i: (head, 0)),
            pl.BlockSpec((1, 1, rows), lambda i: (head, 0, 0)),
            pl.BlockSpec(memory_space=pl.ANY),
        ],
        [
            pl.BlockSpec((outs, rows), lambda i: (0, 0)),
            pl.BlockSpec((outs + PAD, DP), lambda i: (0, 0)),
        ],
        [shape_of((outs, rows), BF), shape_of((outs + PAD, DP), BF)],
        [
            pltpu.VMEM((2, BLK, rows), BF),
            pltpu.VMEM((2, BLK, rows), BF),
            pltpu.VMEM((2, BLK, rows), F32),
            pltpu.VMEM((2, BLK, rows), F32),
            pltpu.VMEM((HS, rows), F32),
            pltpu.VMEM((DP, rows), BF),
            pltpu.SemaphoreType.DMA(()),
        ],
    )(qkv, grad, mixed, logs, normed)


GELU_A = 0.7978845608028654
GELU_B = 0.044715


def gelu_pair(pre):
    square = pre * pre
    bent = jnp.tanh(GELU_A * pre * (1.0 + GELU_B * square))
    half_up = 0.5 * (1.0 + bent)
    slope = half_up + 0.5 * pre * (1.0 - bent * bent) * (GELU_A * (1.0 + 3.0 * GELU_B * square))
    return pre * half_up, slope


def mlp_body(
    where_ref, a0, a1, a2, a3, wout0, wout1, wout2, wout3, b_out, b_down, x_mine, x_other, c_mine, c_other, w_own, w_other,
    y_ref, stats_ref, normed_ref, m_other_ref, dn_ref, gd_own, gu_own, gd_other, gu_other,
    wout, a_scr, x_scr, c_scr, h_scr, up_scr, down_scr, bias_scr, pre_scr, back_scr, g_scr, du_scr, gd, gu, gb, pack_scr, w_sem, pack_sem,
):
    step = pl.program_id(0)
    last = pl.num_programs(0) - 1
    core = where_ref[0]
    half, block = x_mine.shape
    units = DP
    fetch = []
    for i, ref in enumerate((w_own, w_other)):
        at = pl.ds(i * units, units)
        for j, (source, target) in enumerate(
            (
                (ref.at[pl.ds(0, DP), :], up_scr.at[:, at]),
                (ref.at[pl.ds(DP, units), :], down_scr.at[at, :]),
                (ref.at[pl.ds(DP + units + 2 * a0.shape[0], PAD), :], bias_scr.at[:, at]),
            )
        ):
            fetch.append(pltpu.make_async_copy(source, target, w_sem.at[i, j]))
    split = ((gd_own, pl.ds(0, units)), (gu_own, pl.ds(units, DP + PAD)))
    split += ((gd_other, pl.ds(0, units)), (gu_other, pl.ds(units, DP + PAD)))
    store = [
        pltpu.make_async_copy(pack_scr.at[i // 2, at, :], ref, pack_sem.at[i]) for i, (ref, at) in enumerate(split)
    ]

    @pl.when(step == 0)
    def _():
        for copy in fetch:
            copy.start()
        start = 0
        for ref in (wout0, wout1, wout2, wout3):
            wout[start : start + ref.shape[0], :] = ref[...]
            start += ref.shape[0]
        for ref in (gd, gu, gb):
            ref[...] = jnp.zeros_like(ref)

    for i, a_ref in enumerate((a0, a1, a2, a3)):
        part = a_ref.shape[0]
        a_scr[i * part : (i + 1) * part, :] = a_ref[...]
    position = step * block + lax.broadcasted_iota(jnp.int32, (1, block), 1)
    valid = (position < where_ref[1]).astype(F32)
    stream = join_halves(x_scr, x_mine, x_other, core).astype(F32)
    branch = dot(wout[...], a_scr[...], 0, 0) + b_out[...].astype(F32).T
    hidden = stream + valid * branch
    h_scr[...] = hidden
    kept, scale, total = crms_stats(hidden)
    stats_ref[0:1, :] = scale
    stats_ref[1:2, :] = total
    normed = (kept * scale).astype(BF)
    normed_ref[...] = normed
    grad_out = join_halves(c_scr, c_mine, c_other, core)
    keep_row = lax.broadcasted_iota(jnp.int32, (DP, block), 0) < DS
    dm = jnp.where(keep_row, grad_out.astype(F32) * valid, 0.0).astype(BF)

    @pl.when(step == 0)
    def _():
        for copy in fetch:
            copy.wait()

    ones = jnp.ones((block, 128), BF)
    gb[2 * units :] += dot(dm, ones, 1, 0)
    starts = [which * units + start for which in (1, 0) for start in range(0, units, UNIT_BLK)]

    def expand(i):
        at = slice(starts[i], starts[i] + UNIT_BLK)
        pre_scr[i % 2] = dot(up_scr[:, at], normed, 0, 0)
        back_scr[i % 2] = dot(down_scr[at, :], dm, 1, 0)

    def bend(i):
        at = slice(starts[i], starts[i] + UNIT_BLK)
        act, slope = gelu_pair(pre_scr[i % 2] + bias_scr[0:1, at].astype(F32).T)
        g_scr[at, :] = act.astype(BF)
        du_scr[at, :] = (back_scr[i % 2] * slope).astype(BF)

    def collect(i):
        at = slice(starts[i], starts[i] + UNIT_BLK)
        gd[at, :] += dot(g_scr[at, :], dm, 1, 1)
        gu[:, at] += dot(normed, du_scr[at, :], 1, 1)
        gb[at] += dot(du_scr[at, :], ones, 1, 0)

    expand(0)
    for i in range(len(starts)):
        if i + 1 < len(starts):
            expand(i + 1)
        if i:
            collect(i - 1)
        bend(i)
    collect(len(starts) - 1)

    @pl.when(step == last)
    def _():
        for which in (1, 0):
            mine = slice(which * units, (which + 1) * units)
            pack_scr[which, 0:units, :] = gd[mine, :].astype(BF)
            pack_scr[which, units : units + DP, :] = gu[:, mine].astype(BF)
            pack_scr[which, units + DP :, :] = jnp.zeros((PAD, DP), BF)
            pack_scr[which, units + DP : units + DP + 1, :] = gb[mine].T[:1].astype(BF)
            pack_scr[which, units + DP + 1 : units + DP + 2, :] = gb[2 * units :].T[:1].astype(BF)
            store[2 * which].start()
            store[2 * which + 1].start()

    own = pl.ds(pl.multiple_of(core * half, half), half)
    far = pl.ds(pl.multiple_of((1 - core) * half, half), half)
    m_part = h_scr
    column = b_down[...].astype(F32).T
    bias = jnp.where(core == 0, column[:half], column[half:])
    y_ref[...] = h_scr[own, :] + valid * bias
    m_part[...] = dot(down_scr[...], g_scr[...], 0, 0)
    y_ref[...] += valid * m_part[own, :]
    m_other_ref[...] = (valid * m_part[far, :]).astype(BF)
    dn_ref[...] = dot(up_scr[...], du_scr[...], 1, 0).astype(BF)

    @pl.when(step == last)
    def _():
        for copy in store:
            copy.wait()


def pack_rows(part, which):
    return pl.BlockSpec((part, DP), lambda i, *_: (2 * DP // part + which, 0), pipeline_mode=pl.Buffered(1))


def mlp(where, mixed, b_out, b_down, stream, cot, weights):
    half, rows = stream[0].shape
    part = mixed[0].shape[0]
    units = DP
    block = ROWS_BLK
    pack = (units + DP + PAD, DP)
    anywhere = pl.BlockSpec(memory_space=pl.ANY)
    return call(
        mlp_body,
        "out_project_mlp",
        40,
        (rows // block,),
        [rows_spec(part, block)] * 4
        + [pack_rows(part, which) for which in (0, 0, 1, 1)]
        + [whole_spec((1, DP))] * 2
        + [rows_spec(half, block)] * 4
        + [anywhere] * 2,
        [
            rows_spec(half, block),
            rows_spec(8, block),
            rows_spec(DP, block),
            rows_spec(half, block),
            rows_spec(DP, block),
        ]
        + [anywhere] * 4,
        [
            shape_of((half, rows), F32),
            shape_of((8, rows), F32),
            shape_of((DP, rows), BF),
            shape_of((half, rows), BF),
            shape_of((DP, rows), BF),
        ]
        + [shape_of((units, DP), BF), shape_of((DP + PAD, DP), BF)] * 2,
        [pltpu.VMEM((DP, DP), BF)]
        + [pltpu.VMEM((DP, block), BF)] * 3
        + [
            pltpu.VMEM((DP, block), F32),
            pltpu.VMEM((DP, 2 * units), BF),
            pltpu.VMEM((2 * units, DP), BF),
            pltpu.VMEM((PAD, 2 * units), BF),
            pltpu.VMEM((2, UNIT_BLK, block), F32),
            pltpu.VMEM((2, UNIT_BLK, block), F32),
            pltpu.VMEM((2 * units, block), BF),
            pltpu.VMEM((2 * units, block), BF),
            pltpu.VMEM((2 * units, DP), F32),
            pltpu.VMEM((DP, 2 * units), F32),
            pltpu.VMEM((2 * units + DP, 128), F32),
            pltpu.VMEM((2, *pack), BF),
            pltpu.SemaphoreType.DMA((2, 3)),
            pltpu.SemaphoreType.DMA((4,)),
        ],
        1,
    )(where, *mixed, *weights, *weights, b_out, b_down, *stream, *cot, *weights)


def out_back_body(
    where_ref, dn_mine, dn_other, normed_ref, stats_ref, c_mine, c_other, w0, w1, a0, a1,
    dh_ref, da_ref, pack_own, pack_other, c_scr, dh_scr, gw_scr, gb_scr,
):
    step = pl.program_id(0)
    core = where_ref[0]
    half, block = c_mine.shape
    position = step * block + lax.broadcasted_iota(jnp.int32, (1, block), 1)
    valid = (position < where_ref[1]).astype(F32)
    row_mask = lax.broadcasted_iota(jnp.int32, (DP, 1), 0) < DS
    grad_norm = dn_mine[...].astype(F32) + dn_other[...].astype(F32)
    normed = normed_ref[...].astype(F32)
    scale, total = stats_ref[0:1, :], stats_ref[1:2, :]
    inner = jnp.sum(grad_norm * normed, 0, keepdims=True) * (1.0 / DP)
    grad_out = join_halves(c_scr, c_mine, c_other, core).astype(F32)
    pulled = scale * (grad_norm - (normed + scale * total) * inner)
    grad_hidden = grad_out + jnp.where(row_mask, pulled, 0.0)
    dh_scr[...] = grad_hidden
    dh_ref[...] = dh_scr[pl.ds(pl.multiple_of(core * half, half), half), :].astype(BF)
    branch_f = jnp.where(row_mask, grad_hidden * valid, 0.0)
    branch = branch_f.astype(BF)
    part = a0.shape[0]
    da_ref[:part, :] = dot(w0[...], branch, 1, 0).astype(BF)
    da_ref[part:, :] = dot(w1[...], branch, 1, 0).astype(BF)

    @pl.when(step == 0)
    def _():
        gw_scr[...] = jnp.zeros_like(gw_scr)
        gb_scr[...] = jnp.zeros_like(gb_scr)

    gw_scr[:part] += dot(a0[...], branch, 1, 1)
    gw_scr[part:] += dot(a1[...], branch, 1, 1)
    gb_scr[...] += jnp.sum(branch_f, 1, keepdims=True)

    @pl.when(step == pl.num_programs(0) - 1)
    def _():
        for i, pack in enumerate((pack_own, pack_other)):
            pack[:part, :] = gw_scr[i * part : (i + 1) * part, :].astype(BF)
            pack[part:, :] = jnp.zeros((PAD, DP), BF)
            pack[part : part + 1, :] = gb_scr[...].T.astype(BF)


def out_back(where, dn, normed, stats, cot, weights, mixed):
    rows = normed.shape[1]
    half = cot[0].shape[0]
    part = mixed[0].shape[0]
    block = ROWS_BLK
    return call(
        out_back_body,
        "out_project_back",
        12,
        (rows // block,),
        [rows_spec(DP, block)] * 3
        + [rows_spec(8, block)]
        + [rows_spec(half, block)] * 2
        + [pack_rows(part, 0)] * 2
        + [rows_spec(part, block)] * 2,
        [
            rows_spec(half, block),
            rows_spec(2 * part, block),
            whole_spec((part + PAD, DP)),
            whole_spec((part + PAD, DP)),
        ],
        [
            shape_of((half, rows), BF),
            shape_of((2 * part, rows), BF),
            shape_of((part + PAD, DP), BF),
            shape_of((part + PAD, DP), BF),
        ],
        [
            pltpu.VMEM((DP, block), BF),
            pltpu.VMEM((DP, block), F32),
            pltpu.VMEM((2 * part, DP), F32),
            pltpu.VMEM((DP, 1), F32),
        ],
        1,
    )(where, *dn, normed, stats, *cot, *weights, *mixed)


def project_back_body(
    where_ref, g0, g1, g2, g3, g4, g5, normed_ref, w0, w1, dn_own_ref, dn_other_ref, inner_ref, p_scr, dn_scr, w_scr
):
    core = where_ref[0]
    outs = 3 * HS

    @pl.when(pl.program_id(0) == 0)
    def _():
        at = 0
        for ref in (w0, w1):
            for start in range(0, ref.shape[0], outs + PAD):
                w_scr[at : at + outs, :] = ref[start : start + outs, :]
                at += outs

    part = g0.shape[0]
    for i, ref in enumerate((g0, g1, g2, g3, g4, g5)):
        p_scr[i * part : (i + 1) * part, :] = ref[...]
    grad_norm = dot(w_scr[...], p_scr[...], 0, 0)
    dn_scr[...] = grad_norm
    half = DP // 2
    dn_own_ref[...] = dn_scr[pl.ds(pl.multiple_of(core * half, half), half), :].astype(BF)
    dn_other_ref[...] = dn_scr[pl.ds(pl.multiple_of((1 - core) * half, half), half), :].astype(BF)
    inner = jnp.sum(grad_norm * normed_ref[...].astype(F32), 0, keepdims=True)
    inner_ref[...] = jnp.broadcast_to(inner, inner_ref.shape)


def project_back(where, grads, normed, weights):
    part, rows = grads[0].shape
    half = DP // 2
    block = ROWS_BLK
    return call(
        project_back_body,
        "project_back",
        8,
        (rows // block,),
        [rows_spec(part, block)] * 6 + [rows_spec(DP, block)] + [whole_spec(w.shape) for w in weights],
        [rows_spec(half, block), rows_spec(half, block), rows_spec(8, block)],
        [shape_of((half, rows), BF), shape_of((half, rows), BF), shape_of((8, rows), F32)],
        [pltpu.VMEM((6 * part, block), BF), pltpu.VMEM((DP, block), F32), pltpu.VMEM((6 * part, DP), BF)],
        1,
    )(where, *grads, normed, *weights)


def swap(value, axis):
    return lax.ppermute(value, axis, [(0, 1), (1, 0)])


def cross(value):
    return lax.ppermute(value, ("core", "x"), [(1, 2), (2, 1)])


def after(value, *others):
    return lax.optimization_barrier((value, *others))[0]


def quarter(value, core, axis):
    size = value.shape[axis] // 2
    return lax.dynamic_slice_in_dim(value, core * size, size, axis)


def both(mine, other, core, axis):
    first = jnp.where(core == 0, mine, other)
    second = jnp.where(core == 0, other, mine)
    return jnp.concatenate([first, second], axis)


def pad_last(value):
    return jnp.pad(value, [(0, 0)] * (value.ndim - 1) + [(0, DP - value.shape[-1])])


def pad_rows(value, count):
    return jnp.pad(value, ((0, count - value.shape[0]), (0, 0)))


def sum_steps(value, index, count):
    levels = count.bit_length() - 1
    for level in range(levels):
        halves = value.reshape(2, -1, value.shape[-1])
        low = (index >> level) & 1 == 0
        keep = jnp.where(low, halves[0], halves[1])
        value = keep + (yield level, jnp.where(low, halves[1], halves[0]))
    for level in reversed(range(levels)):
        low = (index >> level) & 1 == 0
        got = yield level, value
        value = jnp.concatenate([jnp.where(low, value, got), jnp.where(low, got, value)])
    yield None, value


class ChipSum:
    def __init__(self, value, index, count):
        self.count = count
        self.steps = sum_steps(value, index, count)
        self.level, self.value = next(self.steps)
        self.got = None

    def send(self):
        if self.level is not None:
            pairs = [(i, i ^ (1 << self.level)) for i in range(self.count)]
            self.got = lax.ppermute(self.value, "zy", pairs)

    def take(self, *others):
        if self.level is not None:
            got = after(self.got, *others) if others else self.got
            self.level, self.value = self.steps.send(got)
            self.got = None
        return self.value

    def finish(self, *others):
        while self.level is not None:
            if self.got is None:
                self.send()
            self.take(*others)
        return self.value


def on_device(chips, stream, lengths, w_qkv, b_qkv, w_out, b_out, w_up, b_up, w_down, b_down, cotangent):
    core = lax.axis_index("core")
    chip = lax.axis_index("x")
    place = lax.axis_index("zy")
    stays = core == chip
    half, rows = stream.shape

    def home(value):
        return jnp.where(stays, value, cross(value))

    side = core[None].astype(jnp.int32)

    part = w_out.shape[0] // 2
    units = DP
    own_mlp = jnp.concatenate(
        [
            jnp.pad(quarter(w_up, core, 1), ((0, DP - DS), (0, 0))),
            pad_last(quarter(w_down, core, 0)),
            pad_last(quarter(w_out, core, 0)),
            pad_last(quarter(w_out, 1 - core, 0)),
            pad_rows(quarter(b_up, core, 0)[None], 128),
        ]
    )
    share = own_mlp.shape[0] // chips
    piece = lax.dynamic_slice_in_dim(own_mlp, place * share, share, 0)
    got_piece = swap(piece, "x")
    x_mine = home(stream)
    other_mlp = lax.all_gather(got_piece, "zy", axis=0, tiled=True)

    outs = 3 * HS
    heads = b_qkv.shape[1] // (2 * HS)
    head_w = pad_last(quarter(w_qkv, core, 1)).reshape(3, heads, HS, DP).swapaxes(0, 1).reshape(heads, outs, DP)
    head_b = quarter(b_qkv, core, 1).reshape(3, heads, HS).swapaxes(0, 1).reshape(heads, 1, outs)
    head_b = jnp.pad(head_b, ((0, 0), (0, PAD - 1), (0, DP - outs)))
    own_qkv = jnp.concatenate([head_w, head_b], 1).reshape(-1, DP)
    x_mine, own_qkv = lax.optimization_barrier((x_mine, own_qkv, got_piece))[:2]
    x_other = swap(x_mine, "core")
    other_qkv = swap(own_qkv, "x")

    normed_one, stats_one, qkv_own, mixed_own, logs_own = norm_attend(side, x_mine, x_other, own_qkv)
    mixed_own_far = swap(mixed_own, "core")
    length = after(lengths, mixed_own)
    length = jnp.where(stays, length, swap(length.astype(F32), "core").astype(jnp.int32))
    where = jnp.concatenate([side, length])
    c_mine = home(after(cotangent, mixed_own))
    qkv_other, mixed_other, logs_other = more_attend(normed_one, other_qkv)
    mixed_other_far = swap(mixed_other, "core")
    c_mine = after(c_mine, mixed_other)
    c_other = swap(c_mine, "core")

    y_own, stats_two, normed_two, m_other, dn_two, gd_own, gu_own, gd_other, gu_other = mlp(
        where,
        (mixed_own, mixed_other, mixed_own_far, mixed_other_far),
        jnp.pad(b_out, (0, 1))[None],
        jnp.pad(b_down, (0, 1))[None],
        (x_mine, x_other),
        (c_mine, c_other),
        (own_mlp, other_mlp),
    )
    dn_two_far = swap(dn_two, "core")
    got_down = swap(gd_other, "x")
    got_up = swap(gu_other, "x")
    m_far = swap(m_other, "core")
    dh_own, grad_mixed, out_own, out_other = out_back(
        where,
        (dn_two, dn_two_far),
        normed_two,
        stats_two,
        (c_mine, c_other),
        (own_mlp, other_mlp),
        (mixed_own, mixed_other),
    )

    got_out = swap(out_other, "x")
    back = {}
    sets = {0: (qkv_own, mixed_own, logs_own), 1: (qkv_other, mixed_other, logs_other)}

    def run_head(which, head, *first):
        qkv, mixed, logs = sets[which]
        done = attend_back(after(qkv, *first), grad_mixed, mixed, logs, normed_one, head, which * heads + head)
        back[which, head] = done
        return done[0]

    total_down = gd_own + after(got_down, grad_mixed)
    last = run_head(1, 0, grad_mixed, total_down)
    sum_down = lax.psum(total_down, "zy")
    last = run_head(1, 1, last)
    result = (y_own + after(m_far, last).astype(F32)).astype(BF)
    last = run_head(1, 2, last, result)
    total_rest = jnp.concatenate([gu_own + after(got_up, last), out_own + after(got_out, last)])
    rest = ChipSum(pad_rows(total_rest, 1024), place, chips)
    output = home(after(result, total_rest))

    def qkv_pack(which):
        return pad_rows(jnp.concatenate([back[which, head][1] for head in range(heads)]), 640)

    got_qkv = swap(qkv_pack(1), "x")
    rest.send()
    for head in range(heads):
        last = run_head(0, head, last, rest.value)
        if head:
            rest.take(last)
            rest.send()
    qkv = ChipSum(qkv_pack(0) + after(got_qkv, last), place, chips)
    qkv.send()
    normed_late = after(normed_one, qkv.value, rest.value, output, last)
    dn_own, dn_other, inner = project_back(
        where,
        [back[which, head][0] for which in (0, 1) for head in range(heads)],
        normed_late,
        (own_qkv, other_qkv),
    )
    rest.take(dn_own)
    rest.send()
    qkv.take(dn_own)
    qkv.send()
    dn_far = swap(after(dn_other, rest.value, qkv.value, sum_down), "core")
    inner = inner[0:1] + swap(inner, "core")[0:1]
    row_mask = core * half + lax.broadcasted_iota(jnp.int32, (half, 1), 0) < DS
    scale_one, total_one = stats_one[0:1], stats_one[1:2]
    grad_in = dh_own.astype(F32) + jnp.where(
        row_mask,
        scale_one * (dn_own.astype(F32) + dn_far.astype(F32))
        - scale_one * scale_one * (x_mine.astype(F32) + total_one) * inner / DP,
        0.0,
    )
    grad_sent = grad_in.astype(BF)
    grad_got = cross(grad_sent)
    grad_stream = jnp.where(stays, grad_sent, grad_got).astype(F32)
    def gather(mine, far, pick, axis):
        return both(pick(mine), pick(far), core, axis).astype(F32)

    def by_head(value):
        return value[: heads * (outs + PAD)].reshape(heads, outs + PAD, DP)

    def pick_w(value):
        return by_head(value)[:, :outs, :DS].reshape(heads, 3, HS, DS).swapaxes(0, 1).reshape(3, -1, DS)

    def pick_b(value):
        return by_head(value)[:, outs, :outs].reshape(heads, 3, HS).swapaxes(0, 1).reshape(3, -1)

    qkv.take(grad_sent)
    qkv.send()
    rest.take(qkv.value)
    rest.send()
    far_down = swap(after(sum_down, qkv.value), "core")
    qkv.take()
    qkv.send()
    rest.take(qkv.value)
    rest.send()
    grad_w_down = gather(sum_down, far_down, lambda v: v[:, :DS], 0)
    qkv.take(grad_w_down)
    qkv.send()
    qkv.take(grad_got)
    qkv.send()
    sum_rest = rest.finish(qkv.value)
    far_rest = swap(sum_rest, "core")
    edge = DP + PAD
    grad_w_up = gather(sum_rest, far_rest, lambda v: v[:DS], 1)
    grad_w_out = gather(sum_rest, far_rest, lambda v: v[edge : edge + part, :DS], 0)
    sum_qkv = qkv.finish(grad_w_up, grad_w_out, grad_stream)
    far_qkv = swap(sum_qkv, "core")

    return (
        output,
        grad_stream,
        gather(sum_qkv, far_qkv, pick_w, 1),
        gather(sum_qkv, far_qkv, pick_b, 1),
        grad_w_out,
        sum_rest[edge + part, :DS].astype(F32),
        grad_w_up,
        gather(sum_rest, far_rest, lambda v: v[DP], 0),
        grad_w_down,
        sum_rest[DP + 1, :DS].astype(F32),
    )


def solution(mesh):
    dp, mp = mesh.shape["dp"], mesh.shape["mp"]
    fine = Mesh(mesh.devices.reshape(dp // 2, 2, mp), ("zy", "core", "x"))
    seqs = ("zy", "core")
    placed = (
        P("x", seqs),
        P(seqs),
        P(None, "x", None),
        P(None, "x"),
        P("x", None),
        P(),
        P(None, "x"),
        P("x"),
        P("x", None),
        P(),
        P("x", seqs),
    )
    return jax.shard_map(
        functools.partial(on_device, dp // 2),
        mesh=fine,
        in_specs=placed,
        out_specs=(
            P("x", seqs),
            P("x", seqs),
            P(None, "x", None),
            P(None, "x"),
            P("x", None),
            P(),
            P(None, "x"),
            P("x"),
            P("x", None),
            P(),
        ),
        check_vma=False,
    )
```

```python
import functools

import jax
import jax.numpy as jnp
from jax import lax
from jax.experimental import pallas as pl
from jax.experimental.pallas import tpu as pltpu
from jax.sharding import Mesh
from jax.sharding import PartitionSpec as P

HS = 64
DS = 767
DP = 768
BLK = 256
EPSILON = 1e-05
NEGATIVE = -1e30
F32 = jnp.float32
BF = jnp.bfloat16
VMEM_MIB = {
    "norm_attend": 28,
    "attend": 26,
    "out_project_mlp": 54,
    "out_project_back": 56,
    "attend_back": 30,
    "project_back": 22,
}
ROWS_BLK = 512
UNIT_BLK = 256
PAD = 16
BACK_MICROS = (8, 3, 3, 4, 4, 4)


def dot(left, right, left_dim, right_dim):
    return lax.dot_general(
        left, right, (((left_dim,), (right_dim,)), ((), ())), preferred_element_type=F32
    )


def call(body, name, micros, grid, in_specs, out_specs, out_shape, scratch, prefetch=0):
    return pl.pallas_call(
        body,
        grid_spec=pltpu.PrefetchScalarGridSpec(
            num_scalar_prefetch=prefetch,
            grid=grid,
            in_specs=in_specs,
            out_specs=out_specs,
            scratch_shapes=scratch,
        ),
        out_shape=out_shape,
        compiler_params=pltpu.CompilerParams(vmem_limit_bytes=VMEM_MIB[name] * 1024 * 1024),
        cost_estimate=pl.CostEstimate(flops=int(micros * 1e9), bytes_accessed=0, transcendentals=0),
        name=name,
    )


def rows_spec(height, block):
    return pl.BlockSpec((height, block), lambda i, *_: (0, i))


def whole_spec(shape):
    return pl.BlockSpec(shape, lambda i, *_: (0,) * len(shape), pipeline_mode=pl.Buffered(1))


def shape_of(shape, dtype):
    return jax.ShapeDtypeStruct(shape, dtype)


def join_halves(scratch, mine_ref, other_ref, core):
    half = mine_ref.shape[0]
    scratch[pl.ds(pl.multiple_of(core * half, half), half), :] = mine_ref[...]
    scratch[pl.ds(pl.multiple_of((1 - core) * half, half), half), :] = other_ref[...]
    return scratch[...]


def crms_stats(values):
    kept = jnp.where(lax.broadcasted_iota(jnp.int32, values.shape, 0) < DS, values, 0.0)
    total = jnp.sum(kept, 0, keepdims=True)
    squares = jnp.sum(kept * kept, 0, keepdims=True)
    scale = lax.rsqrt((squares + total * total) / DP + EPSILON)
    return kept, scale, total


def causal_tile():
    key_pos = lax.broadcasted_iota(jnp.int32, (BLK, BLK), 0)
    query_pos = lax.broadcasted_iota(jnp.int32, (BLK, BLK), 1)
    return key_pos <= query_pos


def attend_head(w_ref, normed_ref, qkv_ref, a_ref, log_ref, s_scr, p_scr):
    rows = normed_ref.shape[1]
    blocks = rows // BLK
    outs = 3 * HS
    bias = w_ref[outs : outs + 1, :outs].astype(F32).T
    qkv_ref[...] = (dot(w_ref[:outs, :], normed_ref[...], 1, 0) + bias).astype(BF)
    key_rows = qkv_ref[HS : 2 * HS, :].T
    queries = qkv_ref[:HS, :] * jnp.asarray(0.125, BF)
    allowed = causal_tile()

    def score(blk):
        at = slice(blk * BLK, (blk + 1) * BLK)
        count = (blk + 1) * BLK
        scores = dot(key_rows[:count], queries[:, at], 1, 0)
        if blk:
            s_scr[blk % 2, : count - BLK] = scores[: count - BLK]
        s_scr[blk % 2, count - BLK : count] = jnp.where(allowed, scores[count - BLK :], NEGATIVE)

    def soften(blk):
        count = (blk + 1) * BLK
        top = jnp.max(s_scr[blk % 2, :count], axis=0, keepdims=True)
        expo = jnp.exp(s_scr[blk % 2, :count] - top)
        total = jnp.sum(expo, axis=0, keepdims=True)
        p_scr[blk % 2, :count] = expo.astype(BF)
        log_ref[0, :, blk * BLK : count] = top + jnp.log(total)
        return total

    def mix(blk, total):
        count = (blk + 1) * BLK
        mixed = dot(qkv_ref[2 * HS :, :count], p_scr[blk % 2, :count], 1, 0)
        a_ref[:, blk * BLK : count] = (mixed * (1.0 / total)).astype(BF)

    score(0)
    totals = {}
    for blk in range(blocks):
        if blk + 1 < blocks:
            score(blk + 1)
        if blk:
            mix(blk - 1, totals[blk - 1])
        totals[blk] = soften(blk)
    mix(blocks - 1, totals[blocks - 1])


def norm_attend_body(
    where_ref, mine_ref, other_ref, w_ref, normed_ref, stats_ref, qkv_ref, a_ref, log_ref, s_scr, p_scr
):
    @pl.when(pl.program_id(0) == 0)
    def _():
        half = mine_ref.shape[0]
        core = where_ref[0]
        first = pl.ds(pl.multiple_of(core * half, half), half)
        second = pl.ds(pl.multiple_of((1 - core) * half, half), half)
        normed_ref[first, :] = mine_ref[...]
        normed_ref[second, :] = other_ref[...]
        for start in range(0, normed_ref.shape[1], BLK):
            at = slice(start, start + BLK)
            kept, scale, total = crms_stats(normed_ref[:, at].astype(F32))
            normed_ref[:, at] = (kept * scale).astype(BF)
            stats_ref[0:1, at] = scale
            stats_ref[1:2, at] = total

    attend_head(w_ref, normed_ref, qkv_ref, a_ref, log_ref, s_scr, p_scr)


def attend_specs(heads, rows):
    outs = 3 * HS
    ins = [pl.BlockSpec((outs + PAD, DP), lambda h, *_: (h, 0))]
    results = [
        pl.BlockSpec((outs, rows), lambda h, *_: (h, 0)),
        pl.BlockSpec((HS, rows), lambda h, *_: (h, 0)),
        pl.BlockSpec((1, 1, rows), lambda h, *_: (h, 0, 0)),
    ]
    shapes = [
        shape_of((heads * outs, rows), BF),
        shape_of((heads * HS, rows), BF),
        shape_of((heads, 1, rows), F32),
    ]
    scratch = [pltpu.VMEM((2, rows, BLK), F32), pltpu.VMEM((2, rows, BLK), BF)]
    return ins, results, shapes, scratch


def norm_attend(where, mine, other, weights):
    half, rows = mine.shape
    heads = weights.shape[0] // (3 * HS + PAD)
    ins, results, shapes, scratch = attend_specs(heads, rows)
    return call(
        norm_attend_body,
        "norm_attend",
        22,
        (heads,),
        [whole_spec((half, rows)), whole_spec((half, rows))] + ins,
        [whole_spec((DP, rows)), whole_spec((8, rows))] + results,
        [shape_of((DP, rows), BF), shape_of((8, rows), F32)] + shapes,
        scratch,
        1,
    )(where, mine, other, weights)


def more_attend_body(normed_ref, w_ref, qkv_ref, a_ref, log_ref, s_scr, p_scr):
    attend_head(w_ref, normed_ref, qkv_ref, a_ref, log_ref, s_scr, p_scr)


def more_attend(normed, weights):
    rows = normed.shape[1]
    heads = weights.shape[0] // (3 * HS + PAD)
    ins, results, shapes, scratch = attend_specs(heads, rows)
    return call(
        more_attend_body,
        "attend",
        20,
        (heads,),
        [whole_spec((DP, rows))] + ins,
        results,
        shapes,
        scratch,
    )(normed, weights)


def attend_back_body(
    qkv_ref, da_ref, a_ref, log_ref, normed_hbm, grad_ref, gw_ref,
    p_scr, ds_scr, s_scr, dp_scr, dq_scr, normed_scr, sem,
):
    fetch = pltpu.make_async_copy(normed_hbm, normed_scr, sem)
    fetch.start()
    rows = qkv_ref.shape[1]
    blocks = rows // BLK
    queries = qkv_ref[:HS, :] * jnp.asarray(0.125, BF)
    query_rows = queries.T
    key_rows = qkv_ref[HS : 2 * HS, :].T
    value_rows = qkv_ref[2 * HS :, :].T
    grad = da_ref[...]
    grad_rows = grad.T
    row_dot = jnp.sum(grad.astype(F32) * a_ref[...].astype(F32), axis=0, keepdims=True)
    logs = log_ref[0]
    allowed = causal_tile()

    def span(blk):
        return slice(blk * BLK, (blk + 1) * BLK)

    def score(blk):
        start = blk * BLK
        s_scr[blk % 2, :, start:] = dot(key_rows[span(blk)], queries[:, start:], 1, 0)
        dp_scr[blk % 2, :, start:] = dot(value_rows[span(blk)], grad[:, start:], 1, 0)

    def soften(blk):
        slot = blk % 2
        for query_blk in range(blk, blocks):
            at = span(query_blk)
            probs = jnp.exp(s_scr[slot, :, at] - logs[:, at])
            if query_blk == blk:
                probs = jnp.where(allowed, probs, 0.0)
            p_scr[slot, :, at] = probs.astype(BF)
            ds_scr[slot, :, at] = (probs * (dp_scr[slot, :, at] - row_dot[:, at])).astype(BF)

    def mix(blk):
        slot, start = blk % 2, blk * BLK
        grad_keys = dot(ds_scr[slot, :, start:], query_rows[start:], 1, 0)
        grad_values = dot(p_scr[slot, :, start:], grad_rows[start:], 1, 0)
        grad_queries = dot(qkv_ref[HS : 2 * HS, span(blk)], ds_scr[slot, :, start:], 1, 0)
        if blk:
            dq_scr[:, start:] += grad_queries
        else:
            dq_scr[...] = grad_queries
        grad_ref[HS : 2 * HS, span(blk)] = grad_keys.T.astype(BF)
        grad_ref[2 * HS :, span(blk)] = grad_values.T.astype(BF)

    score(0)
    for blk in range(blocks):
        if blk + 1 < blocks:
            score(blk + 1)
        if blk:
            mix(blk - 1)
        soften(blk)
    mix(blocks - 1)
    grad_ref[:HS, :] = (dq_scr[...] * 0.125).astype(BF)
    fetch.wait()
    outs = 3 * HS
    gw_ref[:outs, :] = dot(grad_ref[...], normed_scr[...], 1, 1).astype(BF)
    gw_ref[outs:, :] = jnp.zeros((PAD, DP), BF)
    gw_ref[outs : outs + 1, :outs] = jnp.sum(grad_ref[...].astype(F32), 1, keepdims=True).T.astype(BF)


def attend_back(qkv, grad, mixed, logs, normed, head, grad_head):
    rows = qkv.shape[1]
    outs = 3 * HS
    return call(
        attend_back_body,
        "attend_back",
        BACK_MICROS[grad_head],
        (1,),
        [
            pl.BlockSpec((outs, rows), lambda i: (head, 0)),
            pl.BlockSpec((HS, rows), lambda i: (grad_head, 0)),
            pl.BlockSpec((HS, rows), lambda i: (head, 0)),
            pl.BlockSpec((1, 1, rows), lambda i: (head, 0, 0)),
            pl.BlockSpec(memory_space=pl.ANY),
        ],
        [
            pl.BlockSpec((outs, rows), lambda i: (0, 0)),
            pl.BlockSpec((outs + PAD, DP), lambda i: (0, 0)),
        ],
        [shape_of((outs, rows), BF), shape_of((outs + PAD, DP), BF)],
        [
            pltpu.VMEM((2, BLK, rows), BF),
            pltpu.VMEM((2, BLK, rows), BF),
            pltpu.VMEM((2, BLK, rows), F32),
            pltpu.VMEM((2, BLK, rows), F32),
            pltpu.VMEM((HS, rows), F32),
            pltpu.VMEM((DP, rows), BF),
            pltpu.SemaphoreType.DMA(()),
        ],
    )(qkv, grad, mixed, logs, normed)


GELU_A = 0.7978845608028654
GELU_B = 0.044715


def gelu_pair(pre):
    square = pre * pre
    bent = jnp.tanh(GELU_A * pre * (1.0 + GELU_B * square))
    half_up = 0.5 * (1.0 + bent)
    slope = half_up + 0.5 * pre * (1.0 - bent * bent) * (GELU_A * (1.0 + 3.0 * GELU_B * square))
    return pre * half_up, slope


def mlp_body(
    where_ref, a0, a1, a2, a3, wout0, wout1, wout2, wout3, b_out, b_down, x_mine, x_other, c_mine, c_other, w_own, w_other,
    y_ref, stats_ref, normed_ref, m_other_ref, dn_ref, gd_own, gu_own, gd_other, gu_other,
    wout, a_scr, x_scr, c_scr, h_scr, up_scr, down_scr, bias_scr, pre_scr, back_scr, g_scr, du_scr, gd, gu, gb, pack_scr, w_sem, pack_sem,
):
    step = pl.program_id(0)
    last = pl.num_programs(0) - 1
    core = where_ref[0]
    half, block = x_mine.shape
    units = DP
    fetch = []
    for i, ref in enumerate((w_own, w_other)):
        at = pl.ds(i * units, units)
        for j, (source, target) in enumerate(
            (
                (ref.at[pl.ds(0, DP), :], up_scr.at[:, at]),
                (ref.at[pl.ds(DP, units), :], down_scr.at[at, :]),
                (ref.at[pl.ds(DP + units + 2 * a0.shape[0], PAD), :], bias_scr.at[:, at]),
            )
        ):
            fetch.append(pltpu.make_async_copy(source, target, w_sem.at[i, j]))
    split = ((gd_own, pl.ds(0, units)), (gu_own, pl.ds(units, DP + PAD)))
    split += ((gd_other, pl.ds(0, units)), (gu_other, pl.ds(units, DP + PAD)))
    store = [
        pltpu.make_async_copy(pack_scr.at[i // 2, at, :], ref, pack_sem.at[i]) for i, (ref, at) in enumerate(split)
    ]

    @pl.when(step == 0)
    def _():
        for copy in fetch:
            copy.start()
        start = 0
        for ref in (wout0, wout1, wout2, wout3):
            wout[start : start + ref.shape[0], :] = ref[...]
            start += ref.shape[0]
        for ref in (gd, gu, gb):
            ref[...] = jnp.zeros_like(ref)

    for i, a_ref in enumerate((a0, a1, a2, a3)):
        part = a_ref.shape[0]
        a_scr[i * part : (i + 1) * part, :] = a_ref[...]
    position = step * block + lax.broadcasted_iota(jnp.int32, (1, block), 1)
    valid = (position < where_ref[1]).astype(F32)
    stream = join_halves(x_scr, x_mine, x_other, core).astype(F32)
    branch = dot(wout[...], a_scr[...], 0, 0) + b_out[...].astype(F32).T
    hidden = stream + valid * branch
    h_scr[...] = hidden
    kept, scale, total = crms_stats(hidden)
    stats_ref[0:1, :] = scale
    stats_ref[1:2, :] = total
    normed = (kept * scale).astype(BF)
    normed_ref[...] = normed
    grad_out = join_halves(c_scr, c_mine, c_other, core)
    keep_row = lax.broadcasted_iota(jnp.int32, (DP, block), 0) < DS
    dm = jnp.where(keep_row, grad_out.astype(F32) * valid, 0.0).astype(BF)

    @pl.when(step == 0)
    def _():
        for copy in fetch:
            copy.wait()

    ones = jnp.ones((block, 128), BF)
    gb[2 * units :] += dot(dm, ones, 1, 0)
    starts = [which * units + start for which in (1, 0) for start in range(0, units, UNIT_BLK)]

    def expand(i):
        at = slice(starts[i], starts[i] + UNIT_BLK)
        pre_scr[i % 2] = dot(up_scr[:, at], normed, 0, 0)
        back_scr[i % 2] = dot(down_scr[at, :], dm, 1, 0)

    def bend(i):
        at = slice(starts[i], starts[i] + UNIT_BLK)
        act, slope = gelu_pair(pre_scr[i % 2] + bias_scr[0:1, at].astype(F32).T)
        g_scr[at, :] = act.astype(BF)
        du_scr[at, :] = (back_scr[i % 2] * slope).astype(BF)

    def collect(i):
        at = slice(starts[i], starts[i] + UNIT_BLK)
        gd[at, :] += dot(g_scr[at, :], dm, 1, 1)
        gu[:, at] += dot(normed, du_scr[at, :], 1, 1)
        gb[at] += dot(du_scr[at, :], ones, 1, 0)

    expand(0)
    for i in range(len(starts)):
        if i + 1 < len(starts):
            expand(i + 1)
        if i:
            collect(i - 1)
        bend(i)
    collect(len(starts) - 1)

    @pl.when(step == last)
    def _():
        for which in (1, 0):
            mine = slice(which * units, (which + 1) * units)
            pack_scr[which, 0:units, :] = gd[mine, :].astype(BF)
            pack_scr[which, units : units + DP, :] = gu[:, mine].astype(BF)
            pack_scr[which, units + DP :, :] = jnp.zeros((PAD, DP), BF)
            pack_scr[which, units + DP : units + DP + 1, :] = gb[mine].T[:1].astype(BF)
            pack_scr[which, units + DP + 1 : units + DP + 2, :] = gb[2 * units :].T[:1].astype(BF)
            store[2 * which].start()
            store[2 * which + 1].start()

    own = pl.ds(pl.multiple_of(core * half, half), half)
    far = pl.ds(pl.multiple_of((1 - core) * half, half), half)
    m_part = h_scr
    column = b_down[...].astype(F32).T
    bias = jnp.where(core == 0, column[:half], column[half:])
    y_ref[...] = h_scr[own, :] + valid * bias
    m_part[...] = dot(down_scr[...], g_scr[...], 0, 0)
    y_ref[...] += valid * m_part[own, :]
    m_other_ref[...] = (valid * m_part[far, :]).astype(BF)
    dn_ref[...] = dot(up_scr[...], du_scr[...], 1, 0).astype(BF)

    @pl.when(step == last)
    def _():
        for copy in store:
            copy.wait()


def pack_rows(part, which):
    return pl.BlockSpec((part, DP), lambda i, *_: (2 * DP // part + which, 0), pipeline_mode=pl.Buffered(1))


def mlp(where, mixed, b_out, b_down, stream, cot, weights):
    half, rows = stream[0].shape
    part = mixed[0].shape[0]
    units = DP
    block = ROWS_BLK
    pack = (units + DP + PAD, DP)
    anywhere = pl.BlockSpec(memory_space=pl.ANY)
    return call(
        mlp_body,
        "out_project_mlp",
        40,
        (rows // block,),
        [rows_spec(part, block)] * 4
        + [pack_rows(part, which) for which in (0, 0, 1, 1)]
        + [whole_spec((1, DP))] * 2
        + [rows_spec(half, block)] * 4
        + [anywhere] * 2,
        [
            rows_spec(half, block),
            rows_spec(8, block),
            rows_spec(DP, block),
            rows_spec(half, block),
            rows_spec(DP, block),
        ]
        + [anywhere] * 4,
        [
            shape_of((half, rows), F32),
            shape_of((8, rows), F32),
            shape_of((DP, rows), BF),
            shape_of((half, rows), BF),
            shape_of((DP, rows), BF),
        ]
        + [shape_of((units, DP), BF), shape_of((DP + PAD, DP), BF)] * 2,
        [pltpu.VMEM((DP, DP), BF)]
        + [pltpu.VMEM((DP, block), BF)] * 3
        + [
            pltpu.VMEM((DP, block), F32),
            pltpu.VMEM((DP, 2 * units), BF),
            pltpu.VMEM((2 * units, DP), BF),
            pltpu.VMEM((PAD, 2 * units), BF),
            pltpu.VMEM((2, UNIT_BLK, block), F32),
            pltpu.VMEM((2, UNIT_BLK, block), F32),
            pltpu.VMEM((2 * units, block), BF),
            pltpu.VMEM((2 * units, block), BF),
            pltpu.VMEM((2 * units, DP), F32),
            pltpu.VMEM((DP, 2 * units), F32),
            pltpu.VMEM((2 * units + DP, 128), F32),
            pltpu.VMEM((2, *pack), BF),
            pltpu.SemaphoreType.DMA((2, 3)),
            pltpu.SemaphoreType.DMA((4,)),
        ],
        1,
    )(where, *mixed, *weights, *weights, b_out, b_down, *stream, *cot, *weights)


def out_back_body(
    where_ref, dn_mine, dn_other, normed_ref, stats_ref, c_mine, c_other, w0, w1, a0, a1,
    dh_ref, da_ref, pack_own, pack_other, c_scr, dh_scr, gw_scr, gb_scr,
):
    step = pl.program_id(0)
    core = where_ref[0]
    half, block = c_mine.shape
    position = step * block + lax.broadcasted_iota(jnp.int32, (1, block), 1)
    valid = (position < where_ref[1]).astype(F32)
    row_mask = lax.broadcasted_iota(jnp.int32, (DP, 1), 0) < DS
    grad_norm = dn_mine[...].astype(F32) + dn_other[...].astype(F32)
    normed = normed_ref[...].astype(F32)
    scale, total = stats_ref[0:1, :], stats_ref[1:2, :]
    inner = jnp.sum(grad_norm * normed, 0, keepdims=True) * (1.0 / DP)
    grad_out = join_halves(c_scr, c_mine, c_other, core).astype(F32)
    pulled = scale * (grad_norm - (normed + scale * total) * inner)
    grad_hidden = grad_out + jnp.where(row_mask, pulled, 0.0)
    dh_scr[...] = grad_hidden
    dh_ref[...] = dh_scr[pl.ds(pl.multiple_of(core * half, half), half), :].astype(BF)
    branch_f = jnp.where(row_mask, grad_hidden * valid, 0.0)
    branch = branch_f.astype(BF)
    part = a0.shape[0]
    da_ref[:part, :] = dot(w0[...], branch, 1, 0).astype(BF)
    da_ref[part:, :] = dot(w1[...], branch, 1, 0).astype(BF)

    @pl.when(step == 0)
    def _():
        gw_scr[...] = jnp.zeros_like(gw_scr)
        gb_scr[...] = jnp.zeros_like(gb_scr)

    gw_scr[:part] += dot(a0[...], branch, 1, 1)
    gw_scr[part:] += dot(a1[...], branch, 1, 1)
    gb_scr[...] += jnp.sum(branch_f, 1, keepdims=True)

    @pl.when(step == pl.num_programs(0) - 1)
    def _():
        for i, pack in enumerate((pack_own, pack_other)):
            pack[:part, :] = gw_scr[i * part : (i + 1) * part, :].astype(BF)
            pack[part:, :] = jnp.zeros((PAD, DP), BF)
            pack[part : part + 1, :] = gb_scr[...].T.astype(BF)


def out_back(where, dn, normed, stats, cot, weights, mixed):
    rows = normed.shape[1]
    half = cot[0].shape[0]
    part = mixed[0].shape[0]
    block = ROWS_BLK
    return call(
        out_back_body,
        "out_project_back",
        12,
        (rows // block,),
        [rows_spec(DP, block)] * 3
        + [rows_spec(8, block)]
        + [rows_spec(half, block)] * 2
        + [pack_rows(part, 0)] * 2
        + [rows_spec(part, block)] * 2,
        [
            rows_spec(half, block),
            rows_spec(2 * part, block),
            whole_spec((part + PAD, DP)),
            whole_spec((part + PAD, DP)),
        ],
        [
            shape_of((half, rows), BF),
            shape_of((2 * part, rows), BF),
            shape_of((part + PAD, DP), BF),
            shape_of((part + PAD, DP), BF),
        ],
        [
            pltpu.VMEM((DP, block), BF),
            pltpu.VMEM((DP, block), F32),
            pltpu.VMEM((2 * part, DP), F32),
            pltpu.VMEM((DP, 1), F32),
        ],
        1,
    )(where, *dn, normed, stats, *cot, *weights, *mixed)


def project_back_body(
    where_ref, g0, g1, g2, g3, g4, g5, normed_ref, w0, w1, dn_own_ref, dn_other_ref, inner_ref, p_scr, dn_scr, w_scr
):
    core = where_ref[0]
    outs = 3 * HS

    @pl.when(pl.program_id(0) == 0)
    def _():
        at = 0
        for ref in (w0, w1):
            for start in range(0, ref.shape[0], outs + PAD):
                w_scr[at : at + outs, :] = ref[start : start + outs, :]
                at += outs

    part = g0.shape[0]
    for i, ref in enumerate((g0, g1, g2, g3, g4, g5)):
        p_scr[i * part : (i + 1) * part, :] = ref[...]
    grad_norm = dot(w_scr[...], p_scr[...], 0, 0)
    dn_scr[...] = grad_norm
    half = DP // 2
    dn_own_ref[...] = dn_scr[pl.ds(pl.multiple_of(core * half, half), half), :].astype(BF)
    dn_other_ref[...] = dn_scr[pl.ds(pl.multiple_of((1 - core) * half, half), half), :].astype(BF)
    inner = jnp.sum(grad_norm * normed_ref[...].astype(F32), 0, keepdims=True)
    inner_ref[...] = jnp.broadcast_to(inner, inner_ref.shape)


def project_back(where, grads, normed, weights):
    part, rows = grads[0].shape
    half = DP // 2
    block = ROWS_BLK
    return call(
        project_back_body,
        "project_back",
        8,
        (rows // block,),
        [rows_spec(part, block)] * 6 + [rows_spec(DP, block)] + [whole_spec(w.shape) for w in weights],
        [rows_spec(half, block), rows_spec(half, block), rows_spec(8, block)],
        [shape_of((half, rows), BF), shape_of((half, rows), BF), shape_of((8, rows), F32)],
        [pltpu.VMEM((6 * part, block), BF), pltpu.VMEM((DP, block), F32), pltpu.VMEM((6 * part, DP), BF)],
        1,
    )(where, *grads, normed, *weights)


def swap(value, axis):
    return lax.ppermute(value, axis, [(0, 1), (1, 0)])


def cross(value):
    return lax.ppermute(value, ("core", "x"), [(1, 2), (2, 1)])


def after(value, *others):
    return lax.optimization_barrier((value, *others))[0]


def quarter(value, core, axis):
    size = value.shape[axis] // 2
    return lax.dynamic_slice_in_dim(value, core * size, size, axis)


def both(mine, other, core, axis):
    first = jnp.where(core == 0, mine, other)
    second = jnp.where(core == 0, other, mine)
    return jnp.concatenate([first, second], axis)


def pad_last(value):
    return jnp.pad(value, [(0, 0)] * (value.ndim - 1) + [(0, DP - value.shape[-1])])


def pad_rows(value, count):
    return jnp.pad(value, ((0, count - value.shape[0]), (0, 0)))


def sum_steps(value, index, count):
    levels = count.bit_length() - 1
    for level in range(levels):
        halves = value.reshape(2, -1, value.shape[-1])
        low = (index >> level) & 1 == 0
        keep = jnp.where(low, halves[0], halves[1])
        value = keep + (yield level, jnp.where(low, halves[1], halves[0]))
    for level in reversed(range(levels)):
        low = (index >> level) & 1 == 0
        got = yield level, value
        value = jnp.concatenate([jnp.where(low, value, got), jnp.where(low, got, value)])
    yield None, value


class ChipSum:
    def __init__(self, value, index, count):
        self.count = count
        self.steps = sum_steps(value, index, count)
        self.level, self.value = next(self.steps)
        self.got = None

    def send(self):
        if self.level is not None:
            pairs = [(i, i ^ (1 << self.level)) for i in range(self.count)]
            self.got = lax.ppermute(self.value, "zy", pairs)

    def take(self, *others):
        if self.level is not None:
            got = after(self.got, *others) if others else self.got
            self.level, self.value = self.steps.send(got)
            self.got = None
        return self.value

    def finish(self, *others):
        while self.level is not None:
            if self.got is None:
                self.send()
            self.take(*others)
        return self.value


def on_device(chips, stream, lengths, w_qkv, b_qkv, w_out, b_out, w_up, b_up, w_down, b_down, cotangent):
    core = lax.axis_index("core")
    chip = lax.axis_index("x")
    place = lax.axis_index("zy")
    stays = core == chip
    half, rows = stream.shape

    def home(value):
        return jnp.where(stays, value, cross(value))

    side = core[None].astype(jnp.int32)

    part = w_out.shape[0] // 2
    units = DP
    own_mlp = jnp.concatenate(
        [
            jnp.pad(quarter(w_up, core, 1), ((0, DP - DS), (0, 0))),
            pad_last(quarter(w_down, core, 0)),
            pad_last(quarter(w_out, core, 0)),
            pad_last(quarter(w_out, 1 - core, 0)),
            pad_rows(quarter(b_up, core, 0)[None], 128),
        ]
    )
    share = own_mlp.shape[0] // chips
    piece = lax.dynamic_slice_in_dim(own_mlp, place * share, share, 0)
    got_piece = swap(piece, "x")
    x_mine = home(stream)
    other_mlp = lax.all_gather(got_piece, "zy", axis=0, tiled=True)

    outs = 3 * HS
    heads = b_qkv.shape[1] // (2 * HS)
    head_w = pad_last(quarter(w_qkv, core, 1)).reshape(3, heads, HS, DP).swapaxes(0, 1).reshape(heads, outs, DP)
    head_b = quarter(b_qkv, core, 1).reshape(3, heads, HS).swapaxes(0, 1).reshape(heads, 1, outs)
    head_b = jnp.pad(head_b, ((0, 0), (0, PAD - 1), (0, DP - outs)))
    own_qkv = jnp.concatenate([head_w, head_b], 1).reshape(-1, DP)
    x_mine, own_qkv = lax.optimization_barrier((x_mine, own_qkv, got_piece))[:2]
    x_other = swap(x_mine, "core")
    other_qkv = swap(own_qkv, "x")

    normed_one, stats_one, qkv_own, mixed_own, logs_own = norm_attend(side, x_mine, x_other, own_qkv)
    mixed_own_far = swap(mixed_own, "core")
    length = after(lengths, mixed_own)
    length = jnp.where(stays, length, swap(length.astype(F32), "core").astype(jnp.int32))
    where = jnp.concatenate([side, length])
    c_mine = home(after(cotangent, mixed_own))
    qkv_other, mixed_other, logs_other = more_attend(normed_one, other_qkv)
    mixed_other_far = swap(mixed_other, "core")
    c_mine = after(c_mine, mixed_other)
    c_other = swap(c_mine, "core")

    y_own, stats_two, normed_two, m_other, dn_two, gd_own, gu_own, gd_other, gu_other = mlp(
        where,
        (mixed_own, mixed_other, mixed_own_far, mixed_other_far),
        jnp.pad(b_out, (0, 1))[None],
        jnp.pad(b_down, (0, 1))[None],
        (x_mine, x_other),
        (c_mine, c_other),
        (own_mlp, other_mlp),
    )
    dn_two_far = swap(dn_two, "core")
    got_down = swap(gd_other, "x")
    got_up = swap(gu_other, "x")
    m_far = swap(m_other, "core")
    dh_own, grad_mixed, out_own, out_other = out_back(
        where,
        (dn_two, dn_two_far),
        normed_two,
        stats_two,
        (c_mine, c_other),
        (own_mlp, other_mlp),
        (mixed_own, mixed_other),
    )

    got_out = swap(out_other, "x")
    back = {}
    sets = {0: (qkv_own, mixed_own, logs_own), 1: (qkv_other, mixed_other, logs_other)}

    def run_head(which, head, *first):
        qkv, mixed, logs = sets[which]
        done = attend_back(after(qkv, *first), grad_mixed, mixed, logs, normed_one, head, which * heads + head)
        back[which, head] = done
        return done[0]

    total_down = gd_own + after(got_down, grad_mixed)
    last = run_head(1, 0, grad_mixed, total_down)
    sum_down = lax.psum(total_down, "zy")
    last = run_head(1, 1, last)
    result = (y_own + after(m_far, last).astype(F32)).astype(BF)
    last = run_head(1, 2, last, result)
    total_rest = jnp.concatenate([gu_own + after(got_up, last), out_own + after(got_out, last)])
    rest = ChipSum(pad_rows(total_rest, 1024), place, chips)
    output = home(after(result, total_rest))

    def qkv_pack(which):
        return pad_rows(jnp.concatenate([back[which, head][1] for head in range(heads)]), 640)

    got_qkv = swap(qkv_pack(1), "x")
    rest.send()
    for head in range(heads):
        last = run_head(0, head, last, rest.value)
        if head:
            rest.take(last)
            rest.send()
    qkv = ChipSum(qkv_pack(0) + after(got_qkv, last), place, chips)
    qkv.send()
    normed_late = after(normed_one, qkv.value, rest.value, output, last)
    dn_own, dn_other, inner = project_back(
        where,
        [back[which, head][0] for which in (0, 1) for head in range(heads)],
        normed_late,
        (own_qkv, other_qkv),
    )
    rest.take(dn_own)
    rest.send()
    qkv.take(dn_own)
    qkv.send()
    dn_far = swap(after(dn_other, rest.value, qkv.value, sum_down), "core")
    inner = inner[0:1] + swap(inner, "core")[0:1]
    row_mask = core * half + lax.broadcasted_iota(jnp.int32, (half, 1), 0) < DS
    scale_one, total_one = stats_one[0:1], stats_one[1:2]
    grad_in = dh_own.astype(F32) + jnp.where(
        row_mask,
        scale_one * (dn_own.astype(F32) + dn_far.astype(F32))
        - scale_one * scale_one * (x_mine.astype(F32) + total_one) * inner / DP,
        0.0,
    )
    grad_sent = grad_in.astype(BF)
    grad_got = cross(grad_sent)
    grad_stream = jnp.where(stays, grad_sent, grad_got).astype(F32)
    def gather(mine, far, pick, axis):
        return both(pick(mine), pick(far), core, axis).astype(F32)

    def by_head(value):
        return value[: heads * (outs + PAD)].reshape(heads, outs + PAD, DP)

    def pick_w(value):
        return by_head(value)[:, :outs, :DS].reshape(heads, 3, HS, DS).swapaxes(0, 1).reshape(3, -1, DS)

    def pick_b(value):
        return by_head(value)[:, outs, :outs].reshape(heads, 3, HS).swapaxes(0, 1).reshape(3, -1)

    qkv.take(grad_sent)
    qkv.send()
    rest.take(qkv.value)
    rest.send()
    far_down = swap(after(sum_down, qkv.value), "core")
    qkv.take()
    qkv.send()
    rest.take(qkv.value)
    rest.send()
    grad_w_down = gather(sum_down, far_down, lambda v: v[:, :DS], 0)
    qkv.take(grad_w_down)
    qkv.send()
    qkv.take(grad_got)
    qkv.send()
    sum_rest = rest.finish(qkv.value)
    far_rest = swap(sum_rest, "core")
    edge = DP + PAD
    grad_w_up = gather(sum_rest, far_rest, lambda v: v[:DS], 1)
    grad_w_out = gather(sum_rest, far_rest, lambda v: v[edge : edge + part, :DS], 0)
    sum_qkv = qkv.finish(grad_stream, sum_rest)
    far_qkv = swap(sum_qkv, "core")

    return (
        output,
        grad_stream,
        gather(sum_qkv, far_qkv, pick_w, 1),
        gather(sum_qkv, far_qkv, pick_b, 1),
        grad_w_out,
        sum_rest[edge + part, :DS].astype(F32),
        grad_w_up,
        gather(sum_rest, far_rest, lambda v: v[DP], 0),
        grad_w_down,
        sum_rest[DP + 1, :DS].astype(F32),
    )


def solution(mesh):
    dp, mp = mesh.shape["dp"], mesh.shape["mp"]
    fine = Mesh(mesh.devices.reshape(dp // 2, 2, mp), ("zy", "core", "x"))
    seqs = ("zy", "core")
    placed = (
        P("x", seqs),
        P(seqs),
        P(None, "x", None),
        P(None, "x"),
        P("x", None),
        P(),
        P(None, "x"),
        P("x"),
        P("x", None),
        P(),
        P("x", seqs),
    )
    return jax.shard_map(
        functools.partial(on_device, dp // 2),
        mesh=fine,
        in_specs=placed,
        out_specs=(
            P("x", seqs),
            P("x", seqs),
            P(None, "x", None),
            P(None, "x"),
            P("x", None),
            P(),
            P(None, "x"),
            P("x"),
            P("x", None),
            P(),
        ),
        check_vma=False,
    )
```

```python
import functools

import jax
import jax.numpy as jnp
from jax import lax
from jax.experimental import pallas as pl
from jax.experimental.pallas import tpu as pltpu
from jax.sharding import Mesh
from jax.sharding import PartitionSpec as P

HS = 64
DS = 767
DP = 768
BLK = 256
EPSILON = 1e-05
NEGATIVE = -1e30
F32 = jnp.float32
BF = jnp.bfloat16
VMEM_MIB = {
    "norm_attend": 28,
    "attend": 26,
    "out_project_mlp": 54,
    "out_project_back": 56,
    "attend_back": 30,
    "project_back": 22,
}
ROWS_BLK = 512
UNIT_BLK = 256
PAD = 16
BACK_MICROS = (8, 3, 3, 4, 4, 4)


def dot(left, right, left_dim, right_dim):
    return lax.dot_general(
        left, right, (((left_dim,), (right_dim,)), ((), ())), preferred_element_type=F32
    )


def call(body, name, micros, grid, in_specs, out_specs, out_shape, scratch, prefetch=0):
    return pl.pallas_call(
        body,
        grid_spec=pltpu.PrefetchScalarGridSpec(
            num_scalar_prefetch=prefetch,
            grid=grid,
            in_specs=in_specs,
            out_specs=out_specs,
            scratch_shapes=scratch,
        ),
        out_shape=out_shape,
        compiler_params=pltpu.CompilerParams(vmem_limit_bytes=VMEM_MIB[name] * 1024 * 1024),
        cost_estimate=pl.CostEstimate(flops=int(micros * 1e9), bytes_accessed=0, transcendentals=0),
        name=name,
    )


def rows_spec(height, block):
    return pl.BlockSpec((height, block), lambda i, *_: (0, i))


def whole_spec(shape):
    return pl.BlockSpec(shape, lambda i, *_: (0,) * len(shape), pipeline_mode=pl.Buffered(1))


def shape_of(shape, dtype):
    return jax.ShapeDtypeStruct(shape, dtype)


def join_halves(scratch, mine_ref, other_ref, core):
    half = mine_ref.shape[0]
    scratch[pl.ds(pl.multiple_of(core * half, half), half), :] = mine_ref[...]
    scratch[pl.ds(pl.multiple_of((1 - core) * half, half), half), :] = other_ref[...]
    return scratch[...]


def crms_stats(values):
    kept = jnp.where(lax.broadcasted_iota(jnp.int32, values.shape, 0) < DS, values, 0.0)
    total = jnp.sum(kept, 0, keepdims=True)
    squares = jnp.sum(kept * kept, 0, keepdims=True)
    scale = lax.rsqrt((squares + total * total) / DP + EPSILON)
    return kept, scale, total


def causal_tile():
    key_pos = lax.broadcasted_iota(jnp.int32, (BLK, BLK), 0)
    query_pos = lax.broadcasted_iota(jnp.int32, (BLK, BLK), 1)
    return key_pos <= query_pos


def attend_head(w_ref, normed_ref, qkv_ref, a_ref, log_ref, s_scr, p_scr):
    rows = normed_ref.shape[1]
    blocks = rows // BLK
    outs = 3 * HS
    bias = w_ref[outs : outs + 1, :outs].astype(F32).T
    qkv_ref[...] = (dot(w_ref[:outs, :], normed_ref[...], 1, 0) + bias).astype(BF)
    key_rows = qkv_ref[HS : 2 * HS, :].T
    queries = qkv_ref[:HS, :] * jnp.asarray(0.125, BF)
    allowed = causal_tile()

    def score(blk):
        at = slice(blk * BLK, (blk + 1) * BLK)
        count = (blk + 1) * BLK
        scores = dot(key_rows[:count], queries[:, at], 1, 0)
        if blk:
            s_scr[blk % 2, : count - BLK] = scores[: count - BLK]
        s_scr[blk % 2, count - BLK : count] = jnp.where(allowed, scores[count - BLK :], NEGATIVE)

    def soften(blk):
        count = (blk + 1) * BLK
        top = jnp.max(s_scr[blk % 2, :count], axis=0, keepdims=True)
        expo = jnp.exp(s_scr[blk % 2, :count] - top)
        total = jnp.sum(expo, axis=0, keepdims=True)
        p_scr[blk % 2, :count] = expo.astype(BF)
        log_ref[0, :, blk * BLK : count] = top + jnp.log(total)
        return total

    def mix(blk, total):
        count = (blk + 1) * BLK
        mixed = dot(qkv_ref[2 * HS :, :count], p_scr[blk % 2, :count], 1, 0)
        a_ref[:, blk * BLK : count] = (mixed * (1.0 / total)).astype(BF)

    score(0)
    totals = {}
    for blk in range(blocks):
        if blk + 1 < blocks:
            score(blk + 1)
        if blk:
            mix(blk - 1, totals[blk - 1])
        totals[blk] = soften(blk)
    mix(blocks - 1, totals[blocks - 1])


def norm_attend_body(
    where_ref, mine_ref, other_ref, w_ref, normed_ref, stats_ref, qkv_ref, a_ref, log_ref, s_scr, p_scr
):
    @pl.when(pl.program_id(0) == 0)
    def _():
        half = mine_ref.shape[0]
        core = where_ref[0]
        first = pl.ds(pl.multiple_of(core * half, half), half)
        second = pl.ds(pl.multiple_of((1 - core) * half, half), half)
        normed_ref[first, :] = mine_ref[...]
        normed_ref[second, :] = other_ref[...]
        for start in range(0, normed_ref.shape[1], BLK):
            at = slice(start, start + BLK)
            kept, scale, total = crms_stats(normed_ref[:, at].astype(F32))
            normed_ref[:, at] = (kept * scale).astype(BF)
            stats_ref[0:1, at] = scale
            stats_ref[1:2, at] = total

    attend_head(w_ref, normed_ref, qkv_ref, a_ref, log_ref, s_scr, p_scr)


def attend_specs(heads, rows):
    outs = 3 * HS
    ins = [pl.BlockSpec((outs + PAD, DP), lambda h, *_: (h, 0))]
    results = [
        pl.BlockSpec((outs, rows), lambda h, *_: (h, 0)),
        pl.BlockSpec((HS, rows), lambda h, *_: (h, 0)),
        pl.BlockSpec((1, 1, rows), lambda h, *_: (h, 0, 0)),
    ]
    shapes = [
        shape_of((heads * outs, rows), BF),
        shape_of((heads * HS, rows), BF),
        shape_of((heads, 1, rows), F32),
    ]
    scratch = [pltpu.VMEM((2, rows, BLK), F32), pltpu.VMEM((2, rows, BLK), BF)]
    return ins, results, shapes, scratch


def norm_attend(where, mine, other, weights):
    half, rows = mine.shape
    heads = weights.shape[0] // (3 * HS + PAD)
    ins, results, shapes, scratch = attend_specs(heads, rows)
    return call(
        norm_attend_body,
        "norm_attend",
        22,
        (heads,),
        [whole_spec((half, rows)), whole_spec((half, rows))] + ins,
        [whole_spec((DP, rows)), whole_spec((8, rows))] + results,
        [shape_of((DP, rows), BF), shape_of((8, rows), F32)] + shapes,
        scratch,
        1,
    )(where, mine, other, weights)


def more_attend_body(normed_ref, w_ref, qkv_ref, a_ref, log_ref, s_scr, p_scr):
    attend_head(w_ref, normed_ref, qkv_ref, a_ref, log_ref, s_scr, p_scr)


def more_attend(normed, weights):
    rows = normed.shape[1]
    heads = weights.shape[0] // (3 * HS + PAD)
    ins, results, shapes, scratch = attend_specs(heads, rows)
    return call(
        more_attend_body,
        "attend",
        20,
        (heads,),
        [whole_spec((DP, rows))] + ins,
        results,
        shapes,
        scratch,
    )(normed, weights)


def attend_back_body(
    qkv_ref, da_ref, a_ref, log_ref, normed_hbm, grad_ref, gw_ref,
    p_scr, ds_scr, s_scr, dp_scr, dq_scr, normed_scr, sem,
):
    fetch = pltpu.make_async_copy(normed_hbm, normed_scr, sem)
    fetch.start()
    rows = qkv_ref.shape[1]
    blocks = rows // BLK
    queries = qkv_ref[:HS, :] * jnp.asarray(0.125, BF)
    query_rows = queries.T
    key_rows = qkv_ref[HS : 2 * HS, :].T
    value_rows = qkv_ref[2 * HS :, :].T
    grad = da_ref[...]
    grad_rows = grad.T
    row_dot = jnp.sum(grad.astype(F32) * a_ref[...].astype(F32), axis=0, keepdims=True)
    logs = log_ref[0]
    allowed = causal_tile()

    def span(blk):
        return slice(blk * BLK, (blk + 1) * BLK)

    def score(blk):
        start = blk * BLK
        s_scr[blk % 2, :, start:] = dot(key_rows[span(blk)], queries[:, start:], 1, 0)
        dp_scr[blk % 2, :, start:] = dot(value_rows[span(blk)], grad[:, start:], 1, 0)

    def soften(blk):
        slot = blk % 2
        for query_blk in range(blk, blocks):
            at = span(query_blk)
            probs = jnp.exp(s_scr[slot, :, at] - logs[:, at])
            if query_blk == blk:
                probs = jnp.where(allowed, probs, 0.0)
            p_scr[slot, :, at] = probs.astype(BF)
            ds_scr[slot, :, at] = (probs * (dp_scr[slot, :, at] - row_dot[:, at])).astype(BF)

    def mix(blk):
        slot, start = blk % 2, blk * BLK
        grad_keys = dot(ds_scr[slot, :, start:], query_rows[start:], 1, 0)
        grad_values = dot(p_scr[slot, :, start:], grad_rows[start:], 1, 0)
        grad_queries = dot(qkv_ref[HS : 2 * HS, span(blk)], ds_scr[slot, :, start:], 1, 0)
        if blk:
            dq_scr[:, start:] += grad_queries
        else:
            dq_scr[...] = grad_queries
        grad_ref[HS : 2 * HS, span(blk)] = grad_keys.T.astype(BF)
        grad_ref[2 * HS :, span(blk)] = grad_values.T.astype(BF)

    score(0)
    for blk in range(blocks):
        if blk + 1 < blocks:
            score(blk + 1)
        if blk:
            mix(blk - 1)
        soften(blk)
    mix(blocks - 1)
    grad_ref[:HS, :] = (dq_scr[...] * 0.125).astype(BF)
    fetch.wait()
    outs = 3 * HS
    gw_ref[:outs, :] = dot(grad_ref[...], normed_scr[...], 1, 1).astype(BF)
    gw_ref[outs:, :] = jnp.zeros((PAD, DP), BF)
    gw_ref[outs : outs + 1, :outs] = jnp.sum(grad_ref[...].astype(F32), 1, keepdims=True).T.astype(BF)


def attend_back(qkv, grad, mixed, logs, normed, head, grad_head):
    rows = qkv.shape[1]
    outs = 3 * HS
    return call(
        attend_back_body,
        "attend_back",
        BACK_MICROS[grad_head],
        (1,),
        [
            pl.BlockSpec((outs, rows), lambda i: (head, 0)),
            pl.BlockSpec((HS, rows), lambda i: (grad_head, 0)),
            pl.BlockSpec((HS, rows), lambda i: (head, 0)),
            pl.BlockSpec((1, 1, rows), lambda i: (head, 0, 0)),
            pl.BlockSpec(memory_space=pl.ANY),
        ],
        [
            pl.BlockSpec((outs, rows), lambda i: (0, 0)),
            pl.BlockSpec((outs + PAD, DP), lambda i: (0, 0)),
        ],
        [shape_of((outs, rows), BF), shape_of((outs + PAD, DP), BF)],
        [
            pltpu.VMEM((2, BLK, rows), BF),
            pltpu.VMEM((2, BLK, rows), BF),
            pltpu.VMEM((2, BLK, rows), F32),
            pltpu.VMEM((2, BLK, rows), F32),
            pltpu.VMEM((HS, rows), F32),
            pltpu.VMEM((DP, rows), BF),
            pltpu.SemaphoreType.DMA(()),
        ],
    )(qkv, grad, mixed, logs, normed)


GELU_A = 0.7978845608028654
GELU_B = 0.044715


def gelu_pair(pre):
    square = pre * pre
    bent = jnp.tanh(GELU_A * pre * (1.0 + GELU_B * square))
    half_up = 0.5 * (1.0 + bent)
    slope = half_up + 0.5 * pre * (1.0 - bent * bent) * (GELU_A * (1.0 + 3.0 * GELU_B * square))
    return pre * half_up, slope


def mlp_body(
    where_ref, a0, a1, a2, a3, wout0, wout1, wout2, wout3, b_out, b_down, x_mine, x_other, c_mine, c_other, w_own, w_other,
    y_ref, stats_ref, normed_ref, m_other_ref, dn_ref, gd_own, gu_own, gd_other, gu_other,
    wout, a_scr, x_scr, c_scr, h_scr, up_scr, down_scr, bias_scr, pre_scr, back_scr, g_scr, du_scr, gd, gu, gb, pack_scr, w_sem, pack_sem,
):
    step = pl.program_id(0)
    last = pl.num_programs(0) - 1
    core = where_ref[0]
    half, block = x_mine.shape
    units = DP
    fetch = []
    for i, ref in enumerate((w_own, w_other)):
        at = pl.ds(i * units, units)
        for j, (source, target) in enumerate(
            (
                (ref.at[pl.ds(0, DP), :], up_scr.at[:, at]),
                (ref.at[pl.ds(DP, units), :], down_scr.at[at, :]),
                (ref.at[pl.ds(DP + units + 2 * a0.shape[0], PAD), :], bias_scr.at[:, at]),
            )
        ):
            fetch.append(pltpu.make_async_copy(source, target, w_sem.at[i, j]))
    split = ((gd_own, pl.ds(0, units)), (gu_own, pl.ds(units, DP + PAD)))
    split += ((gd_other, pl.ds(0, units)), (gu_other, pl.ds(units, DP + PAD)))
    store = [
        pltpu.make_async_copy(pack_scr.at[i // 2, at, :], ref, pack_sem.at[i]) for i, (ref, at) in enumerate(split)
    ]

    @pl.when(step == 0)
    def _():
        for copy in fetch:
            copy.start()
        start = 0
        for ref in (wout0, wout1, wout2, wout3):
            wout[start : start + ref.shape[0], :] = ref[...]
            start += ref.shape[0]
        for ref in (gd, gu, gb):
            ref[...] = jnp.zeros_like(ref)

    for i, a_ref in enumerate((a0, a1, a2, a3)):
        part = a_ref.shape[0]
        a_scr[i * part : (i + 1) * part, :] = a_ref[...]
    position = step * block + lax.broadcasted_iota(jnp.int32, (1, block), 1)
    valid = (position < where_ref[1]).astype(F32)
    stream = join_halves(x_scr, x_mine, x_other, core).astype(F32)
    branch = dot(wout[...], a_scr[...], 0, 0) + b_out[...].astype(F32).T
    hidden = stream + valid * branch
    h_scr[...] = hidden
    kept, scale, total = crms_stats(hidden)
    stats_ref[0:1, :] = scale
    stats_ref[1:2, :] = total
    normed = (kept * scale).astype(BF)
    normed_ref[...] = normed
    grad_out = join_halves(c_scr, c_mine, c_other, core)
    keep_row = lax.broadcasted_iota(jnp.int32, (DP, block), 0) < DS
    dm = jnp.where(keep_row, grad_out.astype(F32) * valid, 0.0).astype(BF)

    @pl.when(step == 0)
    def _():
        for copy in fetch:
            copy.wait()

    ones = jnp.ones((block, 128), BF)
    gb[2 * units :] += dot(dm, ones, 1, 0)
    starts = [which * units + start for which in (1, 0) for start in range(0, units, UNIT_BLK)]

    def expand(i):
        at = slice(starts[i], starts[i] + UNIT_BLK)
        pre_scr[i % 2] = dot(up_scr[:, at], normed, 0, 0)
        back_scr[i % 2] = dot(down_scr[at, :], dm, 1, 0)

    def bend(i):
        at = slice(starts[i], starts[i] + UNIT_BLK)
        act, slope = gelu_pair(pre_scr[i % 2] + bias_scr[0:1, at].astype(F32).T)
        g_scr[at, :] = act.astype(BF)
        du_scr[at, :] = (back_scr[i % 2] * slope).astype(BF)

    def collect(i):
        at = slice(starts[i], starts[i] + UNIT_BLK)
        gd[at, :] += dot(g_scr[at, :], dm, 1, 1)
        gu[:, at] += dot(normed, du_scr[at, :], 1, 1)
        gb[at] += dot(du_scr[at, :], ones, 1, 0)

    expand(0)
    for i in range(len(starts)):
        if i + 1 < len(starts):
            expand(i + 1)
        if i:
            collect(i - 1)
        bend(i)
    collect(len(starts) - 1)

    @pl.when(step == last)
    def _():
        for which in (1, 0):
            mine = slice(which * units, (which + 1) * units)
            pack_scr[which, 0:units, :] = gd[mine, :].astype(BF)
            pack_scr[which, units : units + DP, :] = gu[:, mine].astype(BF)
            pack_scr[which, units + DP :, :] = jnp.zeros((PAD, DP), BF)
            pack_scr[which, units + DP : units + DP + 1, :] = gb[mine].T[:1].astype(BF)
            pack_scr[which, units + DP + 1 : units + DP + 2, :] = gb[2 * units :].T[:1].astype(BF)
            store[2 * which].start()
            store[2 * which + 1].start()

    own = pl.ds(pl.multiple_of(core * half, half), half)
    far = pl.ds(pl.multiple_of((1 - core) * half, half), half)
    m_part = h_scr
    column = b_down[...].astype(F32).T
    bias = jnp.where(core == 0, column[:half], column[half:])
    y_ref[...] = h_scr[own, :] + valid * bias
    m_part[...] = dot(down_scr[...], g_scr[...], 0, 0)
    y_ref[...] += valid * m_part[own, :]
    m_other_ref[...] = (valid * m_part[far, :]).astype(BF)
    dn_ref[...] = dot(up_scr[...], du_scr[...], 1, 0).astype(BF)

    @pl.when(step == last)
    def _():
        for copy in store:
            copy.wait()


def pack_rows(part, which):
    return pl.BlockSpec((part, DP), lambda i, *_: (2 * DP // part + which, 0), pipeline_mode=pl.Buffered(1))


def mlp(where, mixed, b_out, b_down, stream, cot, weights):
    half, rows = stream[0].shape
    part = mixed[0].shape[0]
    units = DP
    block = ROWS_BLK
    pack = (units + DP + PAD, DP)
    anywhere = pl.BlockSpec(memory_space=pl.ANY)
    return call(
        mlp_body,
        "out_project_mlp",
        40,
        (rows // block,),
        [rows_spec(part, block)] * 4
        + [pack_rows(part, which) for which in (0, 0, 1, 1)]
        + [whole_spec((1, DP))] * 2
        + [rows_spec(half, block)] * 4
        + [anywhere] * 2,
        [
            rows_spec(half, block),
            rows_spec(8, block),
            rows_spec(DP, block),
            rows_spec(half, block),
            rows_spec(DP, block),
        ]
        + [anywhere] * 4,
        [
            shape_of((half, rows), F32),
            shape_of((8, rows), F32),
            shape_of((DP, rows), BF),
            shape_of((half, rows), BF),
            shape_of((DP, rows), BF),
        ]
        + [shape_of((units, DP), BF), shape_of((DP + PAD, DP), BF)] * 2,
        [pltpu.VMEM((DP, DP), BF)]
        + [pltpu.VMEM((DP, block), BF)] * 3
        + [
            pltpu.VMEM((DP, block), F32),
            pltpu.VMEM((DP, 2 * units), BF),
            pltpu.VMEM((2 * units, DP), BF),
            pltpu.VMEM((PAD, 2 * units), BF),
            pltpu.VMEM((2, UNIT_BLK, block), F32),
            pltpu.VMEM((2, UNIT_BLK, block), F32),
            pltpu.VMEM((2 * units, block), BF),
            pltpu.VMEM((2 * units, block), BF),
            pltpu.VMEM((2 * units, DP), F32),
            pltpu.VMEM((DP, 2 * units), F32),
            pltpu.VMEM((2 * units + DP, 128), F32),
            pltpu.VMEM((2, *pack), BF),
            pltpu.SemaphoreType.DMA((2, 3)),
            pltpu.SemaphoreType.DMA((4,)),
        ],
        1,
    )(where, *mixed, *weights, *weights, b_out, b_down, *stream, *cot, *weights)


def out_back_body(
    where_ref, dn_mine, dn_other, normed_ref, stats_ref, c_mine, c_other, w0, w1, a0, a1,
    dh_ref, da_ref, pack_own, pack_other, c_scr, dh_scr, gw_scr, gb_scr,
):
    step = pl.program_id(0)
    core = where_ref[0]
    half, block = c_mine.shape
    position = step * block + lax.broadcasted_iota(jnp.int32, (1, block), 1)
    valid = (position < where_ref[1]).astype(F32)
    row_mask = lax.broadcasted_iota(jnp.int32, (DP, 1), 0) < DS
    grad_norm = dn_mine[...].astype(F32) + dn_other[...].astype(F32)
    normed = normed_ref[...].astype(F32)
    scale, total = stats_ref[0:1, :], stats_ref[1:2, :]
    inner = jnp.sum(grad_norm * normed, 0, keepdims=True) * (1.0 / DP)
    grad_out = join_halves(c_scr, c_mine, c_other, core).astype(F32)
    pulled = scale * (grad_norm - (normed + scale * total) * inner)
    grad_hidden = grad_out + jnp.where(row_mask, pulled, 0.0)
    dh_scr[...] = grad_hidden
    dh_ref[...] = dh_scr[pl.ds(pl.multiple_of(core * half, half), half), :].astype(BF)
    branch_f = jnp.where(row_mask, grad_hidden * valid, 0.0)
    branch = branch_f.astype(BF)
    part = a0.shape[0]
    da_ref[:part, :] = dot(w0[...], branch, 1, 0).astype(BF)
    da_ref[part:, :] = dot(w1[...], branch, 1, 0).astype(BF)

    @pl.when(step == 0)
    def _():
        gw_scr[...] = jnp.zeros_like(gw_scr)
        gb_scr[...] = jnp.zeros_like(gb_scr)

    gw_scr[:part] += dot(a0[...], branch, 1, 1)
    gw_scr[part:] += dot(a1[...], branch, 1, 1)
    gb_scr[...] += jnp.sum(branch_f, 1, keepdims=True)

    @pl.when(step == pl.num_programs(0) - 1)
    def _():
        for i, pack in enumerate((pack_own, pack_other)):
            pack[:part, :] = gw_scr[i * part : (i + 1) * part, :].astype(BF)
            pack[part:, :] = jnp.zeros((PAD, DP), BF)
            pack[part : part + 1, :] = gb_scr[...].T.astype(BF)


def out_back(where, dn, normed, stats, cot, weights, mixed):
    rows = normed.shape[1]
    half = cot[0].shape[0]
    part = mixed[0].shape[0]
    block = ROWS_BLK
    return call(
        out_back_body,
        "out_project_back",
        12,
        (rows // block,),
        [rows_spec(DP, block)] * 3
        + [rows_spec(8, block)]
        + [rows_spec(half, block)] * 2
        + [pack_rows(part, 0)] * 2
        + [rows_spec(part, block)] * 2,
        [
            rows_spec(half, block),
            rows_spec(2 * part, block),
            whole_spec((part + PAD, DP)),
            whole_spec((part + PAD, DP)),
        ],
        [
            shape_of((half, rows), BF),
            shape_of((2 * part, rows), BF),
            shape_of((part + PAD, DP), BF),
            shape_of((part + PAD, DP), BF),
        ],
        [
            pltpu.VMEM((DP, block), BF),
            pltpu.VMEM((DP, block), F32),
            pltpu.VMEM((2 * part, DP), F32),
            pltpu.VMEM((DP, 1), F32),
        ],
        1,
    )(where, *dn, normed, stats, *cot, *weights, *mixed)


def project_back_body(
    where_ref, g0, g1, g2, g3, g4, g5, normed_ref, w0, w1, dn_own_ref, dn_other_ref, inner_ref, p_scr, dn_scr, w_scr
):
    core = where_ref[0]
    outs = 3 * HS

    @pl.when(pl.program_id(0) == 0)
    def _():
        at = 0
        for ref in (w0, w1):
            for start in range(0, ref.shape[0], outs + PAD):
                w_scr[at : at + outs, :] = ref[start : start + outs, :]
                at += outs

    part = g0.shape[0]
    for i, ref in enumerate((g0, g1, g2, g3, g4, g5)):
        p_scr[i * part : (i + 1) * part, :] = ref[...]
    grad_norm = dot(w_scr[...], p_scr[...], 0, 0)
    dn_scr[...] = grad_norm
    half = DP // 2
    dn_own_ref[...] = dn_scr[pl.ds(pl.multiple_of(core * half, half), half), :].astype(BF)
    dn_other_ref[...] = dn_scr[pl.ds(pl.multiple_of((1 - core) * half, half), half), :].astype(BF)
    inner = jnp.sum(grad_norm * normed_ref[...].astype(F32), 0, keepdims=True)
    inner_ref[...] = jnp.broadcast_to(inner, inner_ref.shape)


def project_back(where, grads, normed, weights):
    part, rows = grads[0].shape
    half = DP // 2
    block = ROWS_BLK
    return call(
        project_back_body,
        "project_back",
        8,
        (rows // block,),
        [rows_spec(part, block)] * 6 + [rows_spec(DP, block)] + [whole_spec(w.shape) for w in weights],
        [rows_spec(half, block), rows_spec(half, block), rows_spec(8, block)],
        [shape_of((half, rows), BF), shape_of((half, rows), BF), shape_of((8, rows), F32)],
        [pltpu.VMEM((6 * part, block), BF), pltpu.VMEM((DP, block), F32), pltpu.VMEM((6 * part, DP), BF)],
        1,
    )(where, *grads, normed, *weights)


def swap(value, axis):
    return lax.ppermute(value, axis, [(0, 1), (1, 0)])


def cross(value):
    return lax.ppermute(value, ("core", "x"), [(1, 2), (2, 1)])


def after(value, *others):
    return lax.optimization_barrier((value, *others))[0]


def quarter(value, core, axis):
    size = value.shape[axis] // 2
    return lax.dynamic_slice_in_dim(value, core * size, size, axis)


def both(mine, other, core, axis):
    first = jnp.where(core == 0, mine, other)
    second = jnp.where(core == 0, other, mine)
    return jnp.concatenate([first, second], axis)


def pad_last(value):
    return jnp.pad(value, [(0, 0)] * (value.ndim - 1) + [(0, DP - value.shape[-1])])


def pad_rows(value, count):
    return jnp.pad(value, ((0, count - value.shape[0]), (0, 0)))


def sum_steps(value, index, count):
    levels = count.bit_length() - 1
    for level in range(levels):
        halves = value.reshape(2, -1, value.shape[-1])
        low = (index >> level) & 1 == 0
        keep = jnp.where(low, halves[0], halves[1])
        value = keep + (yield level, jnp.where(low, halves[1], halves[0]))
    for level in reversed(range(levels)):
        low = (index >> level) & 1 == 0
        got = yield level, value
        value = jnp.concatenate([jnp.where(low, value, got), jnp.where(low, got, value)])
    yield None, value


class ChipSum:
    def __init__(self, value, index, count):
        self.count = count
        self.steps = sum_steps(value, index, count)
        self.level, self.value = next(self.steps)
        self.got = None

    def send(self):
        if self.level is not None:
            pairs = [(i, i ^ (1 << self.level)) for i in range(self.count)]
            self.got = lax.ppermute(self.value, "zy", pairs)

    def take(self, *others):
        if self.level is not None:
            got = after(self.got, *others) if others else self.got
            self.level, self.value = self.steps.send(got)
            self.got = None
        return self.value

    def finish(self, *others):
        while self.level is not None:
            if self.got is None:
                self.send()
            self.take(*others)
        return self.value


def on_device(chips, stream, lengths, w_qkv, b_qkv, w_out, b_out, w_up, b_up, w_down, b_down, cotangent):
    core = lax.axis_index("core")
    chip = lax.axis_index("x")
    place = lax.axis_index("zy")
    stays = core == chip
    half, rows = stream.shape

    def home(value):
        return jnp.where(stays, value, cross(value))

    side = core[None].astype(jnp.int32)

    part = w_out.shape[0] // 2
    units = DP
    own_mlp = jnp.concatenate(
        [
            jnp.pad(quarter(w_up, core, 1), ((0, DP - DS), (0, 0))),
            pad_last(quarter(w_down, core, 0)),
            pad_last(quarter(w_out, core, 0)),
            pad_last(quarter(w_out, 1 - core, 0)),
            pad_rows(quarter(b_up, core, 0)[None], 128),
        ]
    )
    share = own_mlp.shape[0] // chips
    piece = lax.dynamic_slice_in_dim(own_mlp, place * share, share, 0)
    got_piece = swap(piece, "x")
    x_mine = home(stream)
    other_mlp = lax.all_gather(got_piece, "zy", axis=0, tiled=True)

    outs = 3 * HS
    heads = b_qkv.shape[1] // (2 * HS)
    head_w = pad_last(quarter(w_qkv, core, 1)).reshape(3, heads, HS, DP).swapaxes(0, 1).reshape(heads, outs, DP)
    head_b = quarter(b_qkv, core, 1).reshape(3, heads, HS).swapaxes(0, 1).reshape(heads, 1, outs)
    head_b = jnp.pad(head_b, ((0, 0), (0, PAD - 1), (0, DP - outs)))
    own_qkv = jnp.concatenate([head_w, head_b], 1).reshape(-1, DP)
    x_mine, own_qkv = lax.optimization_barrier((x_mine, own_qkv, got_piece))[:2]
    x_other = swap(x_mine, "core")
    other_qkv = swap(own_qkv, "x")

    normed_one, stats_one, qkv_own, mixed_own, logs_own = norm_attend(side, x_mine, x_other, own_qkv)
    mixed_own_far = swap(mixed_own, "core")
    length = after(lengths, mixed_own)
    length = jnp.where(stays, length, swap(length.astype(F32), "core").astype(jnp.int32))
    where = jnp.concatenate([side, length])
    c_mine = home(after(cotangent, mixed_own))
    qkv_other, mixed_other, logs_other = more_attend(normed_one, other_qkv)
    mixed_other_far = swap(mixed_other, "core")
    c_mine = after(c_mine, mixed_other)
    c_other = swap(c_mine, "core")

    y_own, stats_two, normed_two, m_other, dn_two, gd_own, gu_own, gd_other, gu_other = mlp(
        where,
        (mixed_own, mixed_other, mixed_own_far, mixed_other_far),
        jnp.pad(b_out, (0, 1))[None],
        jnp.pad(b_down, (0, 1))[None],
        (x_mine, x_other),
        (c_mine, c_other),
        (own_mlp, other_mlp),
    )
    dn_two_far = swap(dn_two, "core")
    got_down = swap(gd_other, "x")
    got_up = swap(gu_other, "x")
    m_far = swap(m_other, "core")
    dh_own, grad_mixed, out_own, out_other = out_back(
        where,
        (dn_two, dn_two_far),
        normed_two,
        stats_two,
        (c_mine, c_other),
        (own_mlp, other_mlp),
        (mixed_own, mixed_other),
    )

    got_out = swap(out_other, "x")
    back = {}
    sets = {0: (qkv_own, mixed_own, logs_own), 1: (qkv_other, mixed_other, logs_other)}

    def run_head(which, head, *first):
        qkv, mixed, logs = sets[which]
        done = attend_back(after(qkv, *first), grad_mixed, mixed, logs, normed_one, head, which * heads + head)
        back[which, head] = done
        return done[0]

    total_down = gd_own + after(got_down, grad_mixed)
    last = run_head(1, 0, grad_mixed, total_down)
    sum_down = lax.psum(total_down, "zy")
    last = run_head(1, 1, last)
    result = (y_own + after(m_far, last).astype(F32)).astype(BF)
    last = run_head(1, 2, last, result)
    total_rest = jnp.concatenate([gu_own + after(got_up, last), out_own + after(got_out, last)])
    rest = ChipSum(pad_rows(total_rest, 1024), place, chips)
    output = home(after(result, total_rest))

    def qkv_pack(which):
        return pad_rows(jnp.concatenate([back[which, head][1] for head in range(heads)]), 640)

    got_qkv = swap(qkv_pack(1), "x")
    rest.send()
    for head in range(heads):
        last = run_head(0, head, last, rest.value)
        if head:
            rest.take(last)
            rest.send()
    qkv = ChipSum(qkv_pack(0) + after(got_qkv, last), place, chips)
    qkv.send()
    normed_late = after(normed_one, qkv.value, rest.value, output, last)
    dn_own, dn_other, inner = project_back(
        where,
        [back[which, head][0] for which in (0, 1) for head in range(heads)],
        normed_late,
        (own_qkv, other_qkv),
    )
    rest.take(dn_own)
    rest.send()
    qkv.take(dn_own)
    qkv.send()
    dn_far = swap(after(dn_other, rest.value, qkv.value, sum_down), "core")
    inner = inner[0:1] + swap(inner, "core")[0:1]
    row_mask = core * half + lax.broadcasted_iota(jnp.int32, (half, 1), 0) < DS
    scale_one, total_one = stats_one[0:1], stats_one[1:2]
    grad_in = dh_own.astype(F32) + jnp.where(
        row_mask,
        scale_one * (dn_own.astype(F32) + dn_far.astype(F32))
        - scale_one * scale_one * (x_mine.astype(F32) + total_one) * inner / DP,
        0.0,
    )
    grad_sent = grad_in.astype(BF)
    grad_got = cross(grad_sent)
    grad_stream = jnp.where(stays, grad_sent, grad_got).astype(F32)
    def gather(mine, far, pick, axis):
        return both(pick(mine), pick(far), core, axis).astype(F32)

    def by_head(value):
        return value[: heads * (outs + PAD)].reshape(heads, outs + PAD, DP)

    def pick_w(value):
        return by_head(value)[:, :outs, :DS].reshape(heads, 3, HS, DS).swapaxes(0, 1).reshape(3, -1, DS)

    def pick_b(value):
        return by_head(value)[:, outs, :outs].reshape(heads, 3, HS).swapaxes(0, 1).reshape(3, -1)

    qkv.take(grad_sent)
    qkv.send()
    rest.take(qkv.value)
    rest.send()
    far_down = swap(after(sum_down, qkv.value), "core")
    qkv.take()
    qkv.send()
    rest.take(qkv.value)
    rest.send()
    grad_w_down = gather(sum_down, far_down, lambda v: v[:, :DS], 0)
    qkv.take(grad_w_down)
    qkv.send()
    qkv.take(grad_got)
    qkv.send()
    sum_rest = rest.finish(qkv.value)
    far_rest = jnp.concatenate([swap(piece, "core") for piece in jnp.split(sum_rest, 4)])
    edge = DP + PAD
    grad_w_up = gather(sum_rest, far_rest, lambda v: v[:DS], 1)
    grad_w_out = gather(sum_rest, far_rest, lambda v: v[edge : edge + part, :DS], 0)
    sum_qkv = qkv.finish(grad_stream, far_rest)
    far_qkv = swap(sum_qkv, "core")

    return (
        output,
        grad_stream,
        gather(sum_qkv, far_qkv, pick_w, 1),
        gather(sum_qkv, far_qkv, pick_b, 1),
        grad_w_out,
        sum_rest[edge + part, :DS].astype(F32),
        grad_w_up,
        gather(sum_rest, far_rest, lambda v: v[DP], 0),
        grad_w_down,
        sum_rest[DP + 1, :DS].astype(F32),
    )


def solution(mesh):
    dp, mp = mesh.shape["dp"], mesh.shape["mp"]
    fine = Mesh(mesh.devices.reshape(dp // 2, 2, mp), ("zy", "core", "x"))
    seqs = ("zy", "core")
    placed = (
        P("x", seqs),
        P(seqs),
        P(None, "x", None),
        P(None, "x"),
        P("x", None),
        P(),
        P(None, "x"),
        P("x"),
        P("x", None),
        P(),
        P("x", seqs),
    )
    return jax.shard_map(
        functools.partial(on_device, dp // 2),
        mesh=fine,
        in_specs=placed,
        out_specs=(
            P("x", seqs),
            P("x", seqs),
            P(None, "x", None),
            P(None, "x"),
            P("x", None),
            P(),
            P(None, "x"),
            P("x"),
            P("x", None),
            P(),
        ),
        check_vma=False,
    )
```
